32 devices in a mesh: dp: 2 (over x), seq: 4 (over z), tensor: 4 (over y, core).
Axes of the slice: x: 2, y: 2, z: 4, core: 2. Of those that a mesh axis runs over, the one named last changes fastest.
Arguments:
- tokens: bfloat16 [2048, 4, 1536], P(('seq', 'tensor'), 'dp'), may hold values from -6 to 6
- attn_gain: bfloat16 [1536], replicated, may hold values from 0.5 to 1.5
- w_query: bfloat16 [1536, 1536], P(None, 'tensor'), may hold values from -0.15625 to 0.15625
- w_key: bfloat16 [1536, 768], P(None, 'tensor'), may hold values from -0.15625 to 0.15625
- w_value: bfloat16 [1536, 768], P(None, 'tensor'), may hold values from -0.15625 to 0.15625
- w_output: bfloat16 [1536, 1536], P('tensor'), may hold values from -0.625 to 0.625
- ffn_gain: bfloat16 [1536], replicated, may hold values from 0.5 to 1.5
- w_gate: bfloat16 [1536, 4096], P(None, 'tensor'), may hold values from -0.15625 to 0.15625
- w_up: bfloat16 [1536, 4096], P(None, 'tensor'), may hold values from -0.15625 to 0.15625
- w_down: bfloat16 [4096, 1536], P('tensor'), may hold values from -0.09375 to 0.09375
- cotangent: bfloat16 [2048, 4, 1536], P(('seq', 'tensor'), 'dp'), may hold values from -6 to 6
Outputs:
- activation: bfloat16 [2048, 4, 1536], P(('seq', 'tensor'), 'dp')
- input_grad: float32 [2048, 4, 1536], P(('seq', 'tensor'), 'dp')
- attn_gain_grad: float32 [1536], replicated
- query_grad: float32 [1536, 1536], P(None, 'tensor')
- key_grad: float32 [1536, 768], P(None, 'tensor')
- value_grad: float32 [1536, 768], P(None, 'tensor')
- output_grad: float32 [1536, 1536], P('tensor')
- ffn_gain_grad: float32 [1536], replicated
- gate_grad: float32 [1536, 4096], P(None, 'tensor')
- up_grad: float32 [1536, 4096], P(None, 'tensor')
- down_grad: float32 [4096, 1536], P('tensor')
The draws below stay inside these ranges and needn't reach their ends.
All inputs are finite; a program needn't handle non-finite values.
Results may differ from the reference program's by a relative error of at most 0.014.
Values may be sent and summed in bfloat16 or wider, within the bound.
A program may use at most 192 MiB of HBM per device.

```python
import jax
import jax.numpy as jnp
from jax import lax

D = 1536
HEADS = 16
KV_HEADS = 8
HEAD_DIM = 96
FF = 4096
LEN = 2048
SEQS = 4
Q_WIDTH = 1536
KV_WIDTH = 768


def shard_levels(stream_key, extent, pieces, least, top_value):
    level = 1.0
    for axis_at, shards_of in pieces:
        heights = jax.random.uniform(jax.random.fold_in(jax.random.fold_in(stream_key, 6), axis_at), (shards_of,), jnp.float32, least / len(pieces), top_value / len(pieces))
        level = level * jnp.repeat(jnp.exp(heights), extent[axis_at] // shards_of).reshape((-1,) + (1,) * (len(extent) - 1 - axis_at))
    return level


def gaussian(stream_key, shape, deviation, bound, shards=(), kind=jnp.bfloat16):
    level = shard_levels(stream_key, shape, shards, -0.22, 0.18) if shards else 1.0
    array = jax.random.normal(stream_key, shape, jnp.float32) * deviation * level
    return jnp.minimum(jnp.maximum(array, -bound), bound).astype(kind)


def setup_inputs(seed: int = 0) -> dict:
    streams_of = jax.random.split(jax.random.key(seed), 12)
    return {
        "tokens": gaussian(streams_of[0], (LEN, SEQS, D), 1.0, 6.0, ((0, 16), (1, 2))),
        "attn_gain": jnp.clip(1.0 + 0.1 * jax.random.normal(streams_of[1], (D,), jnp.float32), 0.5, 1.5).astype(jnp.bfloat16),
        "w_query": gaussian(streams_of[2], (D, Q_WIDTH), D ** -0.5, 0.15625, ((1, 4),)),
        "w_key": gaussian(streams_of[3], (D, KV_WIDTH), D ** -0.5, 0.15625, ((1, 4),)),
        "w_value": gaussian(streams_of[4], (D, KV_WIDTH), D ** -0.5, 0.15625, ((1, 4),)),
        "w_output": gaussian(streams_of[5], (Q_WIDTH, D), (Q_WIDTH // 16) ** -0.5, 0.625, ((0, 4),)),
        "ffn_gain": jnp.clip(1.0 + 0.1 * jax.random.normal(streams_of[6], (D,), jnp.float32), 0.5, 1.5).astype(jnp.bfloat16),
        "w_gate": gaussian(streams_of[7], (D, FF), D ** -0.5, 0.15625, ((1, 4),)),
        "w_up": gaussian(streams_of[8], (D, FF), D ** -0.5, 0.15625, ((1, 4),)),
        "w_down": gaussian(streams_of[9], (FF, D), FF ** -0.5, 0.09375, ((0, 4),)),
        "cotangent": gaussian(streams_of[10], (LEN, SEQS, D), 1.0, 6.0, ((0, 16), (1, 2))),
    }


@jax.custom_vjp
def low(v):
    return lax.optimization_barrier(v.astype(jnp.bfloat16)).astype(jnp.float32)

@jax.custom_vjp
def low_back(v):
    return v

def low_keep(v):
    return (low(v), None)

def low_pass(kept, grad):
    return (grad,)

def back_keep(v):
    return (v, None)

def back_low(kept, grad):
    return (low(grad),)
low.defvjp(low_keep, low_pass)
low_back.defvjp(back_keep, back_low)
highest = lax.Precision.HIGHEST
epsilon = 1e-05
theta = 100000.0

def matmul(left, right):
    return jnp.dot(left, right, precision=highest, preferred_element_type=jnp.float32)

def rotary_tables(positions, head_size):
    middle = head_size // 2
    rates = theta ** (-(jnp.arange(middle, dtype=jnp.float32) * 2.0 / head_size))
    angles = positions.astype(jnp.float32)[:, None] * rates[None, :]
    return (jnp.cos(angles), jnp.sin(angles))

def rotary(values, cosine, sine):
    middle = values.shape[-1] // 2
    first = values[..., :middle]
    second = values[..., middle:]
    return jnp.concatenate([first * cosine - second * sine, second * cosine + first * sine], axis=-1)

def norm_rows(values, gain):
    inverse = lax.rsqrt(lax.optimization_barrier(jnp.mean(values * values, axis=-1, keepdims=True)) + epsilon)
    return values * inverse * gain

def attention(query, keys, values):
    block_rows = min(512, LEN)
    blocks = LEN // block_rows
    group = HEADS // KV_HEADS
    keys_wide = jnp.repeat(keys, group, axis=1)
    values_wide = jnp.repeat(values, group, axis=1)
    scale = HEAD_DIM ** (-0.5)
    key_places = jnp.arange(LEN, dtype=jnp.int32)

    @jax.checkpoint
    def one_block(query_block, block_start):
        raw = low_back(jnp.einsum('qhd,khd->hqk', query_block, keys_wide, precision=highest))
        scores = raw * scale
        query_places = block_start + jnp.arange(block_rows, dtype=jnp.int32)
        allowed = key_places[None, :] <= query_places[:, None]
        scores = jnp.where(allowed[None], scores, -1e+30)
        peak = lax.optimization_barrier(jnp.max(scores, axis=-1, keepdims=True))
        weights = jnp.exp(scores - peak)
        probs = low(weights / lax.optimization_barrier(jnp.sum(weights, axis=-1, keepdims=True)))
        return jnp.einsum('hqk,khd->qhd', probs, values_wide, precision=highest)
    starts = jnp.arange(blocks, dtype=jnp.int32) * block_rows
    blocked = query.reshape(blocks, block_rows, HEADS, HEAD_DIM)
    outputs = lax.map(lambda block_pair: one_block(block_pair[0], block_pair[1]), (blocked, starts))
    return outputs.reshape(LEN, HEADS * HEAD_DIM)

def forward(inputs, attn_gain, w_query, w_key, w_value, w_output, ffn_gain, w_gate, w_up, w_down):
    cosine, sine = rotary_tables(jnp.arange(LEN, dtype=jnp.int32), HEAD_DIM)
    cosine = cosine[:, None, :]
    sine = sine[:, None, :]
    normed = low(norm_rows(inputs, attn_gain))
    query = low(rotary(low_back(matmul(normed, w_query)).reshape(LEN, HEADS, HEAD_DIM), cosine, sine))
    keys = low(rotary(low_back(matmul(normed, w_key)).reshape(LEN, KV_HEADS, HEAD_DIM), cosine, sine))
    values = low(low_back(matmul(normed, w_value))).reshape(LEN, KV_HEADS, HEAD_DIM)
    attended = low(low_back(attention(query, keys, values)))
    mid = inputs + low_back(matmul(attended, w_output))
    normed_two = low(norm_rows(mid, ffn_gain))
    gate = low_back(matmul(normed_two, w_gate))
    up_proj = low_back(matmul(normed_two, w_up))
    hidden = low(jax.nn.silu(gate) * up_proj)
    return mid + low_back(matmul(hidden, w_down))

def reference(tokens, attn_gain, w_query, w_key, w_value, w_output, ffn_gain, w_gate, w_up, w_down, cotangent):
    params = tuple((weight_arg.astype(jnp.float32) for weight_arg in (attn_gain, w_query, w_key, w_value, w_output, ffn_gain, w_gate, w_up, w_down)))

    def per_sequence(carry, sequence_pair):
        inputs = sequence_pair[0].astype(jnp.float32)
        result, pull = jax.vjp(forward, inputs, *params)
        grads = pull(sequence_pair[1].astype(jnp.float32))
        carry = tuple((total + grad_part for total, grad_part in zip(carry, grads[1:])))
        return (carry, (result.astype(jnp.bfloat16), grads[0]))
    start_sums = tuple((jnp.zeros_like(weight_arg) for weight_arg in params))
    sums, stacked = lax.scan(per_sequence, start_sums, (jnp.transpose(tokens, (1, 0, 2)), jnp.transpose(cotangent, (1, 0, 2))))
    activation = jnp.transpose(stacked[0], (1, 0, 2))
    input_grad = jnp.transpose(stacked[1], (1, 0, 2))
    return (activation, input_grad, sums[0], sums[1], sums[2], sums[3], sums[4], sums[5], sums[6], sums[7], sums[8])
```

```python
import functools
import numpy as np
import jax, jax.numpy as jnp
from jax import lax
from jax.sharding import PartitionSpec as P
import jax.experimental.pallas as pl
import jax.experimental.pallas.tpu as pltpu

MESH = pl.DeviceIdType.MESH
bf16 = jnp.bfloat16
f32 = jnp.float32
HEAD_DIM = 96
HALF = 48
epsilon = 1e-05
theta = 100000.0
LOG2E = 1.4426950408889634
SCALE = HEAD_DIM ** -0.5
VMEM_BYTES = 63 << 20

K_LANES = [list(range(0, 48)) + list(range(64, 112)), list(range(16, 64)) + list(range(80, 128))]
F_LANES = [list(range(48, 64)) + list(range(112, 128)), list(range(0, 16)) + list(range(64, 80))]
V_LANES = [list(range(0, 48)) + list(range(64, 80)), list(range(48, 64)) + list(range(80, 128))]


def pick_tables():
    q = np.zeros((384, 512), np.float32)
    kv = np.zeros((384, 384), np.float32)
    o = np.zeros((512, 384), np.float32)
    for h in range(4):
        for d in range(96):
            q[h * 96 + d, h * 128 + K_LANES[h // 2][d]] = 1
            lane = F_LANES[h // 2][d] if d < 32 else V_LANES[h // 2][d - 32]
            o[h * 128 + lane, h * 96 + d] = 1
    for g in range(2):
        for d in range(96):
            kv[g * 96 + d, g * 128 + K_LANES[g][d]] = 1
            lane = g * 128 + F_LANES[g][d] if d < 32 else 256 + V_LANES[g][d - 32]
            kv[192 + g * 96 + d, lane] = 1
    return q, kv, o


def in_ranges(lane, lanes):
    mask = None
    lo = prev = lanes[0]
    runs = []
    for x in lanes[1:] + [None]:
        if x is None or x != prev + 1:
            runs.append((lo, prev))
            lo = x
        prev = x
    for a, b in runs:
        m = jnp.logical_and(lane >= a, lane <= b)
        mask = m if mask is None else jnp.logical_or(mask, m)
    return mask


def rope_tables(row_start, span, t):
    rate = np.zeros((2, 128), np.float32)
    sign = np.zeros((2, 128), np.float32)
    for g in range(2):
        for d in range(96):
            rate[g, K_LANES[g][d]] = d % HALF
            sign[g, K_LANES[g][d]] = -1.0 if d < HALF else 1.0
    used = np.abs(sign)
    rates = used * theta ** (-(jnp.asarray(rate) * 2.0 / HEAD_DIM))
    i = jnp.arange(span, dtype=jnp.int32)
    c = span // 4
    places = (row_start + ((i // c) ^ t) * c + i % c).astype(f32)
    angle = places[None, :, None] * rates[:, None, :]
    return jnp.cos(angle), jnp.sin(angle) * sign[:, None, :]


def nt(a, b):
    return lax.dot_general(a, b, (((1,), (1,)), ((), ())), preferred_element_type=f32)


def nn(a, b):
    return jnp.dot(a, b, preferred_element_type=f32)


def tn(a, b):
    return lax.dot_general(a, b, (((0,), (0,)), ((), ())), preferred_element_type=f32)


def rc(src, dst, ss, rr, dev):
    return pltpu.make_async_remote_copy(src, dst, ss, rr, device_id=dev, device_id_type=MESH)


def entry(devs, z_line):
    b = pltpu.get_barrier_semaphore()
    count = len(devs)
    for dev in devs:
        pl.semaphore_signal(b, inc=1, device_id=dev, device_id_type=MESH)
    if z_line:
        zi = lax.axis_index("seq")
        nz = lax.axis_size("seq")
        @pl.when(zi > 0)
        def _():
            pl.semaphore_signal(b, inc=1, device_id={"seq": zi - 1}, device_id_type=MESH)
        @pl.when(zi < nz - 1)
        def _():
            pl.semaphore_signal(b, inc=1, device_id={"seq": zi + 1}, device_id_type=MESH)
        count = count + (zi > 0).astype(jnp.int32) + (zi < nz - 1).astype(jnp.int32)
    pl.semaphore_wait(b, count)


def causal(sT, qt, TQ, RP, t):
    span = sT.shape[0]
    ki = lax.broadcasted_iota(jnp.int32, (span, 1), 0)
    qi = lax.broadcasted_iota(jnp.int32, (1, TQ), 1) + (qt % (span // TQ)) * TQ
    kpos = ((ki // RP) ^ t) * RP + ki % RP
    qpos = ((qi // RP) ^ t) * RP + qi % RP
    return jnp.where(kpos <= qpos, sT, -1e30)


def rms(v, gain):
    return v * lax.rsqrt(jnp.mean(v * v, axis=-1, keepdims=True) + epsilon) * gain


def norm_back_rows(v, e, gain):
    inv = lax.rsqrt(jnp.mean(v * v, axis=-1, keepdims=True) + epsilon)
    part = jnp.sum(e * v * inv, axis=0, keepdims=True)
    sc = e * gain
    return part, inv * sc - v * (inv * inv * inv) * jnp.mean(sc * v, axis=-1, keepdims=True)


def forward_kernel(nz, tok, cot, wq, wk, wv, w_out, pq, pkv, po, cos, sin, gain1, gain2,
                   x1_out, c_out, q_out, kv_out, att_out, lse_out, wqkv_out, wo_out, mid_out, n2_out,
                   xn, X, C, KV, q, att, lse, wqkv, wo, m_s, l_s, o_s, part, rs1, ysend, rs2,
                   sA, rA, sB, rB, sC, rC, sKV, rKV, sR1, rR1, sR2, rR2, osem):
    t = lax.axis_index("tensor")
    zi = lax.axis_index("seq")
    sib, ynb = t ^ 1, t ^ 2
    S, RP, D = tok.shape
    SPAN = 4 * RP
    TQ = 256
    NT = 2 * SPAN // TQ
    g1 = gain1[...].astype(f32)
    for s in range(S):
        xn[s] = rms(tok[s].astype(f32), g1).astype(bf16)
    entry([{"tensor": sib}, {"tensor": ynb}], True)

    def ga(w, s):
        return rc((xn, cot)[w].at[s], (X, C)[w].at[s, 1], sA.at[w, s], rA.at[w, s], {"tensor": sib})
    def gb(w, s):
        return rc((xn, cot)[w].at[s], (X, C)[w].at[s, 2], sB.at[w, s], rB.at[w, s], {"tensor": ynb})
    def gc(w, s):
        buf = (X, C)[w]
        return rc(buf.at[s, 2], buf.at[s, 3], sC.at[w, s], rC.at[w, s], {"tensor": sib})
    for s in range(S):
        gb(0, s).start()
        ga(0, s).start()
    wqkv[:, 0:512] = nn(wq[...], pq[...]).astype(bf16)
    wqkv[:, 512:896] = (nn(wk[...], pkv[0:192, :]) + nn(wv[...], pkv[192:384, :])).astype(bf16)
    for s in range(S):
        X[s, 0] = xn[s]

    def kvc(s, j, hb):
        at = pl.ds(hb * 2 * RP, 2 * RP)
        return rc(KV.at[s, j, at], KV.at[s, j, at], sKV.at[s, j, hb], rKV.at[s, j, hb], {"seq": zi + 1})
    def send_own(s, hb):
        @pl.when(zi < nz - 1)
        def _():
            kvc(s, zi, hb).start()
    def arrive(s, h, hb):
        j = zi - 1 - h
        @pl.when(j >= 0)
        def _():
            kvc(s, j, hb).wait_recv()
            @pl.when(zi < nz - 1)
            def _():
                kvc(s, j, hb).start()

    def project(s, hb):
        r = nn(X[s, 2 * hb:2 * hb + 2].reshape(2 * RP, D), wqkv[...])
        base = hb * 2 * RP
        for slot in range(6):
            g = slot // 2 if slot < 4 else slot - 4
            u = r[:, slot * 128:(slot + 1) * 128]
            u = u * cos[g, base:base + 2 * RP, :] + pltpu.roll(u, 64, 1) * sin[g, base:base + 2 * RP, :]
            if slot < 4:
                q[s, g, (slot % 2) * SPAN + base:(slot % 2) * SPAN + base + 2 * RP, :] = u.astype(bf16)
            else:
                KV[s, zi, base:base + 2 * RP, g * 128:(g + 1) * 128] = u.astype(bf16)
        KV[s, zi, base:base + 2 * RP, 256:384] = r[:, 768:896].astype(bf16)

    def unit(s, j, diag):
        def tile(g, qt):
            qa = pl.ds(pl.multiple_of(qt * TQ, TQ), TQ)
            kp = KV[s, j, :, g * 128:(g + 1) * 128]
            sT = nt(kp, q[s, g, qa, :]) * (SCALE * LOG2E)
            if diag:
                sT = causal(sT, qt, TQ, RP, t)
            mx = jnp.max(sT, axis=0, keepdims=True)
            if diag:
                m = mx
            else:
                m0 = m_s[s, g, :, qa]
                m = jnp.maximum(m0, mx)
                al = jnp.exp2(m0 - m)
            p = jnp.exp2(sT - m)
            total = jnp.sum(p, axis=0, keepdims=True)
            kv = jnp.concatenate([kp, KV[s, j, :, 256:384]], axis=1)
            o = tn(kv, p.astype(bf16))
            m_s[s, g, :, qa] = m
            if diag:
                l_s[s, g, :, qa] = total
                o_s[s, g, :, qa] = o
            else:
                l_s[s, g, :, qa] = l_s[s, g, :, qa] * al + total
                o_s[s, g, :, qa] = o_s[s, g, :, qa] * al + o
        def body(qt, c):
            tile(0, qt)
            tile(1, qt)
            return c
        lax.fori_loop(0, NT, body, 0, unroll=2)
    def hop(s, h):
        @pl.when(zi - 1 - h >= 0)
        def _():
            unit(s, zi - 1 - h, False)

    def rs_a(s):
        return rc(part.at[s, 1], rs1.at[s], sR1.at[s], rR1.at[s], {"tensor": sib})
    def rs_b(s):
        return rc(ysend.at[s], rs2.at[s], sR2.at[s], rR2.at[s], {"tensor": ynb})
    def finish(s):
        lane = lax.broadcasted_iota(jnp.int32, (128, 1), 0)
        for g in range(2):
            lse[s, g] = m_s[s, g] + jnp.log2(l_s[s, g])
            fm = in_ranges(lane, F_LANES[g])
            vm = in_ranges(lane, V_LANES[g])
            o = jnp.where(fm, o_s[s, g, 0:128, :], jnp.where(vm, o_s[s, g, 128:256, :], 0.0)) * (1.0 / l_s[s, g])
            att[s, g] = o.T.astype(bf16)
        for par in (1, 0):
            a = jnp.concatenate([jnp.concatenate([att[s, g, hh * SPAN + r * RP:hh * SPAN + (r + 1) * RP, :]
                                                  for g in range(2) for hh in range(2)], axis=1) for r in (par, par + 2)], axis=0)
            part[s, par] = nn(a, wo[...]).astype(bf16).reshape(2, RP, D)
            if par == 1:
                rs_a(s).start()
    def rs_mid(s):
        rs_a(s).wait_recv()
        ysend[s] = (part[s, 0, 1].astype(f32) + rs1[s, 1].astype(f32)).astype(bf16)
        rs_b(s).start()
    def rs_end(s):
        rs_b(s).wait_recv()
        mid = tok[s].astype(f32) + part[s, 0, 0].astype(f32) + rs1[s, 0].astype(f32) + rs2[s].astype(f32)
        mid_out[s] = mid
        n2_out[s] = rms(mid, gain2[...].astype(f32)).astype(bf16)

    ga(0, 0).wait_recv()
    project(0, 0)
    send_own(0, 0)
    ga(0, 1).wait_recv()
    project(1, 0)
    wo[...] = nn(po[...], w_out[...]).astype(bf16)
    gb(0, 0).wait_recv()
    gc(0, 0).start()
    arrive(0, 0, 0)
    gc(0, 0).wait_recv()
    project(0, 1)
    send_own(0, 1)
    arrive(0, 1, 0)
    gb(0, 1).wait_recv()
    gc(0, 1).start()
    for s in range(S):
        gb(1, s).start()
        ga(1, s).start()
    unit(0, zi, True)
    arrive(0, 0, 1)
    gc(0, 1).wait_recv()
    project(1, 1)
    arrive(0, 1, 1)
    send_own(1, 0)
    send_own(1, 1)
    hop(0, 0)
    for h in range(2, nz - 1):
        arrive(0, h, 0)
        arrive(0, h, 1)
    for s in range(S):
        C[s, 0] = cot[s]
    def more(h, c):
        hop(0, h)
        return c
    hop(0, 1)
    arrive(1, 0, 0)
    arrive(1, 0, 1)
    lax.fori_loop(2, nz - 1, more, 0)
    finish(0)
    unit(1, zi, True)
    gb(1, 0).wait_recv()
    gc(1, 0).start()
    rs_mid(0)
    arrive(1, 1, 0)
    arrive(1, 1, 1)
    hop(1, 0)
    gb(1, 1).wait_recv()
    gc(1, 1).start()
    hop(1, 1)
    rs_end(0)
    def rest(h, c):
        arrive(1, h, 0)
        arrive(1, h, 1)
        hop(1, h)
        return c
    lax.fori_loop(2, nz - 1, rest, 0)
    finish(1)
    for s in range(S):
        gc(1, s).wait_recv()
        ga(1, s).wait_recv()
    outs = [pltpu.make_async_copy(a, o, osem.at[n]) for n, (a, o) in enumerate(
        ((X, x1_out), (C, c_out), (q, q_out), (KV, kv_out), (att, att_out), (lse, lse_out), (wqkv, wqkv_out), (wo, wo_out)))]
    for o in outs:
        o.start()
    rs_mid(1)
    rs_end(1)
    for s in range(S):
        for w in range(2):
            ga(w, s).wait_send()
            gb(w, s).wait_send()
            gc(w, s).wait_send()
        rs_a(s).wait_send()
        rs_b(s).wait_send()
        for j in range(nz):
            @pl.when(jnp.logical_and(j <= zi, zi < nz - 1))
            def _():
                for hb in range(2):
                    kvc(s, j, hb).wait_send()
    for o in outs:
        o.wait()


def attend_forward(tok, cot, wq, wk, wv, w_out, pq, pkv, po, cos, sin, gain1, gain2):
    nz = lax.axis_size("seq")
    S, RP, D = tok.shape
    SPAN = 4 * RP
    V = pl.BlockSpec(memory_space=pltpu.VMEM)
    A = pl.BlockSpec(memory_space=pl.ANY)
    sd = jax.ShapeDtypeStruct
    dma = pltpu.SemaphoreType.DMA
    vm = pltpu.VMEM
    return pl.pallas_call(
        functools.partial(forward_kernel, nz),
        out_shape=[sd((S, 4, RP, D), bf16), sd((S, 4, RP, D), bf16), sd((S, 2, 2 * SPAN, 128), bf16),
                   sd((S, nz, SPAN, 384), bf16), sd((S, 2, 2 * SPAN, 128), bf16), sd((S, 2, 1, 2 * SPAN), f32),
                   sd((D, 896), bf16), sd((512, D), bf16), sd((S, RP, D), f32), sd((S, RP, D), bf16)],
        in_specs=[V] * 13,
        out_specs=[A] * 8 + [V] * 2,
        scratch_shapes=[vm((S, RP, D), bf16), vm((S, 4, RP, D), bf16), vm((S, 4, RP, D), bf16),
                        vm((S, nz, SPAN, 384), bf16), vm((S, 2, 2 * SPAN, 128), bf16),
                        vm((S, 2, 2 * SPAN, 128), bf16), vm((S, 2, 1, 2 * SPAN), f32), vm((D, 896), bf16), vm((512, D), bf16),
                        vm((S, 2, 1, 2 * SPAN), f32), vm((S, 2, 1, 2 * SPAN), f32), vm((S, 2, 256, 2 * SPAN), f32),
                        vm((S, 2, 2, RP, D), bf16), vm((S, 2, RP, D), bf16), vm((S, RP, D), bf16), vm((S, RP, D), bf16)]
        + [dma((2, S))] * 6 + [dma((S, nz, 2))] * 2 + [dma((S,))] * 4 + [dma((8,))],
        compiler_params=pltpu.CompilerParams(collective_id=0, has_side_effects=True, vmem_limit_bytes=VMEM_BYTES),
        name="attend_forward")(tok, cot, wq, wk, wv, w_out, pq, pkv, po, cos, sin, gain1, gain2)


def feed_kernel(n2, mid, c_in, wg_in, wu_in, wd_in, gain2,
                db_out, ga_out, gb_out, down_out, dmid_out, gpart_out,
                X, C, DB, dn, wg, wu, wd, dh, F, G, part, rs1, ysend, rs2, pd,
                sA, rA, sB, rB, sC, rC, sR1, rR1, sR2, rR2, isem, osem):
    t = lax.axis_index("tensor")
    sib, ynb = t ^ 1, t ^ 2
    S, RP, D = n2.shape
    FL = wg.shape[1]
    loads = [pltpu.make_async_copy(a, b, isem.at[i]) for i, (a, b) in enumerate(
        ((wd_in, wd), (c_in, C), (wg_in, wg), (wu_in, wu)))]
    for c in loads:
        c.start()
    entry([{"tensor": sib}, {"tensor": ynb}], False)

    def ga(w, s):
        return rc((n2, dn)[w].at[s], (X, DB)[w].at[s, 1], sA.at[w, s], rA.at[w, s], {"tensor": sib})
    def gb(w, s):
        return rc((n2, dn)[w].at[s], (X, DB)[w].at[s, 2], sB.at[w, s], rB.at[w, s], {"tensor": ynb})
    def gc(w, s):
        buf = (X, DB)[w]
        return rc(buf.at[s, 2], buf.at[s, 3], sC.at[w, s], rC.at[w, s], {"tensor": sib})
    def ra(s, hb):
        return rc(part.at[s, 1, hb], rs1.at[s, hb], sR1.at[s, hb], rR1.at[s, hb], {"tensor": sib})
    def rb(s):
        return rc(ysend.at[s], rs2.at[s], sR2.at[s], rR2.at[s], {"tensor": ynb})
    for s in range(S):
        gb(0, s).start()
        ga(0, s).start()
    for s in range(S):
        X[s, 0] = n2[s]
    loads[0].wait()
    loads[1].wait()
    def early(s, c):
        dh[s] = nt(C[s].reshape(4 * RP, D), wd[...])
        return c
    lax.fori_loop(0, S, early, 0)
    loads[2].wait()
    loads[3].wait()

    def mlp(s, hb):
        x = X[s, pl.ds(2 * hb, 2)].reshape(2 * RP, D)
        rows = pl.ds(pl.multiple_of(hb * 2 * RP, 2 * RP), 2 * RP)
        g = nn(x, wg[...])
        u = nn(x, wu[...])
        sg = 1.0 / (1.0 + jnp.exp(-g))
        si = g * sg
        d = dh[s, rows]
        F[2, s, rows] = (si * u).astype(bf16)
        F[0, s, rows] = (d * u * sg * (1.0 + g * (1.0 - sg))).astype(bf16)
        F[1, s, rows] = (d * si).astype(bf16)
        r = nt(F[0, s, rows], wg[...]) + nt(F[1, s, rows], wu[...])
        part[s, 0, hb] = r[:RP].astype(bf16)
        part[s, 1, hb] = r[RP:].astype(bf16)
        ra(s, hb).start()
    def rs_mid(s):
        ra(s, 1).wait_recv()
        ysend[s] = (part[s, 0, 1].astype(f32) + rs1[s, 1].astype(f32)).astype(bf16)
        rb(s).start()
    gain = gain2[...].astype(f32)
    def rs_end(s):
        ra(s, 0).wait_recv()
        rb(s).wait_recv()
        e = part[s, 0, 0].astype(f32) + rs1[s, 0].astype(f32) + rs2[s].astype(f32)
        gp, dv = norm_back_rows(mid[s], e, gain)
        if s == 0:
            gpart_out[...] = gp
        else:
            gpart_out[...] += gp
        dm = C[s, 0].astype(f32) + dv
        dmid_out[s] = dm
        dn[s] = dm.astype(bf16)
        gb(1, s).start()
        ga(1, s).start()
        DB[s, 0] = dn[s]

    CH = 512
    def wgrad(a, src, f, c):
        at = pl.ds(pl.multiple_of(c * CH, CH), CH)
        left = src[:, :, :, at].reshape(S * 4 * RP, CH).T
        G[a, at, :] = nn(left, F[f].reshape(S * 4 * RP, FL)).astype(bf16)
    def down(s):
        r = nn(F[2, s], wd[...]).astype(bf16)
        for p in range(4):
            pd[t ^ p, s] = r[p * RP:(p + 1) * RP]

    ga(0, 0).wait_recv()
    mlp(0, 0)
    gb(0, 0).wait_recv()
    gc(0, 0).start()
    gc(0, 0).wait_recv()
    mlp(0, 1)
    ga(0, 1).wait_recv()
    gb(0, 1).wait_recv()
    gc(0, 1).start()
    rs_mid(0)
    mlp(1, 0)
    gc(0, 1).wait_recv()
    mlp(1, 1)
    rs_end(0)
    rs_mid(1)
    lax.fori_loop(0, D // CH, lambda c, x: (wgrad(2, C, 2, c), x)[1], 0)
    o_down = pltpu.make_async_copy(G.at[2], gb_out, osem.at[0])
    o_down.start()
    down(0)
    down(1)
    o_pd = pltpu.make_async_copy(pd, down_out, osem.at[1])
    o_pd.start()
    gb(1, 0).wait_recv()
    gc(1, 0).start()
    rs_end(1)
    lax.fori_loop(0, D // CH, lambda c, x: (wgrad(0, X, 0, c), x)[1], 0)
    lax.fori_loop(0, D // CH, lambda c, x: (wgrad(1, X, 1, c), x)[1], 0)
    o_up = pltpu.make_async_copy(G.at[pl.ds(0, 2)], ga_out, osem.at[2])
    o_up.start()
    gb(1, 1).wait_recv()
    gc(1, 1).start()
    for s in range(S):
        ga(1, s).wait_recv()
        gc(1, s).wait_recv()
    o_db = pltpu.make_async_copy(DB, db_out, osem.at[3])
    o_db.start()
    for s in range(S):
        for w in range(2):
            ga(w, s).wait_send()
            gb(w, s).wait_send()
            gc(w, s).wait_send()
        ra(s, 0).wait_send()
        ra(s, 1).wait_send()
        rb(s).wait_send()
    for o in (o_down, o_pd, o_up, o_db):
        o.wait()


def feed_forward(n2, mid, C, wg, wu, wd, gain2):
    S, RP, D = n2.shape
    FL = wg.shape[1]
    V = pl.BlockSpec(memory_space=pltpu.VMEM)
    A = pl.BlockSpec(memory_space=pl.ANY)
    sd = jax.ShapeDtypeStruct
    dma = pltpu.SemaphoreType.DMA
    vm = pltpu.VMEM
    return pl.pallas_call(
        feed_kernel,
        out_shape=[sd((S, 4, RP, D), bf16), sd((2, D, FL), bf16), sd((D, FL), bf16), sd((4, S, RP, D), bf16),
                   sd((S, RP, D), f32), sd((1, D), f32)],
        in_specs=[V, V, A, A, A, A, V],
        out_specs=[A, A, A, A, V, V],
        scratch_shapes=[vm((S, 4, RP, D), bf16), vm((S, 4, RP, D), bf16), vm((S, 4, RP, D), bf16), vm((S, RP, D), bf16),
                        vm((D, FL), bf16), vm((D, FL), bf16), vm((FL, D), bf16), vm((S, 4 * RP, FL), f32),
                        vm((3, S, 4 * RP, FL), bf16), vm((3, D, FL), bf16), vm((S, 2, 2, RP, D), bf16), vm((S, 2, RP, D), bf16),
                        vm((S, RP, D), bf16), vm((S, RP, D), bf16), vm((4, S, RP, D), bf16)]
        + [dma((2, S))] * 6 + [dma((S, 2))] * 2 + [dma((S,))] * 2 + [dma((4,)), dma((4,))],
        compiler_params=pltpu.CompilerParams(collective_id=1, has_side_effects=True, vmem_limit_bytes=VMEM_BYTES),
        name="feed_forward")(n2, mid, C, wg, wu, wd, gain2)


def line(u, nz):
    zi = lax.axis_index("seq")
    root = nz // 2 - 1 + u
    below, above = zi < root, zi > root
    dist = jnp.where(below, root - zi, zi - root)
    return dist, below, above, zi == root, jnp.where(below, zi + 1, zi - 1)


def both(a, b):
    return jnp.logical_and(a, b)


def add(*refs):
    total = refs[0][...].astype(f32)
    for r in refs[1:]:
        total = total + r[...].astype(f32)
    return total.astype(bf16)


class Flow:
    def setup(self, n, p, lag):
        self.n, self.p, self.lag = n, p, lag
        self.nz = lax.axis_size("seq")
        self.far = self.nz // 2
    def at(self, i):
        return pl.ds(pl.multiple_of(i * self.p, self.p), self.p)
    def valid(self, i):
        return both(i >= 0, i < self.n)
    def send_in(self, u, i, own, main, short, sems, act):
        dist, below, above, root, inward = line(u, self.nz)
        ss, rr, r2 = sems
        to_short = both(dist == 1, below if u == 0 else above)
        @pl.when(to_short)
        def _():
            act(rc(own, short.at[self.at(i)], ss.at[u, i], r2.at[i], {"seq": inward}))
        @pl.when(jnp.logical_not(to_short))
        def _():
            act(rc(own, main.at[u, self.at(i)], ss.at[u, i], rr.at[u, i], {"seq": inward}))
    def from_main(self, u, i, own, main, sems):
        ss, rr, r2 = sems
        rc(own, main.at[u, self.at(i)], ss.at[u, i], rr.at[u, i], {"seq": line(u, self.nz)[4]}).wait_recv()
    def from_short(self, u, i, own, short, sems):
        ss, rr, r2 = sems
        rc(own, short.at[self.at(i)], ss.at[u, i], r2.at[i], {"seq": line(u, self.nz)[4]}).wait_recv()
    def outward(self, u, i, buf, bs, br, act):
        zi = lax.axis_index("seq")
        dist, below, above, root, inward = line(u, self.nz)
        @pl.when(both(jnp.logical_not(above), zi > 0))
        def _():
            act(rc(buf.at[u, self.at(i)], buf.at[u, self.at(i)], bs.at[0, u, i], br.at[u, i], {"seq": zi - 1}))
        @pl.when(both(jnp.logical_not(below), zi < self.nz - 1))
        def _():
            act(rc(buf.at[u, self.at(i)], buf.at[u, self.at(i)], bs.at[1, u, i], br.at[u, i], {"seq": zi + 1}))
    def has_farther(self, u):
        zi = lax.axis_index("seq")
        dist, below, above, root, inward = line(u, self.nz)
        return jnp.logical_or(both(below, zi > 0), both(above, zi < self.nz - 1))


class HalfFirst(Flow):
    count = 11
    @staticmethod
    def scratch(n, p, C):
        vm = pltpu.VMEM
        dma = pltpu.SemaphoreType.DMA
        Q = n * p
        return [vm((2, Q, C), bf16), vm((2, Q, C), bf16), vm((Q, C), bf16),
                dma((n,)), dma((n,)), dma((2, n)), dma((2, n)), dma((n,)), dma((2, 2, n)), dma((2, n)), dma((2, 2, n))]
    def __init__(self, src, own, out, bufs, osem, n, p, lag):
        self.setup(n, p, lag)
        self.src, self.own, self.out, self.osem = src, own, out, osem
        self.RX, self.RZ, self.R2, self.x1s, self.x1r, self.rs, self.rr, self.r2, self.bs, self.br, self.x2 = bufs
        self.ticks = n + lag * (2 * self.far + 2)
    def tick(self, k):
        lag, far, RX, RZ, R2 = self.lag, self.far, self.RX, self.RZ, self.R2
        xi = lax.axis_index("dp")
        ox = 1 - xi
        sems = (self.rs, self.rr, self.r2)
        start = lambda c: c.start()
        def x1(i):
            return rc(self.src.at[ox, :, self.at(i)], RX.at[:, self.at(i)], self.x1s.at[i], self.x1r.at[i], {"dp": ox})
        def x2(u, i):
            return rc(RX.at[u, self.at(i)], self.out.at[xi, u, self.at(i)], self.x2.at[0, u, i], self.x2.at[1, u, i], {"dp": ox})
        @pl.when(self.valid(k))
        def _():
            x1(k).start()
        i1 = k - lag
        @pl.when(self.valid(i1))
        def _():
            x1(i1).wait()
            for u in range(2):
                own = self.own(u).at[self.at(i1)]
                own[...] = add(own, RX.at[u, self.at(i1)])
        for u in range(2):
            dist, below, above, root, inward = line(u, self.nz)
            i = k - lag * (1 + far - dist)
            @pl.when(self.valid(i))
            def _():
                own = self.own(u).at[self.at(i)]
                @pl.when(jnp.logical_not(root))
                def _():
                    @pl.when(self.has_farther(u))
                    def _():
                        self.from_main(u, i, own, RZ, sems)
                        own[...] = add(own, RZ.at[u, self.at(i)])
                    self.send_in(u, i, own, RZ, R2, sems, start)
                @pl.when(root)
                def _():
                    self.from_main(u, i, own, RZ, sems)
                    self.from_short(u, i, own, R2, sems)
                    RX[u, self.at(i)] = add(own, RZ.at[u, self.at(i)], R2.at[self.at(i)])
                    self.outward(u, i, RX, self.bs, self.br, start)
                    x2(u, i).start()
            i = k - lag * (1 + far + dist)
            @pl.when(both(self.valid(i), jnp.logical_not(root)))
            def _():
                rc(RX.at[u, self.at(i)], RX.at[u, self.at(i)], self.bs.at[0, u, i], self.br.at[u, i], {"seq": inward}).wait_recv()
                self.outward(u, i, RX, self.bs, self.br, start)
                x2(u, i).start()
            i = i - lag
            @pl.when(self.valid(i))
            def _():
                x2(u, i).wait()
                @pl.when(jnp.logical_not(root))
                def _():
                    self.send_in(u, i, self.own(u).at[self.at(i)], RZ, R2, sems, lambda c: c.wait_send())
                self.outward(u, i, RX, self.bs, self.br, lambda c: c.wait_send())
                pltpu.make_async_copy(RX.at[u, self.at(i)], self.out.at[xi, u, self.at(i)], self.osem).start()
    def drain(self):
        xi = lax.axis_index("dp")
        pltpu.make_async_copy(self.RX, self.out.at[xi], self.osem).wait()


class LineFirst(Flow):
    count = 11
    @staticmethod
    def scratch(n, p, C):
        vm = pltpu.VMEM
        dma = pltpu.SemaphoreType.DMA
        Q = n * p
        return [vm((2, Q, C), bf16), vm((2, Q, C), bf16), vm((Q, C), bf16), vm((Q, C), bf16),
                dma((2, n)), dma((2, n)), dma((n,)), dma((2, 2, n)), dma((2, n)), dma((n,)), dma((n,))]
    def __init__(self, out, bufs, osem, n, p, lag):
        self.setup(n, p, lag)
        self.out, self.osem = out, osem
        self.W, self.Z, self.XB, self.R2, self.rs, self.rr, self.r2, self.bs, self.br, self.xs, self.xr = bufs
        self.ticks = n + lag * (2 * self.far + 2)
    def tick(self, k):
        lag, far, W, Z = self.lag, self.far, self.W, self.Z
        ox = 1 - lax.axis_index("dp")
        sems = (self.rs, self.rr, self.r2)
        start = lambda c: c.start()
        def xb(u, i):
            return rc(W.at[u, self.at(i)], self.XB.at[self.at(i)], self.xs.at[i], self.xr.at[i], {"dp": ox})
        for u in range(2):
            dist, below, above, root, inward = line(u, self.nz)
            i = k - lag * (far - dist)
            @pl.when(self.valid(i))
            def _():
                own = W.at[u, self.at(i)]
                @pl.when(jnp.logical_not(root))
                def _():
                    @pl.when(self.has_farther(u))
                    def _():
                        self.from_main(u, i, own, Z, sems)
                        own[...] = add(own, Z.at[u, self.at(i)])
                    self.send_in(u, i, own, Z, self.R2, sems, start)
                @pl.when(root)
                def _():
                    self.from_main(u, i, own, Z, sems)
                    self.from_short(u, i, own, self.R2, sems)
                    own[...] = add(own, Z.at[u, self.at(i)], self.R2.at[self.at(i)])
                    xb(u, i).start()
            i = k - lag * (far + 1)
            @pl.when(both(self.valid(i), root))
            def _():
                xb(u, i).wait()
                Z[u, self.at(i)] = add(W.at[u, self.at(i)], self.XB.at[self.at(i)])
                self.outward(u, i, Z, self.bs, self.br, start)
            i = k - lag * (far + 1 + dist)
            @pl.when(both(self.valid(i), jnp.logical_not(root)))
            def _():
                rc(Z.at[u, self.at(i)], Z.at[u, self.at(i)], self.bs.at[0, u, i], self.br.at[u, i], {"seq": inward}).wait_recv()
                self.outward(u, i, Z, self.bs, self.br, start)
            i = i - lag
            @pl.when(self.valid(i))
            def _():
                @pl.when(jnp.logical_not(root))
                def _():
                    self.send_in(u, i, W.at[u, self.at(i)], Z, self.R2, sems, lambda c: c.wait_send())
                self.outward(u, i, Z, self.bs, self.br, lambda c: c.wait_send())
                pltpu.make_async_copy(Z.at[u, self.at(i)], self.out.at[u, self.at(i)], self.osem).start()
    def drain(self):
        pltpu.make_async_copy(self.Z, self.out, self.osem).wait()


def backward_kernel(summed, n1, n2, lag, db_in, q_in, kv_in, att_in, lse, wo_in, wt_in, x1_in, pq, pkv, po, cos, sin, tok, dmid_in, gain1, gp2,
                    ga_in, gb_in, ig_out, gains_out, oa, ob, oc, *scr):
    t = lax.axis_index("tensor")
    zi = lax.axis_index("seq")
    nz = lax.axis_size("seq")
    sib, ynb = t ^ 1, t ^ 2
    S, RP, D = tok.shape
    SPAN = 4 * RP
    TQ = 512
    NT = 2 * SPAN // TQ
    HC = D // 4
    scr = list(scr)
    (DB, q, KV, att, wbuf, da, delta, dqT, acc, PB, RB, dqkv, rs1, rs2, W3, GS, GL,
     sKV, rKV, sR1, rR1, sR2, rR2, sG, rG, isem, sems_out) = scr[:27]
    scr = scr[27:]
    xi = lax.axis_index("dp")
    rings = []
    loads = [pltpu.make_async_copy(a, b, isem.at[i]) for i, (a, b) in enumerate(
        ((db_in, DB), (wo_in, wbuf.at[pl.ds(0, 512)]), (att_in, att), (q_in, q), (kv_in, KV), (dmid_in, ig_out)))]
    first = []
    if summed:
        own = scr.pop(0)
        Q1 = own.shape[1]
        b1, scr = scr[:HalfFirst.count], scr[HalfFirst.count:]
        b2, scr = scr[:LineFirst.count], scr[LineFirst.count:]
        b3, scr = scr[:HalfFirst.count], scr[HalfFirst.count:]
        ring_a = HalfFirst(ga_in, lambda u: own.at[u], oa, b1, sems_out.at[0], n1, Q1 // n1, lag)
        ring_b = LineFirst(ob, b2, sems_out.at[1], n1, gb_in.shape[1] // n1, lag)
        ring_c = HalfFirst(W3, lambda u: W3.at[xi, u], oc, b3, sems_out.at[2], n2, HC // n2, lag)
        first = [pltpu.make_async_copy(ga_in.at[xi], own, isem.at[6]), pltpu.make_async_copy(gb_in, ring_b.W, isem.at[7])]
    wt_load = pltpu.make_async_copy(wt_in, wbuf, isem.at[8])
    x1_loads = [pltpu.make_async_copy(x1_in.at[:, :, pl.ds(c * HC, HC)], PB.at[pl.ds(S * c, S)], isem.at[9 + c]) for c in range(4)]
    for c in loads[:2] + first + loads[2:]:
        c.start()
    devs = [{"tensor": sib}, {"tensor": ynb}]
    if summed:
        devs.append({"dp": 1 - xi})
        b = 2
        while b < nz:
            devs.append({"seq": zi ^ b})
            b *= 2
    entry(devs, True)
    def tick(k):
        if summed:
            ring_a.tick(k)
            ring_b.tick(k)
    loads[0].wait()
    loads[1].wait()

    def dast(it, c):
        s = it // 2
        hb = it % 2
        r = nt(DB[s, pl.ds(2 * hb, 2)].reshape(2 * RP, D), wbuf[0:512, :])
        for h in range(4):
            rows = pl.ds(pl.multiple_of((h % 2) * SPAN + hb * 2 * RP, 2 * RP), 2 * RP)
            da[s, h // 2, rows, :] = r[:, h * 128:(h + 1) * 128].astype(bf16)
        @pl.when(it == 0)
        def _():
            for c2 in first:
                c2.wait()
        tick(it)
        return c
    lax.fori_loop(0, 2 * S, dast, 0)
    wt_load.start()
    k = 2 * S
    loads[2].wait()
    def dlt(it, c):
        s = it // 2
        g = it % 2
        d = da[s, g].astype(f32) * att[s, g].astype(f32)
        delta[s, g] = jnp.sum(d.T, axis=0, keepdims=True)
        dqT[s, g] = jnp.zeros((128, 2 * SPAN), f32)
        return c
    lax.fori_loop(0, 2 * S, dlt, 0)
    for c in loads[3:5]:
        c.wait()

    def unit(s, j, diag):
        lane = lax.broadcasted_iota(jnp.int32, (1, 128), 1)
        acc[...] = jnp.zeros((SPAN, 384), f32)
        for g in range(2):
            fm = in_ranges(lane, F_LANES[g])
            def body(qt, c):
                qa = pl.ds(pl.multiple_of(qt * TQ, TQ), TQ)
                kp = KV[s, j, :, g * 128:(g + 1) * 128]
                kv = jnp.concatenate([kp, KV[s, j, :, 256:384]], axis=1)
                qq = q[s, g, qa, :]
                d = da[s, g, qa, :]
                zero = jnp.zeros_like(d)
                d2 = jnp.concatenate([jnp.where(fm, d, zero), jnp.where(fm, zero, d)], axis=1)
                sT = nt(kp, qq) * (SCALE * LOG2E) - lse[s, g, :, qa]
                if diag:
                    sT = causal(sT, qt, TQ, RP, t)
                p = jnp.exp2(sT)
                ds = (p * (nt(kv, d2) - delta[s, g, :, qa])).astype(bf16)
                dk = nn(ds, qq) * SCALE
                dv = nn(p.astype(bf16), d2)
                acc[:, g * 128:(g + 1) * 128] += dk + dv[:, :128]
                acc[:, 256:384] += dv[:, 128:]
                dqT[s, g, :, qa] += tn(kp, ds)
                return c
            lax.fori_loop(0, NT, body, 0, unroll=2)
        PB[j * S + s] = acc[...].astype(bf16)

    def chain(s, j):
        return rc(RB.at[j, s], RB.at[j, s], sKV.at[j, s], rKV.at[j, s], {"seq": zi - 1})
    def event(e):
        j = e // S
        s = e % S
        @pl.when(both(both(e >= 0, e < nz * S), j <= zi))
        def _():
            acc[...] = PB[e].astype(f32)
            @pl.when(zi < nz - 1)
            def _():
                chain(s, j).wait_recv()
                acc[...] += RB[j, s].astype(f32)
            @pl.when(j < zi)
            def _():
                RB[j, s] = acc[...].astype(bf16)
                chain(s, j).start()
            @pl.when(j == zi)
            def _():
                for g in range(2):
                    u = acc[:, g * 128:(g + 1) * 128]
                    dqkv[s, :, 512 + g * 128:512 + (g + 1) * 128] = (u * cos[g] - pltpu.roll(u, 64, 1) * sin[g]).astype(bf16)
                dqkv[s, :, 768:896] = acc[:, 256:384].astype(bf16)
    def step(m, c):
        j = m // S
        s = m % S
        @pl.when(j < zi)
        def _():
            unit(s, j, False)
        @pl.when(j == zi)
        def _():
            unit(s, j, True)
        event(m - 1 - (nz - 1 - zi))
        tick(k + m)
        return c
    steps = nz * S + nz
    lax.fori_loop(0, steps, step, 0)
    k = k + steps
    for c in x1_loads:
        c.start()

    def out_grad(c, x):
        left = DB[:, :, :, pl.ds(pl.multiple_of(c * HC, HC), HC)].reshape(S * SPAN, HC).T
        heads = jnp.concatenate([jnp.concatenate([att[s, g, hh * SPAN:(hh + 1) * SPAN, :] for g in range(2) for hh in range(2)], axis=1)
                                 for s in range(S)], axis=0)
        g0 = nn(left, heads).astype(bf16)
        W3[c // 2, c % 2, :, 0:384] = nn(g0, po[...]).astype(bf16)
        s = c // 2
        for g in range(2):
            @pl.when(c % 2 == g)
            def _():
                for hh in range(2):
                    u = dqT[s, g, :, hh * SPAN:(hh + 1) * SPAN].T * SCALE
                    dqkv[s, :, (2 * g + hh) * 128:(2 * g + hh + 1) * 128] = (u * cos[g] - pltpu.roll(u, 64, 1) * sin[g]).astype(bf16)
        tick(k + c)
        return x
    lax.fori_loop(0, 4, out_grad, 0)
    k = k + 4
    wt_load.wait()

    def ra(s, hb):
        return rc(DB.at[s, 2 + hb], rs1.at[s, hb], sR1.at[s, hb], rR1.at[s, hb], {"tensor": sib})
    def rb(s):
        return rc(DB.at[s, 1], rs2.at[s], sR2.at[s], rR2.at[s], {"tensor": ynb})
    def d_one(it, c):
        s = it // 2
        hb = 1 - it % 2
        rows = pl.ds(pl.multiple_of(hb * 2 * RP, 2 * RP), 2 * RP)
        r = nn(dqkv[s, rows, :], wbuf[...])
        DB[s, hb] = r[:RP].astype(bf16)
        DB[s, 2 + hb] = r[RP:].astype(bf16)
        ra(s, hb).start()
        tick(k + it)
        return c
    lax.fori_loop(0, 2 * S, d_one, 0)
    k = k + 2 * S
    for s in range(S):
        ra(s, 1).wait_recv()
        DB[s, 1] = add(DB.at[s, 1], rs1.at[s, 1])
        rb(s).start()
    for c in x1_loads:
        c.wait()
    def in_grad(c, x):
        left = PB[pl.ds(S * c, S)].reshape(S * SPAN, HC).T
        g0 = nn(left, dqkv[...].reshape(S * SPAN, 896)).astype(bf16)
        W3[c // 2, c % 2, :, 384:768] = nt(g0[:, 0:512], pq[...]).astype(bf16)
        W3[c // 2, c % 2, :, 768:1152] = nt(g0[:, 512:896], pkv[...]).astype(bf16)
        tick(k + c)
        return x
    lax.fori_loop(0, 4, in_grad, 0)
    k = k + 4
    if summed:
        k_c = k
        def joint(m):
            tick(m)
            ring_c.tick(m - k_c)
    else:
        o3 = pltpu.make_async_copy(W3, oc, sems_out.at[2])
        o3.start()
        def joint(m):
            pass
    joint(k)
    joint(k + 1)
    k = k + 2
    loads[5].wait()
    gain = gain1[...].astype(f32)
    gp1 = None
    for s in range(S):
        ra(s, 0).wait_recv()
        rb(s).wait_recv()
        e = DB[s, 0].astype(f32) + rs1[s, 0].astype(f32) + rs2[s].astype(f32)
        gp, dv = norm_back_rows(tok[s].astype(f32), e, gain)
        gp1 = gp if gp1 is None else gp1 + gp
        ig_out[s] += dv
    gains_out[...] = jnp.concatenate([gp1, gp2[...], jnp.zeros((6, D), f32)], axis=0)
    if summed:
        peers = [{"tensor": sib}, {"tensor": ynb}, {"dp": 1 - xi}]
        b = 1
        while b < nz:
            peers.append({"seq": zi ^ b})
            b *= 2
        for m, dev in enumerate(peers):
            GS[m] = gains_out[...]
            c = rc(GS.at[m], GL.at[m], sG.at[m], rG.at[m], dev)
            c.start()
            joint(k)
            k = k + 1
            c.wait()
            gains_out[...] += GL[m]
        last = max(ring_a.ticks, ring_b.ticks, k_c + ring_c.ticks)
        lax.fori_loop(k, last, lambda m, c: (joint(m), c)[1], 0)
    for s in range(S):
        ra(s, 0).wait_send()
        ra(s, 1).wait_send()
        rb(s).wait_send()
        for j in range(nz):
            @pl.when(j < zi)
            def _():
                chain(s, j).wait_send()
    if summed:
        ring_a.drain()
        ring_b.drain()
        ring_c.drain()
    else:
        o3.wait()


def attend_backward(DB, q, KV, att, lse, wo, wt, X1, pq, pkv, po, cos, sin, tok, dmid, gain1, gp2, ga, gb, summed, n1=24, n2=12, lag=1):
    nz = lax.axis_size("seq")
    S, RP, D = tok.shape
    SPAN = 4 * RP
    FL = ga.shape[-1]
    HC = D // 4
    Q1 = ga.shape[0] * ga.shape[1] // 4
    Q2 = gb.shape[0] // 2
    V = pl.BlockSpec(memory_space=pltpu.VMEM)
    A = pl.BlockSpec(memory_space=pl.ANY)
    sd = jax.ShapeDtypeStruct
    dma = pltpu.SemaphoreType.DMA
    vm = pltpu.VMEM
    scratch = [vm(DB.shape, bf16), vm(q.shape, bf16), vm(KV.shape, bf16), vm(att.shape, bf16), vm((896, D), bf16),
               vm(q.shape, bf16), vm((S, 2, 1, 2 * SPAN), f32), vm((S, 2, 128, 2 * SPAN), f32), vm((SPAN, 384), f32),
               vm((nz * S, SPAN, 384), bf16), vm((nz - 1, S, SPAN, 384), bf16), vm((S, SPAN, 896), bf16),
               vm((S, 2, RP, D), bf16), vm((S, RP, D), bf16), vm((2, 2, HC, 1152), bf16), vm((6, 8, D), f32), vm((6, 8, D), f32),
               dma((nz, S)), dma((nz, S)), dma((S, 2)), dma((S, 2)), dma((S,)), dma((S,)), dma((6,)), dma((6,)), dma((13,)), dma((3,))]
    if summed:
        scratch += [vm((2, Q1, FL), bf16)] + HalfFirst.scratch(n1, Q1 // n1, FL) + LineFirst.scratch(n1, Q2 // n1, FL)
        scratch += HalfFirst.scratch(n2, HC // n2, 1152)
    return pl.pallas_call(
        functools.partial(backward_kernel, summed, n1, n2, lag),
        out_shape=[sd((S, RP, D), f32), sd((8, D), f32), sd((2, 2, Q1, FL), bf16), sd((2, Q2, FL), bf16), sd((2, 2, HC, 1152), bf16)],
        in_specs=[A, A, A, A, V, A, A, A, V, V, V, V, V, V, A, V, V, A, A],
        out_specs=[V, V, A, A, A],
        scratch_shapes=scratch,
        compiler_params=pltpu.CompilerParams(collective_id=2, has_side_effects=True, vmem_limit_bytes=VMEM_BYTES),
        name="attend_backward")(DB, q, KV, att, lse, wo, wt, X1.reshape(S, SPAN, D), pq, pkv, po, cos, sin, tok, dmid, gain1, gp2,
                                ga.reshape(2, 2, Q1, FL), gb.reshape(2, Q2, FL))


def local(
    tokens, attn_gain, w_query, w_key, w_value, w_output, ffn_gain, w_gate, w_up, w_down, cotangent
):
    t = lax.axis_index("tensor")
    zi = lax.axis_index("seq")
    kept = w_query.shape[1]
    kv = w_key.shape[1]
    pq, pkv, po = (jnp.asarray(v, bf16) for v in pick_tables())
    tok = jnp.swapaxes(tokens, 0, 1)
    cot = jnp.swapaxes(cotangent, 0, 1)
    S, RP, D = tok.shape
    cos, sin = rope_tables(zi * 4 * RP, 4 * RP, t)
    gain1 = attn_gain.reshape(1, -1)
    gain2 = ffn_gain.reshape(1, -1)
    X1, C, q, KV, att, lse, wqkv, wo, mid, n2 = attend_forward(
        tok, cot, w_query, w_key, w_value, w_output, pq, pkv, po, cos, sin, gain1, gain2)
    DB, ga, gb, down, dmid, gp2 = feed_forward(n2, mid, C, w_gate, w_up, w_down, gain2)
    down_local = lax.psum_scatter(down, "tensor", scatter_dimension=0, tiled=True)[0]
    summed = lax.axis_size("dp") == 2
    ig, gains, oa, ob, oc = attend_backward(
        DB, q, KV, att, lse, wo, wqkv.T, X1, pq, pkv, po, cos, sin, tok, dmid, gain1, gp2, ga, gb, summed)
    FL = w_gate.shape[1]
    if summed:
        gate_up, down_t = oa.reshape(2, D, FL).astype(f32), ob.reshape(D, FL).astype(f32)
        rest = oc.reshape(D, -1).astype(f32)
    else:
        gate_up, down_t, rest = lax.psum((ga.astype(f32), gb.astype(f32), oc.reshape(D, -1).astype(f32)), ("dp", "seq"))
        gains = lax.psum(gains, ("dp", "seq", "tensor"))
    activation = (mid + down_local.astype(f32)).astype(bf16)
    return (
        jnp.swapaxes(activation, 0, 1),
        jnp.swapaxes(ig, 0, 1),
        gains[0],
        rest[:, kept:2 * kept],
        rest[:, 2 * kept:2 * kept + kv],
        rest[:, 2 * kept + kv:],
        rest[:, :kept].T,
        gains[1],
        gate_up[0],
        gate_up[1],
        down_t.T,
    )


def solution(mesh):
    rows = P(("seq", "tensor"), "dp", None)
    columns = P(None, "tensor")
    placed = (rows, P(), columns, columns, columns, P("tensor", None), P(), columns, columns, P("tensor", None), rows)
    return jax.shard_map(
        local,
        mesh=mesh,
        in_specs=placed,
        out_specs=(rows, rows, P(), columns, columns, columns, P("tensor", None), P(), columns, columns, P("tensor", None)),
        check_vma=False,
    )
```

```python
import functools
import numpy as np
import jax, jax.numpy as jnp
from jax import lax
from jax.sharding import PartitionSpec as P
import jax.experimental.pallas as pl
import jax.experimental.pallas.tpu as pltpu

MESH = pl.DeviceIdType.MESH
bf16 = jnp.bfloat16
f32 = jnp.float32
HEAD_DIM = 96
HALF = 48
epsilon = 1e-05
theta = 100000.0
LOG2E = 1.4426950408889634
SCALE = HEAD_DIM ** -0.5
VMEM_BYTES = 63 << 20

K_LANES = [list(range(0, 48)) + list(range(64, 112)), list(range(16, 64)) + list(range(80, 128))]
F_LANES = [list(range(48, 64)) + list(range(112, 128)), list(range(0, 16)) + list(range(64, 80))]
V_LANES = [list(range(0, 48)) + list(range(64, 80)), list(range(48, 64)) + list(range(80, 128))]


def pick_tables():
    q = np.zeros((512, 384), np.float32)
    kv = np.zeros((384, 384), np.float32)
    o = np.zeros((384, 512), np.float32)
    for h in range(4):
        for d in range(96):
            q[h * 128 + K_LANES[h // 2][d], h * 96 + d] = 1
            lane = F_LANES[h // 2][d] if d < 32 else V_LANES[h // 2][d - 32]
            o[h * 96 + d, h * 128 + lane] = 1
    for g in range(2):
        for d in range(96):
            kv[g * 128 + K_LANES[g][d], g * 96 + d] = 1
            lane = g * 128 + F_LANES[g][d] if d < 32 else 256 + V_LANES[g][d - 32]
            kv[lane, 192 + g * 96 + d] = 1
    return q, kv, o


def in_ranges(lane, lanes):
    mask = None
    lo = prev = lanes[0]
    runs = []
    for x in lanes[1:] + [None]:
        if x is None or x != prev + 1:
            runs.append((lo, prev))
            lo = x
        prev = x
    for a, b in runs:
        m = jnp.logical_and(lane >= a, lane <= b)
        mask = m if mask is None else jnp.logical_or(mask, m)
    return mask


def rope_tables(row_start, span, t):
    rate = np.zeros((2, 128), np.float32)
    sign = np.zeros((2, 128), np.float32)
    for g in range(2):
        for d in range(96):
            rate[g, K_LANES[g][d]] = d % HALF
            sign[g, K_LANES[g][d]] = -1.0 if d < HALF else 1.0
    used = np.abs(sign)
    rates = used * theta ** (-(jnp.asarray(rate) * 2.0 / HEAD_DIM))
    i = jnp.arange(span, dtype=jnp.int32)
    c = span // 4
    places = (row_start + ((i // c) ^ t) * c + i % c).astype(f32)
    angle = places[None, :, None] * rates[:, None, :]
    return jnp.cos(angle), jnp.sin(angle) * sign[:, None, :]


def nt(a, b):
    return lax.dot_general(a, b, (((1,), (1,)), ((), ())), preferred_element_type=f32)


def nn(a, b):
    return jnp.dot(a, b, preferred_element_type=f32)


def tn(a, b):
    return lax.dot_general(a, b, (((0,), (0,)), ((), ())), preferred_element_type=f32)


def rc(src, dst, ss, rr, dev):
    return pltpu.make_async_remote_copy(src, dst, ss, rr, device_id=dev, device_id_type=MESH)


def entry(devs, z_line):
    b = pltpu.get_barrier_semaphore()
    count = len(devs)
    for dev in devs:
        pl.semaphore_signal(b, inc=1, device_id=dev, device_id_type=MESH)
    if z_line:
        zi = lax.axis_index("seq")
        nz = lax.axis_size("seq")
        @pl.when(zi > 0)
        def _():
            pl.semaphore_signal(b, inc=1, device_id={"seq": zi - 1}, device_id_type=MESH)
        @pl.when(zi < nz - 1)
        def _():
            pl.semaphore_signal(b, inc=1, device_id={"seq": zi + 1}, device_id_type=MESH)
        count = count + (zi > 0).astype(jnp.int32) + (zi < nz - 1).astype(jnp.int32)
    pl.semaphore_wait(b, count)


def causal(sT, qt, TQ, RP, t):
    span = sT.shape[0]
    ki = lax.broadcasted_iota(jnp.int32, (span, 1), 0)
    qi = lax.broadcasted_iota(jnp.int32, (1, TQ), 1) + (qt % (span // TQ)) * TQ
    kpos = ((ki // RP) ^ t) * RP + ki % RP
    qpos = ((qi // RP) ^ t) * RP + qi % RP
    return jnp.where(kpos <= qpos, sT, -1e30)


def rms(v, gain):
    return v * lax.rsqrt(jnp.mean(v * v, axis=-1, keepdims=True) + epsilon) * gain


def norm_back_rows(v, e, gain):
    inv = lax.rsqrt(jnp.mean(v * v, axis=-1, keepdims=True) + epsilon)
    part = jnp.sum(e * v * inv, axis=0, keepdims=True)
    sc = e * gain
    return part, inv * sc - v * (inv * inv * inv) * jnp.mean(sc * v, axis=-1, keepdims=True)


def forward_kernel(nz, tok, cot, wq, wk, wv, w_out, pq, pkv, po, cos, sin, gain1, gain2,
                   x1_out, c_out, q_out, kv_out, att_out, lse_out, wqkv_out, wo_out, mid_out, n2_out,
                   xn, X, C, KV, q, att, lse, wqkv, wo, m_s, l_s, o_s, part, rs1, ysend, rs2,
                   sA, rA, sB, rB, sC, rC, sKV, rKV, sR1, rR1, sR2, rR2, osem):
    t = lax.axis_index("tensor")
    zi = lax.axis_index("seq")
    sib, ynb = t ^ 1, t ^ 2
    S, RP, D = tok.shape
    SPAN = 4 * RP
    TQ = 256
    NT = 2 * SPAN // TQ
    g1 = gain1[...].astype(f32).reshape(1, D)
    for s in range(S):
        xn[s] = rms(tok[s].astype(f32), g1).astype(bf16)
    entry([{"tensor": sib}, {"tensor": ynb}], True)

    def ga(w, s):
        return rc((xn, cot)[w].at[s], (X, C)[w].at[s, 1], sA.at[w, s], rA.at[w, s], {"tensor": sib})
    def gb(w, s):
        return rc((xn, cot)[w].at[s], (X, C)[w].at[s, 2], sB.at[w, s], rB.at[w, s], {"tensor": ynb})
    def gc(w, s):
        buf = (X, C)[w]
        return rc(buf.at[s, 2], buf.at[s, 3], sC.at[w, s], rC.at[w, s], {"tensor": sib})
    for s in range(S):
        gb(0, s).start()
        ga(0, s).start()
    wqkv[0:512, :] = nt(pq[...], wq[...]).astype(bf16)
    wqkv[512:896, :] = (nn(pkv[:, 0:192], wk[...]) + nn(pkv[:, 192:384], wv[...])).astype(bf16)
    for s in range(S):
        X[s, 0] = xn[s]

    def kvc(s, j, hb):
        at = pl.ds(hb * 2 * RP, 2 * RP)
        return rc(KV.at[s, j, at], KV.at[s, j, at], sKV.at[s, j, hb], rKV.at[s, j, hb], {"seq": zi + 1})
    def send_own(s, hb):
        @pl.when(zi < nz - 1)
        def _():
            kvc(s, zi, hb).start()
    def arrive(s, h, hb):
        j = zi - 1 - h
        @pl.when(j >= 0)
        def _():
            kvc(s, j, hb).wait_recv()
            @pl.when(zi < nz - 1)
            def _():
                kvc(s, j, hb).start()

    def project(s, hb):
        r = nt(X[s, 2 * hb:2 * hb + 2].reshape(2 * RP, D), wqkv[...])
        base = hb * 2 * RP
        for slot in range(6):
            g = slot // 2 if slot < 4 else slot - 4
            u = r[:, slot * 128:(slot + 1) * 128]
            u = u * cos[g, base:base + 2 * RP, :] + pltpu.roll(u, 64, 1) * sin[g, base:base + 2 * RP, :]
            if slot < 4:
                q[s, g, (slot % 2) * SPAN + base:(slot % 2) * SPAN + base + 2 * RP, :] = u.astype(bf16)
            else:
                KV[s, zi, base:base + 2 * RP, g * 128:(g + 1) * 128] = u.astype(bf16)
        KV[s, zi, base:base + 2 * RP, 256:384] = r[:, 768:896].astype(bf16)

    def unit(s, j, diag):
        def tile(g, qt):
            qa = pl.ds(pl.multiple_of(qt * TQ, TQ), TQ)
            kp = KV[s, j, :, g * 128:(g + 1) * 128]
            sT = nt(kp, q[s, g, qa, :]) * (SCALE * LOG2E)
            if diag:
                sT = causal(sT, qt, TQ, RP, t)
            mx = jnp.max(sT, axis=0, keepdims=True)
            if diag:
                m = mx
            else:
                m0 = m_s[s, g, :, qa]
                m = jnp.maximum(m0, mx)
                al = jnp.exp2(m0 - m)
            p = jnp.exp2(sT - m)
            total = jnp.sum(p, axis=0, keepdims=True)
            kv = jnp.concatenate([kp, KV[s, j, :, 256:384]], axis=1)
            o = tn(kv, p.astype(bf16))
            m_s[s, g, :, qa] = m
            if diag:
                l_s[s, g, :, qa] = total
                o_s[s, g, :, qa] = o
            else:
                l_s[s, g, :, qa] = l_s[s, g, :, qa] * al + total
                o_s[s, g, :, qa] = o_s[s, g, :, qa] * al + o
        def body(qt, c):
            tile(0, qt)
            tile(1, qt)
            return c
        lax.fori_loop(0, NT, body, 0, unroll=2)
    def hop(s, h):
        @pl.when(zi - 1 - h >= 0)
        def _():
            unit(s, zi - 1 - h, False)

    def rs_a(s):
        return rc(part.at[s, 1], rs1.at[s], sR1.at[s], rR1.at[s], {"tensor": sib})
    def rs_b(s):
        return rc(ysend.at[s], rs2.at[s], sR2.at[s], rR2.at[s], {"tensor": ynb})
    def finish(s):
        lane = lax.broadcasted_iota(jnp.int32, (128, 1), 0)
        for g in range(2):
            lse[s, g] = m_s[s, g] + jnp.log2(l_s[s, g])
            fm = in_ranges(lane, F_LANES[g])
            vm = in_ranges(lane, V_LANES[g])
            o = jnp.where(fm, o_s[s, g, 0:128, :], jnp.where(vm, o_s[s, g, 128:256, :], 0.0)) * (1.0 / l_s[s, g])
            att[s, g] = o.T.astype(bf16)
        for par in (1, 0):
            a = jnp.concatenate([jnp.concatenate([att[s, g, hh * SPAN + r * RP:hh * SPAN + (r + 1) * RP, :]
                                                  for g in range(2) for hh in range(2)], axis=1) for r in (par, par + 2)], axis=0)
            part[s, par] = nn(a, wo[...]).astype(bf16).reshape(2, RP, D)
            if par == 1:
                rs_a(s).start()
    def rs_mid(s):
        rs_a(s).wait_recv()
        ysend[s] = (part[s, 0, 1].astype(f32) + rs1[s, 1].astype(f32)).astype(bf16)
        rs_b(s).start()
    def rs_end(s):
        rs_b(s).wait_recv()
        mid = tok[s].astype(f32) + part[s, 0, 0].astype(f32) + rs1[s, 0].astype(f32) + rs2[s].astype(f32)
        mid_out[s] = mid
        n2_out[s] = rms(mid, gain2[...].astype(f32).reshape(1, D)).astype(bf16)

    ga(0, 0).wait_recv()
    project(0, 0)
    send_own(0, 0)
    ga(0, 1).wait_recv()
    project(1, 0)
    wo[...] = tn(po[...], w_out[...]).astype(bf16)
    gb(0, 0).wait_recv()
    gc(0, 0).start()
    arrive(0, 0, 0)
    gc(0, 0).wait_recv()
    project(0, 1)
    send_own(0, 1)
    arrive(0, 1, 0)
    gb(0, 1).wait_recv()
    gc(0, 1).start()
    for s in range(S):
        gb(1, s).start()
        ga(1, s).start()
    unit(0, zi, True)
    arrive(0, 0, 1)
    gc(0, 1).wait_recv()
    project(1, 1)
    arrive(0, 1, 1)
    send_own(1, 0)
    send_own(1, 1)
    hop(0, 0)
    for h in range(2, nz - 1):
        arrive(0, h, 0)
        arrive(0, h, 1)
    for s in range(S):
        C[s, 0] = cot[s]
    def more(h, c):
        hop(0, h)
        return c
    hop(0, 1)
    arrive(1, 0, 0)
    arrive(1, 0, 1)
    lax.fori_loop(2, nz - 1, more, 0)
    finish(0)
    unit(1, zi, True)
    gb(1, 0).wait_recv()
    gc(1, 0).start()
    rs_mid(0)
    arrive(1, 1, 0)
    arrive(1, 1, 1)
    hop(1, 0)
    gb(1, 1).wait_recv()
    gc(1, 1).start()
    hop(1, 1)
    rs_end(0)
    def rest(h, c):
        arrive(1, h, 0)
        arrive(1, h, 1)
        hop(1, h)
        return c
    lax.fori_loop(2, nz - 1, rest, 0)
    finish(1)
    for s in range(S):
        gc(1, s).wait_recv()
        ga(1, s).wait_recv()
    outs = [pltpu.make_async_copy(a, o, osem.at[n]) for n, (a, o) in enumerate(
        ((X, x1_out), (C, c_out), (q, q_out), (KV, kv_out), (att, att_out), (lse, lse_out), (wqkv, wqkv_out), (wo, wo_out)))]
    for o in outs:
        o.start()
    rs_mid(1)
    rs_end(1)
    for s in range(S):
        for w in range(2):
            ga(w, s).wait_send()
            gb(w, s).wait_send()
            gc(w, s).wait_send()
        rs_a(s).wait_send()
        rs_b(s).wait_send()
        for j in range(nz):
            @pl.when(jnp.logical_and(j <= zi, zi < nz - 1))
            def _():
                for hb in range(2):
                    kvc(s, j, hb).wait_send()
    for o in outs:
        o.wait()


def attend_forward(tok, cot, wq, wk, wv, w_out, pq, pkv, po, cos, sin, gain1, gain2):
    nz = lax.axis_size("seq")
    S, RP, D = tok.shape
    SPAN = 4 * RP
    V = pl.BlockSpec(memory_space=pltpu.VMEM)
    A = pl.BlockSpec(memory_space=pl.ANY)
    sd = jax.ShapeDtypeStruct
    dma = pltpu.SemaphoreType.DMA
    vm = pltpu.VMEM
    return pl.pallas_call(
        functools.partial(forward_kernel, nz),
        out_shape=[sd((S, 4, RP, D), bf16), sd((S, 4, RP, D), bf16), sd((S, 2, 2 * SPAN, 128), bf16),
                   sd((S, nz, SPAN, 384), bf16), sd((S, 2, 2 * SPAN, 128), bf16), sd((S, 2, 1, 2 * SPAN), f32),
                   sd((896, D), bf16), sd((512, D), bf16), sd((S, RP, D), f32), sd((S, RP, D), bf16)],
        in_specs=[V] * 13,
        out_specs=[A] * 8 + [V] * 2,
        scratch_shapes=[vm((S, RP, D), bf16), vm((S, 4, RP, D), bf16), vm((S, 4, RP, D), bf16),
                        vm((S, nz, SPAN, 384), bf16), vm((S, 2, 2 * SPAN, 128), bf16),
                        vm((S, 2, 2 * SPAN, 128), bf16), vm((S, 2, 1, 2 * SPAN), f32), vm((896, D), bf16), vm((512, D), bf16),
                        vm((S, 2, 1, 2 * SPAN), f32), vm((S, 2, 1, 2 * SPAN), f32), vm((S, 2, 256, 2 * SPAN), f32),
                        vm((S, 2, 2, RP, D), bf16), vm((S, 2, RP, D), bf16), vm((S, RP, D), bf16), vm((S, RP, D), bf16)]
        + [dma((2, S))] * 6 + [dma((S, nz, 2))] * 2 + [dma((S,))] * 4 + [dma((8,))],
        compiler_params=pltpu.CompilerParams(collective_id=0, has_side_effects=True, vmem_limit_bytes=VMEM_BYTES),
        name="attend_forward")(tok, cot, wq, wk, wv, w_out, pq, pkv, po, cos, sin, gain1, gain2)


def feed_kernel(n2, mid, c_in, wg_in, wu_in, wd_in, gain2,
                db_out, ga_out, gb_out, down_out, dmid_out, gpart_out,
                X, C, DB, dn, wg, wu, wd, dh, F, G, GD, part, rs1, ysend, rs2, pd,
                sA, rA, sB, rB, sC, rC, sR1, rR1, sR2, rR2, isem, osem):
    t = lax.axis_index("tensor")
    sib, ynb = t ^ 1, t ^ 2
    S, RP, D = n2.shape
    FL = wg.shape[1]
    loads = [pltpu.make_async_copy(a, b, isem.at[i]) for i, (a, b) in enumerate(
        ((wd_in, wd), (c_in, C), (wg_in, wg), (wu_in, wu)))]
    for c in loads:
        c.start()
    entry([{"tensor": sib}, {"tensor": ynb}], False)

    def ga(w, s):
        return rc((n2, dn)[w].at[s], (X, DB)[w].at[s, 1], sA.at[w, s], rA.at[w, s], {"tensor": sib})
    def gb(w, s):
        return rc((n2, dn)[w].at[s], (X, DB)[w].at[s, 2], sB.at[w, s], rB.at[w, s], {"tensor": ynb})
    def gc(w, s):
        buf = (X, DB)[w]
        return rc(buf.at[s, 2], buf.at[s, 3], sC.at[w, s], rC.at[w, s], {"tensor": sib})
    def ra(s, hb):
        return rc(part.at[s, 1, hb], rs1.at[s, hb], sR1.at[s, hb], rR1.at[s, hb], {"tensor": sib})
    def rb(s):
        return rc(ysend.at[s], rs2.at[s], sR2.at[s], rR2.at[s], {"tensor": ynb})
    for s in range(S):
        gb(0, s).start()
        ga(0, s).start()
    for s in range(S):
        X[s, 0] = n2[s]
    loads[0].wait()
    loads[1].wait()
    def early(s, c):
        dh[s] = nt(C[s].reshape(4 * RP, D), wd[...])
        return c
    lax.fori_loop(0, S, early, 0)
    loads[2].wait()
    loads[3].wait()

    def mlp(s, hb):
        x = X[s, pl.ds(2 * hb, 2)].reshape(2 * RP, D)
        rows = pl.ds(pl.multiple_of(hb * 2 * RP, 2 * RP), 2 * RP)
        g = nn(x, wg[...])
        u = nn(x, wu[...])
        sg = 1.0 / (1.0 + jnp.exp(-g))
        si = g * sg
        d = dh[s, rows]
        F[2, s, rows] = (si * u).astype(bf16)
        F[0, s, rows] = (d * u * sg * (1.0 + g * (1.0 - sg))).astype(bf16)
        F[1, s, rows] = (d * si).astype(bf16)
        r = nt(F[0, s, rows], wg[...]) + nt(F[1, s, rows], wu[...])
        part[s, 0, hb] = r[:RP].astype(bf16)
        part[s, 1, hb] = r[RP:].astype(bf16)
        ra(s, hb).start()
    def rs_mid(s):
        ra(s, 1).wait_recv()
        ysend[s] = (part[s, 0, 1].astype(f32) + rs1[s, 1].astype(f32)).astype(bf16)
        rb(s).start()
    gain = gain2[...].astype(f32).reshape(1, D)
    def rs_end(s):
        ra(s, 0).wait_recv()
        rb(s).wait_recv()
        e = part[s, 0, 0].astype(f32) + rs1[s, 0].astype(f32) + rs2[s].astype(f32)
        gp, dv = norm_back_rows(mid[s], e, gain)
        if s == 0:
            gpart_out[...] = gp
        else:
            gpart_out[...] += gp
        dm = C[s, 0].astype(f32) + dv
        dmid_out[s] = dm
        dn[s] = dm.astype(bf16)
        gb(1, s).start()
        ga(1, s).start()
        DB[s, 0] = dn[s]

    CH = 512
    def wgrad(a, src, f, c):
        at = pl.ds(pl.multiple_of(c * CH, CH), CH)
        left = src[:, :, :, at].reshape(S * 4 * RP, CH).T
        G[a, at, :] = nn(left, F[f].reshape(S * 4 * RP, FL)).astype(bf16)
    half = FL // 2
    def dgrad(h):
        left = F[2, :, :, pl.ds(pl.multiple_of(h * half, half), half)].reshape(S * 4 * RP, half).T
        for c in range(D // CH):
            at = pl.ds(c * CH, CH)
            GD[h, :, at] = nn(left, C[:, :, :, at].reshape(S * 4 * RP, CH)).astype(bf16)
    def down(s):
        r = nn(F[2, s], wd[...]).astype(bf16)
        for p in range(4):
            pd[t ^ p, s] = r[p * RP:(p + 1) * RP]

    ga(0, 0).wait_recv()
    mlp(0, 0)
    gb(0, 0).wait_recv()
    gc(0, 0).start()
    gc(0, 0).wait_recv()
    mlp(0, 1)
    ga(0, 1).wait_recv()
    gb(0, 1).wait_recv()
    gc(0, 1).start()
    rs_mid(0)
    mlp(1, 0)
    gc(0, 1).wait_recv()
    mlp(1, 1)
    rs_end(0)
    rs_mid(1)
    lax.fori_loop(0, 2, lambda h, x: (dgrad(h), x)[1], 0)
    o_down = pltpu.make_async_copy(GD, gb_out, osem.at[0])
    o_down.start()
    down(0)
    down(1)
    o_pd = pltpu.make_async_copy(pd, down_out, osem.at[1])
    o_pd.start()
    gb(1, 0).wait_recv()
    gc(1, 0).start()
    rs_end(1)
    lax.fori_loop(0, D // CH, lambda c, x: (wgrad(0, X, 0, c), x)[1], 0)
    lax.fori_loop(0, D // CH, lambda c, x: (wgrad(1, X, 1, c), x)[1], 0)
    o_up = pltpu.make_async_copy(G, ga_out, osem.at[2])
    o_up.start()
    gb(1, 1).wait_recv()
    gc(1, 1).start()
    for s in range(S):
        ga(1, s).wait_recv()
        gc(1, s).wait_recv()
    o_db = pltpu.make_async_copy(DB, db_out, osem.at[3])
    o_db.start()
    for s in range(S):
        for w in range(2):
            ga(w, s).wait_send()
            gb(w, s).wait_send()
            gc(w, s).wait_send()
        ra(s, 0).wait_send()
        ra(s, 1).wait_send()
        rb(s).wait_send()
    for o in (o_down, o_pd, o_up, o_db):
        o.wait()


def feed_forward(n2, mid, C, wg, wu, wd, gain2):
    S, RP, D = n2.shape
    FL = wg.shape[1]
    V = pl.BlockSpec(memory_space=pltpu.VMEM)
    A = pl.BlockSpec(memory_space=pl.ANY)
    sd = jax.ShapeDtypeStruct
    dma = pltpu.SemaphoreType.DMA
    vm = pltpu.VMEM
    return pl.pallas_call(
        feed_kernel,
        out_shape=[sd((S, 4, RP, D), bf16), sd((2, D, FL), bf16), sd((2, FL // 2, D), bf16), sd((4, S, RP, D), bf16),
                   sd((S, RP, D), f32), sd((1, D), f32)],
        in_specs=[V, V, A, A, A, A, V],
        out_specs=[A, A, A, A, V, V],
        scratch_shapes=[vm((S, 4, RP, D), bf16), vm((S, 4, RP, D), bf16), vm((S, 4, RP, D), bf16), vm((S, RP, D), bf16),
                        vm((D, FL), bf16), vm((D, FL), bf16), vm((FL, D), bf16), vm((S, 4 * RP, FL), f32),
                        vm((3, S, 4 * RP, FL), bf16), vm((2, D, FL), bf16), vm((2, FL // 2, D), bf16), vm((S, 2, 2, RP, D), bf16), vm((S, 2, RP, D), bf16),
                        vm((S, RP, D), bf16), vm((S, RP, D), bf16), vm((4, S, RP, D), bf16)]
        + [dma((2, S))] * 6 + [dma((S, 2))] * 2 + [dma((S,))] * 2 + [dma((4,)), dma((4,))],
        compiler_params=pltpu.CompilerParams(collective_id=1, has_side_effects=True, vmem_limit_bytes=VMEM_BYTES),
        name="feed_forward")(n2, mid, C, wg, wu, wd, gain2)


def line(u, nz):
    zi = lax.axis_index("seq")
    root = nz // 2 - 1 + u
    below, above = zi < root, zi > root
    dist = jnp.where(below, root - zi, zi - root)
    return dist, below, above, zi == root, jnp.where(below, zi + 1, zi - 1)


def both(a, b):
    return jnp.logical_and(a, b)


def add(*refs):
    total = refs[0][...].astype(f32)
    for r in refs[1:]:
        total = total + r[...].astype(f32)
    return total.astype(bf16)


class Flow:
    def setup(self, n, p, lag):
        self.n, self.p, self.lag = n, p, lag
        self.nz = lax.axis_size("seq")
        self.far = self.nz // 2
    def at(self, i):
        return pl.ds(pl.multiple_of(i * self.p, self.p), self.p)
    def valid(self, i):
        return both(i >= 0, i < self.n)
    def send_in(self, u, i, own, main, short, sems, act):
        dist, below, above, root, inward = line(u, self.nz)
        ss, rr, r2 = sems
        to_short = both(dist == 1, below if u == 0 else above)
        @pl.when(to_short)
        def _():
            act(rc(own, short.at[self.at(i)], ss.at[u, i], r2.at[i], {"seq": inward}))
        @pl.when(jnp.logical_not(to_short))
        def _():
            act(rc(own, main.at[u, self.at(i)], ss.at[u, i], rr.at[u, i], {"seq": inward}))
    def from_main(self, u, i, own, main, sems):
        ss, rr, r2 = sems
        rc(own, main.at[u, self.at(i)], ss.at[u, i], rr.at[u, i], {"seq": line(u, self.nz)[4]}).wait_recv()
    def from_short(self, u, i, own, short, sems):
        ss, rr, r2 = sems
        rc(own, short.at[self.at(i)], ss.at[u, i], r2.at[i], {"seq": line(u, self.nz)[4]}).wait_recv()
    def outward(self, u, i, buf, bs, br, act):
        zi = lax.axis_index("seq")
        dist, below, above, root, inward = line(u, self.nz)
        @pl.when(both(jnp.logical_not(above), zi > 0))
        def _():
            act(rc(buf.at[u, self.at(i)], buf.at[u, self.at(i)], bs.at[0, u, i], br.at[u, i], {"seq": zi - 1}))
        @pl.when(both(jnp.logical_not(below), zi < self.nz - 1))
        def _():
            act(rc(buf.at[u, self.at(i)], buf.at[u, self.at(i)], bs.at[1, u, i], br.at[u, i], {"seq": zi + 1}))
    def has_farther(self, u):
        zi = lax.axis_index("seq")
        dist, below, above, root, inward = line(u, self.nz)
        return jnp.logical_or(both(below, zi > 0), both(above, zi < self.nz - 1))


class HalfFirst(Flow):
    count = 11
    @staticmethod
    def scratch(n, p, C):
        vm = pltpu.VMEM
        dma = pltpu.SemaphoreType.DMA
        Q = n * p
        return [vm((2, Q, C), bf16), vm((2, Q, C), bf16), vm((Q, C), bf16),
                dma((n,)), dma((n,)), dma((2, n)), dma((2, n)), dma((n,)), dma((2, 2, n)), dma((2, n)), dma((2, 2, n))]
    def __init__(self, src, own, out, bufs, osem, n, p, lag, ahead=False):
        self.setup(n, p, lag)
        self.src, self.own, self.out, self.osem = src, own, out, osem
        self.ahead = ahead
        self.RX, self.RZ, self.R2, self.x1s, self.x1r, self.rs, self.rr, self.r2, self.bs, self.br, self.x2 = bufs
        self.ticks = n + lag * (2 * self.far + 2)
    def tick(self, k):
        lag, far, RX, RZ, R2 = self.lag, self.far, self.RX, self.RZ, self.R2
        xi = lax.axis_index("dp")
        ox = 1 - xi
        sems = (self.rs, self.rr, self.r2)
        start = lambda c: c.start()
        def x1(i):
            return rc(self.src.at[ox, :, self.at(i)], RX.at[:, self.at(i)], self.x1s.at[i], self.x1r.at[i], {"dp": ox})
        def x2(u, i):
            return rc(RX.at[u, self.at(i)], self.out.at[xi, u, self.at(i)], self.x2.at[0, u, i], self.x2.at[1, u, i], {"dp": ox})
        @pl.when(k == 0 if self.ahead else self.valid(k))
        def _():
            if self.ahead:
                lax.fori_loop(0, self.n, lambda i, c: (x1(i).start(), c)[1], 0)
            else:
                x1(k).start()
        i1 = k - lag
        @pl.when(self.valid(i1))
        def _():
            x1(i1).wait()
            for u in range(2):
                own = self.own(u).at[self.at(i1)]
                own[...] = add(own, RX.at[u, self.at(i1)])
        for u in range(2):
            dist, below, above, root, inward = line(u, self.nz)
            i = k - lag * (1 + far - dist)
            @pl.when(self.valid(i))
            def _():
                own = self.own(u).at[self.at(i)]
                @pl.when(jnp.logical_not(root))
                def _():
                    @pl.when(self.has_farther(u))
                    def _():
                        self.from_main(u, i, own, RZ, sems)
                        own[...] = add(own, RZ.at[u, self.at(i)])
                    self.send_in(u, i, own, RZ, R2, sems, start)
                @pl.when(root)
                def _():
                    self.from_main(u, i, own, RZ, sems)
                    self.from_short(u, i, own, R2, sems)
                    RX[u, self.at(i)] = add(own, RZ.at[u, self.at(i)], R2.at[self.at(i)])
                    self.outward(u, i, RX, self.bs, self.br, start)
                    x2(u, i).start()
            i = k - lag * (1 + far + dist)
            @pl.when(both(self.valid(i), jnp.logical_not(root)))
            def _():
                rc(RX.at[u, self.at(i)], RX.at[u, self.at(i)], self.bs.at[0, u, i], self.br.at[u, i], {"seq": inward}).wait_recv()
                self.outward(u, i, RX, self.bs, self.br, start)
                x2(u, i).start()
            i = i - lag
            @pl.when(self.valid(i))
            def _():
                x2(u, i).wait()
                @pl.when(jnp.logical_not(root))
                def _():
                    self.send_in(u, i, self.own(u).at[self.at(i)], RZ, R2, sems, lambda c: c.wait_send())
                self.outward(u, i, RX, self.bs, self.br, lambda c: c.wait_send())
                pltpu.make_async_copy(RX.at[u, self.at(i)], self.out.at[xi, u, self.at(i)], self.osem).start()
    def drain(self):
        xi = lax.axis_index("dp")
        pltpu.make_async_copy(self.RX, self.out.at[xi], self.osem).wait()


class LineFirst(Flow):
    count = 10
    @staticmethod
    def scratch(n, p, C):
        vm = pltpu.VMEM
        dma = pltpu.SemaphoreType.DMA
        Q = n * p
        return [vm((2, Q, C), bf16), vm((Q, C), bf16), vm((Q, C), bf16),
                dma((2, n)), dma((2, n)), dma((n,)), dma((2, 2, n)), dma((2, n)), dma((n,)), dma((n,))]
    def __init__(self, W, out, bufs, osem, n, p, lag):
        self.setup(n, p, lag)
        self.W, self.out, self.osem = W, out, osem
        self.Z, self.XB, self.R2, self.rs, self.rr, self.r2, self.bs, self.br, self.xs, self.xr = bufs
        self.ticks = n + lag * (2 * self.far + 2)
    def tick(self, k):
        lag, far, W, Z = self.lag, self.far, self.W, self.Z
        ox = 1 - lax.axis_index("dp")
        sems = (self.rs, self.rr, self.r2)
        start = lambda c: c.start()
        def xb(u, i):
            return rc(W.at[u, self.at(i)], self.XB.at[self.at(i)], self.xs.at[i], self.xr.at[i], {"dp": ox})
        for u in range(2):
            dist, below, above, root, inward = line(u, self.nz)
            i = k - lag * (far - dist)
            @pl.when(self.valid(i))
            def _():
                own = W.at[u, self.at(i)]
                @pl.when(jnp.logical_not(root))
                def _():
                    @pl.when(self.has_farther(u))
                    def _():
                        self.from_main(u, i, own, Z, sems)
                        own[...] = add(own, Z.at[u, self.at(i)])
                    self.send_in(u, i, own, Z, self.R2, sems, start)
                @pl.when(root)
                def _():
                    self.from_main(u, i, own, Z, sems)
                    self.from_short(u, i, own, self.R2, sems)
                    own[...] = add(own, Z.at[u, self.at(i)], self.R2.at[self.at(i)])
                    xb(u, i).start()
            i = k - lag * (far + 1)
            @pl.when(both(self.valid(i), root))
            def _():
                xb(u, i).wait()
                Z[u, self.at(i)] = add(W.at[u, self.at(i)], self.XB.at[self.at(i)])
                self.outward(u, i, Z, self.bs, self.br, start)
            i = k - lag * (far + 1 + dist)
            @pl.when(both(self.valid(i), jnp.logical_not(root)))
            def _():
                rc(Z.at[u, self.at(i)], Z.at[u, self.at(i)], self.bs.at[0, u, i], self.br.at[u, i], {"seq": inward}).wait_recv()
                self.outward(u, i, Z, self.bs, self.br, start)
            i = i - lag
            @pl.when(self.valid(i))
            def _():
                @pl.when(jnp.logical_not(root))
                def _():
                    self.send_in(u, i, W.at[u, self.at(i)], Z, self.R2, sems, lambda c: c.wait_send())
                self.outward(u, i, Z, self.bs, self.br, lambda c: c.wait_send())
                pltpu.make_async_copy(Z.at[u, self.at(i)], self.out.at[u, self.at(i)], self.osem).start()
    def drain(self):
        pltpu.make_async_copy(self.Z, self.out, self.osem).wait()


NO = 192
CROWS = 6 * NO
HOP = 2


def backward_kernel(summed, plan, db_in, q_in, kv_in, att_in, lse, wo_in, wt_in, x1_in, pq, pkv, po, cos, sin, tok, dmid_in, gain1, gp2,
                    g_in, gd_in, ig_out, gains_out, o_gate, o_up, o_down, o_rest, *scr):
    t = lax.axis_index("tensor")
    zi = lax.axis_index("seq")
    nz = lax.axis_size("seq")
    sib, ynb = t ^ 1, t ^ 2
    S, RP, D = tok.shape
    SPAN = 4 * RP
    TQ = 512
    NT = 2 * SPAN // TQ
    HC = D // 4
    QC = CROWS // 4
    scr = list(scr)
    (DB, q, KV, att, wbuf, da, delta, dqT, acc, PB, RB, dqkv, rs1, rs2, W3, heads, GS, GL,
     sKV, rKV, sR1, rR1, sR2, rR2, sG, rG, isem, sems_out) = scr[:28]
    scr = scr[28:]
    xi = lax.axis_index("dp")
    rings = []
    loads = [pltpu.make_async_copy(a, b, isem.at[i]) for i, (a, b) in enumerate(
        ((db_in, DB), (wo_in, wbuf.at[pl.ds(0, 512)]), (att_in, att), (q_in, q), (kv_in, KV), (dmid_in, ig_out)))]
    first = []
    if summed:
        def take(cls):
            got = scr[:cls.count]
            del scr[:cls.count]
            return got
        own_g, own_d, WU = scr.pop(0), scr.pop(0), scr.pop(0)
        def make(name, cls, *a):
            n, lag, off, pace, *ahead = plan[name]
            return cls(*a[:-1], take(cls), sems_out.at[len(rings)], n, a[-1] // n, lag, *ahead), off, pace
        rings.append(make("gate", HalfFirst, g_in.at[0], lambda u: own_g.at[u], o_gate, own_g.shape[1]))
        rings.append(make("down", HalfFirst, gd_in, lambda u: own_d.at[u], o_down, own_d.shape[1]))
        rings.append(make("up", LineFirst, WU, o_up, WU.shape[1]))
        rings.append(make("rest", HalfFirst, W3, lambda u: W3.at[xi, u], o_rest, QC))
        first = [pltpu.make_async_copy(g_in.at[0, xi], own_g, isem.at[6]), pltpu.make_async_copy(gd_in.at[xi], own_d, isem.at[7])]
        QG = own_g.shape[1]
        for u in range(2):
            for h in range(2):
                first.append(pltpu.make_async_copy(g_in.at[1, u, h], WU.at[u, pl.ds(h * QG, QG)], isem.at[13 + 2 * u + h]))
    def tick(g):
        for ring, off, pace in rings[:3]:
            if pace == 1:
                ring.tick(g - off)
            else:
                @pl.when((g - off) % pace == 0)
                def _():
                    ring.tick((g - off) // pace)
    wt_load = pltpu.make_async_copy(wt_in, wbuf, isem.at[8])
    x1_loads = [pltpu.make_async_copy(x1_in.at[:, :, pl.ds(c * HC, HC)], PB.at[pl.ds(S * c, S)], isem.at[9 + c]) for c in range(4)]
    for c in loads[:2] + first + loads[2:]:
        c.start()
    devs = [{"tensor": sib}, {"tensor": ynb}]
    if summed:
        devs.append({"dp": 1 - xi})
        b = 2
        while b < nz:
            devs.append({"seq": zi ^ b})
            b *= 2
    entry(devs, True)
    loads[0].wait()
    loads[1].wait()

    def dast(it, c):
        s = it // 2
        hb = it % 2
        r = nt(DB[s, pl.ds(2 * hb, 2)].reshape(2 * RP, D), wbuf[0:512, :])
        for h in range(4):
            rows = pl.ds(pl.multiple_of((h % 2) * SPAN + hb * 2 * RP, 2 * RP), 2 * RP)
            da[s, h // 2, rows, :] = r[:, h * 128:(h + 1) * 128].astype(bf16)
        @pl.when(it == 0)
        def _():
            for c2 in first:
                c2.wait()
        tick(it)
        return c
    lax.fori_loop(0, 2 * S, dast, 0)
    wt_load.start()
    k = 2 * S
    loads[2].wait()
    def dlt(it, c):
        s = it // 2
        g = it % 2
        d = da[s, g].astype(f32) * att[s, g].astype(f32)
        delta[s, g] = jnp.sum(d.T, axis=0, keepdims=True)
        dqT[s, g] = jnp.zeros((128, 2 * SPAN), f32)
        return c
    lax.fori_loop(0, 2 * S, dlt, 0)
    for c in loads[3:5]:
        c.wait()

    def unit(s, j, diag):
        lane = lax.broadcasted_iota(jnp.int32, (1, 128), 1)
        acc[...] = jnp.zeros((SPAN, 384), f32)
        for g in range(2):
            fm = in_ranges(lane, F_LANES[g])
            def body(qt, c):
                qa = pl.ds(pl.multiple_of(qt * TQ, TQ), TQ)
                kp = KV[s, j, :, g * 128:(g + 1) * 128]
                kv = jnp.concatenate([kp, KV[s, j, :, 256:384]], axis=1)
                qq = q[s, g, qa, :]
                d = da[s, g, qa, :]
                zero = jnp.zeros_like(d)
                d2 = jnp.concatenate([jnp.where(fm, d, zero), jnp.where(fm, zero, d)], axis=1)
                sT = nt(kp, qq) * (SCALE * LOG2E) - lse[s, g, :, qa]
                if diag:
                    sT = causal(sT, qt, TQ, RP, t)
                p = jnp.exp2(sT)
                ds = (p * (nt(kv, d2) - delta[s, g, :, qa])).astype(bf16)
                dk = nn(ds, qq) * SCALE
                dv = nn(p.astype(bf16), d2)
                acc[:, g * 128:(g + 1) * 128] += dk + dv[:, :128]
                acc[:, 256:384] += dv[:, 128:]
                dqT[s, g, :, qa] += tn(kp, ds)
                return c
            lax.fori_loop(0, NT, body, 0, unroll=2)
        PB[j * S + s] = acc[...].astype(bf16)

    def chain(s, j):
        return rc(RB.at[j, s], RB.at[j, s], sKV.at[j, s], rKV.at[j, s], {"seq": zi - 1})
    def event(e):
        j = e // S
        s = e % S
        @pl.when(both(both(e >= 0, e < nz * S), j <= zi))
        def _():
            acc[...] = PB[e].astype(f32)
            @pl.when(zi < nz - 1)
            def _():
                chain(s, j).wait_recv()
                acc[...] += RB[j, s].astype(f32)
            @pl.when(j < zi)
            def _():
                RB[j, s] = acc[...].astype(bf16)
                chain(s, j).start()
            @pl.when(j == zi)
            def _():
                for g in range(2):
                    u = acc[:, g * 128:(g + 1) * 128]
                    dqkv[s, :, 512 + g * 128:512 + (g + 1) * 128] = (u * cos[g] - pltpu.roll(u, 64, 1) * sin[g]).astype(bf16)
                dqkv[s, :, 768:896] = acc[:, 256:384].astype(bf16)
    def step(m, c):
        j = m // S
        s = m % S
        @pl.when(j < zi)
        def _():
            unit(s, j, False)
        @pl.when(j == zi)
        def _():
            unit(s, j, True)
        event(m - 1 - HOP * (nz - 1 - zi))
        tick(k + m)
        return c
    steps = nz * S + 1 + HOP * (nz - 1)
    lax.fori_loop(0, steps, step, 0)
    k = k + steps
    for c in x1_loads:
        c.start()

    def put(row, at, value):
        lo = 0
        while lo < value.shape[0]:
            blk, r = (row + lo) // QC, (row + lo) % QC
            cnt = min(value.shape[0] - lo, QC - r)
            W3[blk // 2, blk % 2, r:r + cnt, at] = value[lo:lo + cnt, :]
            lo += cnt
    for s in range(S):
        for r in range(4):
            heads[s * SPAN:(s + 1) * SPAN, r * 128:(r + 1) * 128] = att[s, r // 2, (r % 2) * SPAN:(r % 2 + 1) * SPAN, :]
    def out_grad(c, x):
        at = pl.ds(pl.multiple_of(c * HC, HC), HC)
        g0 = nn(heads[...].T, DB[:, :, :, at].reshape(S * SPAN, HC)).astype(bf16)
        g0 = nn(po[...], g0).astype(bf16)
        put(4 * NO, at, g0)
        s = c // 2
        for g in range(2):
            @pl.when(c % 2 == g)
            def _():
                for hh in range(2):
                    u = dqT[s, g, :, hh * SPAN:(hh + 1) * SPAN].T * SCALE
                    dqkv[s, :, (2 * g + hh) * 128:(2 * g + hh + 1) * 128] = (u * cos[g] - pltpu.roll(u, 64, 1) * sin[g]).astype(bf16)
        tick(k + c)
        return x
    lax.fori_loop(0, 4, out_grad, 0)
    k = k + 4
    wt_load.wait()

    def ra(s, hb):
        return rc(DB.at[s, 2 + hb], rs1.at[s, hb], sR1.at[s, hb], rR1.at[s, hb], {"tensor": sib})
    def rb(s):
        return rc(DB.at[s, 1], rs2.at[s], sR2.at[s], rR2.at[s], {"tensor": ynb})
    def d_one(it, c):
        s = it // 2
        hb = 1 - it % 2
        rows = pl.ds(pl.multiple_of(hb * 2 * RP, 2 * RP), 2 * RP)
        r = nn(dqkv[s, rows, :], wbuf[...])
        DB[s, hb] = r[:RP].astype(bf16)
        DB[s, 2 + hb] = r[RP:].astype(bf16)
        ra(s, hb).start()
        tick(k + it)
        return c
    lax.fori_loop(0, 2 * S, d_one, 0)
    k = k + 2 * S
    for s in range(S):
        ra(s, 1).wait_recv()
        DB[s, 1] = add(DB.at[s, 1], rs1.at[s, 1])
        rb(s).start()
    for c in x1_loads:
        c.wait()
    def in_grad(c, x):
        at = pl.ds(pl.multiple_of(c * HC, HC), HC)
        g0 = nn(dqkv[...].reshape(S * SPAN, 896).T, PB[pl.ds(S * c, S)].reshape(S * SPAN, HC)).astype(bf16)
        gq = tn(pq[...], g0[0:512]).astype(bf16)
        gkv = tn(pkv[...], g0[512:896]).astype(bf16)
        put(0, at, gq)
        put(2 * NO, at, gkv)
        tick(k + c)
        return x
    lax.fori_loop(0, 4, in_grad, 0)
    k = k + 4
    if summed:
        start_rest = k
        def joint(g):
            for i, (ring, off, pace) in enumerate(rings):
                kk = g - (start_rest if i == 3 else off)
                if pace == 1:
                    ring.tick(kk)
                else:
                    @pl.when(kk % pace == 0)
                    def _():
                        ring.tick(kk // pace)
    else:
        o3 = pltpu.make_async_copy(W3, o_rest, sems_out.at[3])
        o3.start()
        def joint(g):
            pass
    joint(k)
    joint(k + 1)
    k = k + 2
    loads[5].wait()
    gain = gain1[...].astype(f32).reshape(1, D)
    gp1 = None
    for s in range(S):
        ra(s, 0).wait_recv()
        rb(s).wait_recv()
        e = DB[s, 0].astype(f32) + rs1[s, 0].astype(f32) + rs2[s].astype(f32)
        gp, dv = norm_back_rows(tok[s].astype(f32), e, gain)
        gp1 = gp if gp1 is None else gp1 + gp
        ig_out[s] += dv
    gains_out[...] = jnp.concatenate([gp1, gp2[...], jnp.zeros((6, D), f32)], axis=0)
    if summed:
        peers = [{"tensor": sib}, {"tensor": ynb}, {"dp": 1 - xi}]
        b = 1
        while b < nz:
            peers.append({"seq": zi ^ b})
            b *= 2
        for m, dev in enumerate(peers):
            GS[m] = gains_out[...]
            c = rc(GS.at[m], GL.at[m], sG.at[m], rG.at[m], dev)
            c.start()
            joint(k)
            k = k + 1
            c.wait()
            gains_out[...] += GL[m]
        last = max((start_rest if i == 3 else off) + (ring.ticks - 1) * pace + 1 for i, (ring, off, pace) in enumerate(rings))
        lax.fori_loop(k, last, lambda m, c: (joint(m), c)[1], 0)
    for s in range(S):
        ra(s, 0).wait_send()
        ra(s, 1).wait_send()
        rb(s).wait_send()
        for j in range(nz):
            @pl.when(j < zi)
            def _():
                chain(s, j).wait_send()
    if summed:
        for ring, off, pace in rings:
            ring.drain()
    else:
        o3.wait()


PLAN = {"gate": (12, 2, 9, 1, True), "down": (8, 1, 0, 2, True), "up": (24, 2, 21, 1), "rest": (18, 2, 0, 1)}


def attend_backward(DB, q, KV, att, lse, wo, wt, X1, pq, pkv, po, cos, sin, tok, dmid, gain1, gp2, g, gd, summed, plan=PLAN):
    nz = lax.axis_size("seq")
    S, RP, D = tok.shape
    SPAN = 4 * RP
    FL = g.shape[-1]
    QG, QD, QU, QC = D // 4, FL // 4, D // 2, CROWS // 4
    V = pl.BlockSpec(memory_space=pltpu.VMEM)
    A = pl.BlockSpec(memory_space=pl.ANY)
    sd = jax.ShapeDtypeStruct
    dma = pltpu.SemaphoreType.DMA
    vm = pltpu.VMEM
    scratch = [vm(DB.shape, bf16), vm(q.shape, bf16), vm(KV.shape, bf16), vm(att.shape, bf16), vm((896, D), bf16),
               vm(q.shape, bf16), vm((S, 2, 1, 2 * SPAN), f32), vm((S, 2, 128, 2 * SPAN), f32), vm((SPAN, 384), f32),
               vm((nz * S, SPAN, 384), bf16), vm((nz - 1, S, SPAN, 384), bf16), vm((S, SPAN, 896), bf16),
               vm((S, 2, RP, D), bf16), vm((S, RP, D), bf16), vm((2, 2, QC, D), bf16), vm((S * SPAN, 512), bf16),
               vm((6, 8, D), f32), vm((6, 8, D), f32),
               dma((nz, S)), dma((nz, S)), dma((S, 2)), dma((S, 2)), dma((S,)), dma((S,)), dma((6,)), dma((6,)), dma((17,)), dma((4,))]
    if summed:
        scratch += [vm((2, QG, FL), bf16), vm((2, QD, D), bf16), vm((2, QU, FL), bf16)]
        for name, cls, Q, C in (("gate", HalfFirst, QG, FL), ("down", HalfFirst, QD, D), ("up", LineFirst, QU, FL), ("rest", HalfFirst, QC, D)):
            n = plan[name][0]
            scratch += cls.scratch(n, Q // n, C)
    return pl.pallas_call(
        functools.partial(backward_kernel, summed, plan),
        out_shape=[sd((S, RP, D), f32), sd((8, D), f32), sd((2, 2, QG, FL), bf16), sd((2, QU, FL), bf16), sd((2, 2, QD, D), bf16),
                   sd((2, 2, QC, D), bf16)],
        in_specs=[A, A, A, A, V, A, A, A, V, V, V, V, V, V, A, V, V, A, A],
        out_specs=[V, V, A, A, A, A],
        scratch_shapes=scratch,
        compiler_params=pltpu.CompilerParams(collective_id=2, has_side_effects=True, vmem_limit_bytes=VMEM_BYTES),
        name="attend_backward")(DB, q, KV, att, lse, wo, wt, X1.reshape(S, SPAN, D), pq, pkv, po, cos, sin, tok, dmid, gain1, gp2,
                                g.reshape(2, 2, 2, QG, FL), gd.reshape(2, 2, QD, D))


def local(
    tokens, attn_gain, w_query, w_key, w_value, w_output, ffn_gain, w_gate, w_up, w_down, cotangent
):
    t = lax.axis_index("tensor")
    zi = lax.axis_index("seq")
    pq, pkv, po = (jnp.asarray(v, bf16) for v in pick_tables())
    tok = jnp.swapaxes(tokens, 0, 1)
    cot = jnp.swapaxes(cotangent, 0, 1)
    S, RP, D = tok.shape
    cos, sin = rope_tables(zi * 4 * RP, 4 * RP, t)
    X1, C, q, KV, att, lse, wqkv, wo, mid, n2 = attend_forward(
        tok, cot, w_query, w_key.T, w_value.T, w_output, pq, pkv, po, cos, sin, attn_gain, ffn_gain)
    summed = lax.axis_size("dp") == 2
    DB, g, gd, down, dmid, gp2 = feed_forward(n2, mid, C, w_gate, w_up, w_down, ffn_gain)
    down_local = lax.psum_scatter(down, "tensor", scatter_dimension=0, tiled=True)[0]
    ig, gains, gate, up, wd, rest = attend_backward(
        DB, q, KV, att, lse, wo, wqkv, X1, pq, pkv, po, cos, sin, tok, dmid, attn_gain, gp2, g, gd, summed)
    if not summed:
        g, wd, rest = lax.psum((g.astype(f32), gd.astype(f32), rest.astype(f32)), ("dp", "seq"))
        gate, up = g[0], g[1]
        gains = lax.psum(gains, ("dp", "seq", "tensor"))
    rest = rest.reshape(-1, D).astype(f32)
    nq, nk = w_query.shape[1], w_key.shape[1]
    activation = (mid + down_local.astype(f32)).astype(bf16)
    return (
        jnp.swapaxes(activation, 0, 1),
        jnp.swapaxes(ig, 0, 1),
        gains[0],
        rest[:nq].T,
        rest[nq:nq + nk].T,
        rest[nq + nk:nq + 2 * nk].T,
        rest[nq + 2 * nk:],
        gains[1],
        gate.reshape(D, -1).astype(f32),
        up.reshape(D, -1).astype(f32),
        wd.reshape(-1, D).astype(f32),
    )


def solution(mesh):
    rows = P(("seq", "tensor"), "dp", None)
    columns = P(None, "tensor")
    placed = (rows, P(), columns, columns, columns, P("tensor", None), P(), columns, columns, P("tensor", None), rows)
    return jax.shard_map(
        local,
        mesh=mesh,
        in_specs=placed,
        out_specs=(rows, rows, P(), columns, columns, columns, P("tensor", None), P(), columns, columns, P("tensor", None)),
        check_vma=False,
    )
```

```python
import functools
import numpy as np
import jax, jax.numpy as jnp
from jax import lax
from jax.sharding import PartitionSpec as P
import jax.experimental.pallas as pl
import jax.experimental.pallas.tpu as pltpu

MESH = pl.DeviceIdType.MESH
bf16 = jnp.bfloat16
f32 = jnp.float32
HEAD_DIM = 96
HALF = 48
epsilon = 1e-05
theta = 100000.0
LOG2E = 1.4426950408889634
SCALE = HEAD_DIM ** -0.5
VMEM_BYTES = 63 << 20

K_LANES = [list(range(0, 48)) + list(range(64, 112)), list(range(16, 64)) + list(range(80, 128))]
F_LANES = [list(range(48, 64)) + list(range(112, 128)), list(range(0, 16)) + list(range(64, 80))]
V_LANES = [list(range(0, 48)) + list(range(64, 80)), list(range(48, 64)) + list(range(80, 128))]


def pick_tables():
    q = np.zeros((512, 384), np.float32)
    kv = np.zeros((384, 384), np.float32)
    o = np.zeros((384, 512), np.float32)
    for h in range(4):
        for d in range(96):
            q[h * 128 + K_LANES[h // 2][d], h * 96 + d] = 1
            lane = F_LANES[h // 2][d] if d < 32 else V_LANES[h // 2][d - 32]
            o[h * 96 + d, h * 128 + lane] = 1
    for g in range(2):
        for d in range(96):
            kv[g * 128 + K_LANES[g][d], g * 96 + d] = 1
            lane = g * 128 + F_LANES[g][d] if d < 32 else 256 + V_LANES[g][d - 32]
            kv[lane, 192 + g * 96 + d] = 1
    return q, kv, o


def in_ranges(lane, lanes):
    mask = None
    lo = prev = lanes[0]
    runs = []
    for x in lanes[1:] + [None]:
        if x is None or x != prev + 1:
            runs.append((lo, prev))
            lo = x
        prev = x
    for a, b in runs:
        m = jnp.logical_and(lane >= a, lane <= b)
        mask = m if mask is None else jnp.logical_or(mask, m)
    return mask


def rope_tables(row_start, span, t):
    rate = np.zeros((2, 128), np.float32)
    sign = np.zeros((2, 128), np.float32)
    for g in range(2):
        for d in range(96):
            rate[g, K_LANES[g][d]] = d % HALF
            sign[g, K_LANES[g][d]] = -1.0 if d < HALF else 1.0
    used = np.abs(sign)
    rates = used * theta ** (-(jnp.asarray(rate) * 2.0 / HEAD_DIM))
    i = jnp.arange(span, dtype=jnp.int32)
    c = span // 4
    places = (row_start + ((i // c) ^ t) * c + i % c).astype(f32)
    angle = places[None, :, None] * rates[:, None, :]
    return jnp.cos(angle), jnp.sin(angle) * sign[:, None, :]


def nt(a, b):
    return lax.dot_general(a, b, (((1,), (1,)), ((), ())), preferred_element_type=f32)


def nn(a, b):
    return jnp.dot(a, b, preferred_element_type=f32)


def tn(a, b):
    return lax.dot_general(a, b, (((0,), (0,)), ((), ())), preferred_element_type=f32)


def rc(src, dst, ss, rr, dev):
    return pltpu.make_async_remote_copy(src, dst, ss, rr, device_id=dev, device_id_type=MESH)


def entry(devs, z_line):
    b = pltpu.get_barrier_semaphore()
    count = len(devs)
    for dev in devs:
        pl.semaphore_signal(b, inc=1, device_id=dev, device_id_type=MESH)
    if z_line:
        zi = lax.axis_index("seq")
        nz = lax.axis_size("seq")
        @pl.when(zi > 0)
        def _():
            pl.semaphore_signal(b, inc=1, device_id={"seq": zi - 1}, device_id_type=MESH)
        @pl.when(zi < nz - 1)
        def _():
            pl.semaphore_signal(b, inc=1, device_id={"seq": zi + 1}, device_id_type=MESH)
        count = count + (zi > 0).astype(jnp.int32) + (zi < nz - 1).astype(jnp.int32)
    pl.semaphore_wait(b, count)


def causal(sT, qt, TQ, RP, t):
    span = sT.shape[0]
    ki = lax.broadcasted_iota(jnp.int32, (span, 1), 0)
    qi = lax.broadcasted_iota(jnp.int32, (1, TQ), 1) + (qt % (span // TQ)) * TQ
    kpos = ((ki // RP) ^ t) * RP + ki % RP
    qpos = ((qi // RP) ^ t) * RP + qi % RP
    return jnp.where(kpos <= qpos, sT, -1e30)


def rms(v, gain):
    return v * lax.rsqrt(jnp.mean(v * v, axis=-1, keepdims=True) + epsilon) * gain


def norm_back_rows(v, e, gain):
    inv = lax.rsqrt(jnp.mean(v * v, axis=-1, keepdims=True) + epsilon)
    part = jnp.sum(e * v * inv, axis=0, keepdims=True)
    sc = e * gain
    return part, inv * sc - v * (inv * inv * inv) * jnp.mean(sc * v, axis=-1, keepdims=True)


def forward_kernel(nz, tok, cot, wq, wk, wv, w_out, pq, pkv, po, cos, sin, gain1, gain2,
                   x1_out, c_out, q_out, kv_out, att_out, lse_out, wqkv_out, wo_out, mid_out, n2_out,
                   xn, X, C, KV, q, att, lse, wqkv, wo, m_s, l_s, o_s, part, rs1, ysend, rs2,
                   sA, rA, sB, rB, sC, rC, sKV, rKV, sR1, rR1, sR2, rR2, osem):
    t = lax.axis_index("tensor")
    zi = lax.axis_index("seq")
    sib, ynb = t ^ 1, t ^ 2
    S, RP, D = tok.shape
    SPAN = 4 * RP
    TQ = 256
    NT = 2 * SPAN // TQ
    g1 = gain1[...].astype(f32).reshape(1, D)
    for s in range(S):
        xn[s] = rms(tok[s].astype(f32), g1).astype(bf16)
    entry([{"tensor": sib}, {"tensor": ynb}], True)

    def ga(w, s):
        return rc((xn, cot)[w].at[s], (X, C)[w].at[s, 1], sA.at[w, s], rA.at[w, s], {"tensor": sib})
    def gb(w, s):
        return rc((xn, cot)[w].at[s], (X, C)[w].at[s, 2], sB.at[w, s], rB.at[w, s], {"tensor": ynb})
    def gc(w, s):
        buf = (X, C)[w]
        return rc(buf.at[s, 2], buf.at[s, 3], sC.at[w, s], rC.at[w, s], {"tensor": sib})
    for s in range(S):
        gb(0, s).start()
        ga(0, s).start()
    wqkv[0:512, :] = nt(pq[...], wq[...]).astype(bf16)
    wqkv[512:896, :] = (nn(pkv[:, 0:192], wk[...]) + nn(pkv[:, 192:384], wv[...])).astype(bf16)
    for s in range(S):
        X[s, 0] = xn[s]

    def kvc(s, j, hb):
        at = pl.ds(hb * 2 * RP, 2 * RP)
        return rc(KV.at[s, j, at], KV.at[s, j, at], sKV.at[s, j, hb], rKV.at[s, j, hb], {"seq": zi + 1})
    def send_own(s, hb):
        @pl.when(zi < nz - 1)
        def _():
            kvc(s, zi, hb).start()
    def arrive(s, h, hb):
        j = zi - 1 - h
        @pl.when(j >= 0)
        def _():
            kvc(s, j, hb).wait_recv()
            @pl.when(zi < nz - 1)
            def _():
                kvc(s, j, hb).start()

    def project(s, hb):
        r = nt(X[s, 2 * hb:2 * hb + 2].reshape(2 * RP, D), wqkv[...])
        base = hb * 2 * RP
        for slot in range(6):
            g = slot // 2 if slot < 4 else slot - 4
            u = r[:, slot * 128:(slot + 1) * 128]
            u = u * cos[g, base:base + 2 * RP, :] + pltpu.roll(u, 64, 1) * sin[g, base:base + 2 * RP, :]
            if slot < 4:
                q[s, g, (slot % 2) * SPAN + base:(slot % 2) * SPAN + base + 2 * RP, :] = u.astype(bf16)
            else:
                KV[s, zi, base:base + 2 * RP, g * 128:(g + 1) * 128] = u.astype(bf16)
        KV[s, zi, base:base + 2 * RP, 256:384] = r[:, 768:896].astype(bf16)

    def unit(s, j, diag):
        def tile(g, qt):
            qa = pl.ds(pl.multiple_of(qt * TQ, TQ), TQ)
            kp = KV[s, j, :, g * 128:(g + 1) * 128]
            sT = nt(kp, q[s, g, qa, :]) * (SCALE * LOG2E)
            if diag:
                sT = causal(sT, qt, TQ, RP, t)
            mx = jnp.max(sT, axis=0, keepdims=True)
            if diag:
                m = mx
            else:
                m0 = m_s[s, g, :, qa]
                m = jnp.maximum(m0, mx)
                al = jnp.exp2(m0 - m)
            p = jnp.exp2(sT - m)
            total = jnp.sum(p, axis=0, keepdims=True)
            kv = jnp.concatenate([kp, KV[s, j, :, 256:384]], axis=1)
            o = tn(kv, p.astype(bf16))
            m_s[s, g, :, qa] = m
            if diag:
                l_s[s, g, :, qa] = total
                o_s[s, g, :, qa] = o
            else:
                l_s[s, g, :, qa] = l_s[s, g, :, qa] * al + total
                o_s[s, g, :, qa] = o_s[s, g, :, qa] * al + o
        def body(qt, c):
            tile(0, qt)
            tile(1, qt)
            return c
        lax.fori_loop(0, NT, body, 0, unroll=2)
    def hop(s, h):
        @pl.when(zi - 1 - h >= 0)
        def _():
            unit(s, zi - 1 - h, False)

    def rs_a(s):
        return rc(part.at[s, 1], rs1.at[s], sR1.at[s], rR1.at[s], {"tensor": sib})
    def rs_b(s):
        return rc(ysend.at[s], rs2.at[s], sR2.at[s], rR2.at[s], {"tensor": ynb})
    def finish(s):
        lane = lax.broadcasted_iota(jnp.int32, (128, 1), 0)
        for g in range(2):
            lse[s, g] = m_s[s, g] + jnp.log2(l_s[s, g])
            fm = in_ranges(lane, F_LANES[g])
            vm = in_ranges(lane, V_LANES[g])
            o = jnp.where(fm, o_s[s, g, 0:128, :], jnp.where(vm, o_s[s, g, 128:256, :], 0.0)) * (1.0 / l_s[s, g])
            att[s, g] = o.T.astype(bf16)
        for par in (1, 0):
            a = jnp.concatenate([jnp.concatenate([att[s, g, hh * SPAN + r * RP:hh * SPAN + (r + 1) * RP, :]
                                                  for g in range(2) for hh in range(2)], axis=1) for r in (par, par + 2)], axis=0)
            part[s, par] = nn(a, wo[...]).astype(bf16).reshape(2, RP, D)
            if par == 1:
                rs_a(s).start()
    def rs_mid(s):
        rs_a(s).wait_recv()
        ysend[s] = (part[s, 0, 1].astype(f32) + rs1[s, 1].astype(f32)).astype(bf16)
        rs_b(s).start()
    def rs_end(s):
        rs_b(s).wait_recv()
        mid = tok[s].astype(f32) + part[s, 0, 0].astype(f32) + rs1[s, 0].astype(f32) + rs2[s].astype(f32)
        mid_out[s] = mid
        n2_out[s] = rms(mid, gain2[...].astype(f32).reshape(1, D)).astype(bf16)

    ga(0, 0).wait_recv()
    project(0, 0)
    send_own(0, 0)
    ga(0, 1).wait_recv()
    project(1, 0)
    wo[...] = tn(po[...], w_out[...]).astype(bf16)
    gb(0, 0).wait_recv()
    gc(0, 0).start()
    arrive(0, 0, 0)
    gc(0, 0).wait_recv()
    project(0, 1)
    send_own(0, 1)
    arrive(0, 1, 0)
    gb(0, 1).wait_recv()
    gc(0, 1).start()
    for s in range(S):
        gb(1, s).start()
        ga(1, s).start()
    unit(0, zi, True)
    arrive(0, 0, 1)
    gc(0, 1).wait_recv()
    project(1, 1)
    arrive(0, 1, 1)
    send_own(1, 0)
    send_own(1, 1)
    hop(0, 0)
    for h in range(2, nz - 1):
        arrive(0, h, 0)
        arrive(0, h, 1)
    for s in range(S):
        C[s, 0] = cot[s]
    def more(h, c):
        hop(0, h)
        return c
    hop(0, 1)
    arrive(1, 0, 0)
    arrive(1, 0, 1)
    lax.fori_loop(2, nz - 1, more, 0)
    finish(0)
    unit(1, zi, True)
    gb(1, 0).wait_recv()
    gc(1, 0).start()
    rs_mid(0)
    arrive(1, 1, 0)
    arrive(1, 1, 1)
    hop(1, 0)
    gb(1, 1).wait_recv()
    gc(1, 1).start()
    hop(1, 1)
    rs_end(0)
    def rest(h, c):
        arrive(1, h, 0)
        arrive(1, h, 1)
        hop(1, h)
        return c
    lax.fori_loop(2, nz - 1, rest, 0)
    finish(1)
    for s in range(S):
        gc(1, s).wait_recv()
        ga(1, s).wait_recv()
    outs = [pltpu.make_async_copy(a, o, osem.at[n]) for n, (a, o) in enumerate(
        ((X, x1_out), (C, c_out), (q, q_out), (KV, kv_out), (att, att_out), (lse, lse_out), (wqkv, wqkv_out), (wo, wo_out)))]
    for o in outs:
        o.start()
    rs_mid(1)
    rs_end(1)
    for s in range(S):
        for w in range(2):
            ga(w, s).wait_send()
            gb(w, s).wait_send()
            gc(w, s).wait_send()
        rs_a(s).wait_send()
        rs_b(s).wait_send()
        for j in range(nz):
            @pl.when(jnp.logical_and(j <= zi, zi < nz - 1))
            def _():
                for hb in range(2):
                    kvc(s, j, hb).wait_send()
    for o in outs:
        o.wait()


def attend_forward(tok, cot, wq, wk, wv, w_out, pq, pkv, po, cos, sin, gain1, gain2):
    nz = lax.axis_size("seq")
    S, RP, D = tok.shape
    SPAN = 4 * RP
    V = pl.BlockSpec(memory_space=pltpu.VMEM)
    A = pl.BlockSpec(memory_space=pl.ANY)
    sd = jax.ShapeDtypeStruct
    dma = pltpu.SemaphoreType.DMA
    vm = pltpu.VMEM
    return pl.pallas_call(
        functools.partial(forward_kernel, nz),
        out_shape=[sd((S, 4, RP, D), bf16), sd((S, 4, RP, D), bf16), sd((S, 2, 2 * SPAN, 128), bf16),
                   sd((S, nz, SPAN, 384), bf16), sd((S, 2, 2 * SPAN, 128), bf16), sd((S, 2, 1, 2 * SPAN), f32),
                   sd((896, D), bf16), sd((512, D), bf16), sd((S, RP, D), f32), sd((S, RP, D), bf16)],
        in_specs=[V] * 13,
        out_specs=[A] * 8 + [V] * 2,
        scratch_shapes=[vm((S, RP, D), bf16), vm((S, 4, RP, D), bf16), vm((S, 4, RP, D), bf16),
                        vm((S, nz, SPAN, 384), bf16), vm((S, 2, 2 * SPAN, 128), bf16),
                        vm((S, 2, 2 * SPAN, 128), bf16), vm((S, 2, 1, 2 * SPAN), f32), vm((896, D), bf16), vm((512, D), bf16),
                        vm((S, 2, 1, 2 * SPAN), f32), vm((S, 2, 1, 2 * SPAN), f32), vm((S, 2, 256, 2 * SPAN), f32),
                        vm((S, 2, 2, RP, D), bf16), vm((S, 2, RP, D), bf16), vm((S, RP, D), bf16), vm((S, RP, D), bf16)]
        + [dma((2, S))] * 6 + [dma((S, nz, 2))] * 2 + [dma((S,))] * 4 + [dma((8,))],
        compiler_params=pltpu.CompilerParams(collective_id=0, has_side_effects=True, vmem_limit_bytes=VMEM_BYTES),
        name="attend_forward")(tok, cot, wq, wk, wv, w_out, pq, pkv, po, cos, sin, gain1, gain2)


def feed_kernel(n2, mid, c_in, wg_in, wu_in, wd_in, gain2,
                dn_out, ga_out, gb_out, down_out, dmid_out, gpart_out,
                X, C, wg, wu, wd, dh, F, G, GD, part, rs1, ysend, rs2, pd,
                sA, rA, sB, rB, sC, rC, sR1, rR1, sR2, rR2, isem, osem):
    t = lax.axis_index("tensor")
    sib, ynb = t ^ 1, t ^ 2
    S, RP, D = n2.shape
    FL = wg.shape[1]
    loads = [pltpu.make_async_copy(a, b, isem.at[i]) for i, (a, b) in enumerate(
        ((wd_in, wd), (c_in, C), (wg_in, wg), (wu_in, wu)))]
    for c in loads:
        c.start()
    entry([{"tensor": sib}, {"tensor": ynb}], False)

    def ga(s):
        return rc(n2.at[s], X.at[s, 1], sA.at[s], rA.at[s], {"tensor": sib})
    def gb(s):
        return rc(n2.at[s], X.at[s, 2], sB.at[s], rB.at[s], {"tensor": ynb})
    def gc(s):
        return rc(X.at[s, 2], X.at[s, 3], sC.at[s], rC.at[s], {"tensor": sib})
    def ra(s, hb):
        return rc(part.at[s, 1, hb], rs1.at[s, hb], sR1.at[s, hb], rR1.at[s, hb], {"tensor": sib})
    def rb(s):
        return rc(ysend.at[s], rs2.at[s], sR2.at[s], rR2.at[s], {"tensor": ynb})
    for s in range(S):
        gb(s).start()
        ga(s).start()
    for s in range(S):
        X[s, 0] = n2[s]
    loads[0].wait()
    loads[1].wait()
    def early(s, c):
        dh[s] = nt(C[s].reshape(4 * RP, D), wd[...])
        return c
    lax.fori_loop(0, S, early, 0)
    loads[2].wait()
    loads[3].wait()

    def mlp(s, hb):
        x = X[s, pl.ds(2 * hb, 2)].reshape(2 * RP, D)
        rows = pl.ds(pl.multiple_of(hb * 2 * RP, 2 * RP), 2 * RP)
        g = nn(x, wg[...])
        u = nn(x, wu[...])
        sg = 1.0 / (1.0 + jnp.exp(-g))
        si = g * sg
        d = dh[s, rows]
        F[2, s, rows] = (si * u).astype(bf16)
        F[0, s, rows] = (d * u * sg * (1.0 + g * (1.0 - sg))).astype(bf16)
        F[1, s, rows] = (d * si).astype(bf16)
        r = nt(F[0, s, rows], wg[...]) + nt(F[1, s, rows], wu[...])
        part[s, 0, hb] = r[:RP].astype(bf16)
        part[s, 1, hb] = r[RP:].astype(bf16)
        ra(s, hb).start()
    def rs_mid(s):
        ra(s, 1).wait_recv()
        ysend[s] = (part[s, 0, 1].astype(f32) + rs1[s, 1].astype(f32)).astype(bf16)
        rb(s).start()
    gain = gain2[...].astype(f32).reshape(1, D)
    def rs_end(s):
        ra(s, 0).wait_recv()
        rb(s).wait_recv()
        e = part[s, 0, 0].astype(f32) + rs1[s, 0].astype(f32) + rs2[s].astype(f32)
        gp, dv = norm_back_rows(mid[s], e, gain)
        if s == 0:
            gpart_out[...] = gp
        else:
            gpart_out[...] += gp
        dm = C[s, 0].astype(f32) + dv
        dmid_out[s] = dm
        dn_out[s] = dm.astype(bf16)

    CH = 512
    def wgrad(a, src, f, c):
        at = pl.ds(pl.multiple_of(c * CH, CH), CH)
        left = src[:, :, :, at].reshape(S * 4 * RP, CH).T
        G[a, at, :] = nn(left, F[f].reshape(S * 4 * RP, FL)).astype(bf16)
    half = FL // 2
    def dgrad(h):
        left = F[2, :, :, pl.ds(pl.multiple_of(h * half, half), half)].reshape(S * 4 * RP, half).T
        for c in range(D // CH):
            at = pl.ds(c * CH, CH)
            GD[h, :, at] = nn(left, C[:, :, :, at].reshape(S * 4 * RP, CH)).astype(bf16)
    def down(s):
        r = nn(F[2, s], wd[...]).astype(bf16)
        for p in range(4):
            pd[t ^ p, s] = r[p * RP:(p + 1) * RP]

    ga(0).wait_recv()
    mlp(0, 0)
    gb(0).wait_recv()
    gc(0).start()
    gc(0).wait_recv()
    mlp(0, 1)
    ga(1).wait_recv()
    gb(1).wait_recv()
    gc(1).start()
    rs_mid(0)
    mlp(1, 0)
    gc(1).wait_recv()
    mlp(1, 1)
    rs_end(0)
    rs_mid(1)
    lax.fori_loop(0, 2, lambda h, x: (dgrad(h), x)[1], 0)
    o_down = pltpu.make_async_copy(GD, gb_out, osem.at[0])
    o_down.start()
    down(0)
    down(1)
    o_pd = pltpu.make_async_copy(pd, down_out, osem.at[1])
    o_pd.start()
    rs_end(1)
    lax.fori_loop(0, D // CH, lambda c, x: (wgrad(0, X, 0, c), x)[1], 0)
    lax.fori_loop(0, D // CH, lambda c, x: (wgrad(1, X, 1, c), x)[1], 0)
    o_up = pltpu.make_async_copy(G, ga_out, osem.at[2])
    o_up.start()
    for s in range(S):
        ga(s).wait_send()
        gb(s).wait_send()
        gc(s).wait_send()
        ra(s, 0).wait_send()
        ra(s, 1).wait_send()
        rb(s).wait_send()
    for o in (o_down, o_pd, o_up):
        o.wait()


def feed_forward(n2, mid, C, wg, wu, wd, gain2):
    S, RP, D = n2.shape
    FL = wg.shape[1]
    V = pl.BlockSpec(memory_space=pltpu.VMEM)
    A = pl.BlockSpec(memory_space=pl.ANY)
    sd = jax.ShapeDtypeStruct
    dma = pltpu.SemaphoreType.DMA
    vm = pltpu.VMEM
    return pl.pallas_call(
        feed_kernel,
        out_shape=[sd((S, RP, D), bf16), sd((2, D, FL), bf16), sd((2, FL // 2, D), bf16), sd((4, S, RP, D), bf16),
                   sd((S, RP, D), f32), sd((1, D), f32)],
        in_specs=[V, V, A, A, A, A, V],
        out_specs=[V, A, A, A, V, V],
        scratch_shapes=[vm((S, 4, RP, D), bf16), vm((S, 4, RP, D), bf16),
                        vm((D, FL), bf16), vm((D, FL), bf16), vm((FL, D), bf16), vm((S, 4 * RP, FL), f32),
                        vm((3, S, 4 * RP, FL), bf16), vm((2, D, FL), bf16), vm((2, FL // 2, D), bf16), vm((S, 2, 2, RP, D), bf16), vm((S, 2, RP, D), bf16),
                        vm((S, RP, D), bf16), vm((S, RP, D), bf16), vm((4, S, RP, D), bf16)]
        + [dma((S,))] * 6 + [dma((S, 2))] * 2 + [dma((S,))] * 2 + [dma((4,)), dma((3,))],
        compiler_params=pltpu.CompilerParams(collective_id=1, has_side_effects=True, vmem_limit_bytes=VMEM_BYTES),
        name="feed_forward")(n2, mid, C, wg, wu, wd, gain2)


def line(u, nz, edge=False):
    zi = lax.axis_index("seq")
    root = (nz - 1) * u if edge else nz // 2 - 1 + u
    below, above = zi < root, zi > root
    dist = jnp.where(below, root - zi, zi - root)
    return dist, below, above, zi == root, jnp.where(below, zi + 1, zi - 1)


def both(a, b):
    return jnp.logical_and(a, b)


def add(*refs):
    total = refs[0][...].astype(f32)
    for r in refs[1:]:
        total = total + r[...].astype(f32)
    return total.astype(bf16)


class Flow:
    def setup(self, n, p, lag, edge=False):
        self.n, self.p, self.lag, self.edge = n, p, lag, edge
        self.nz = lax.axis_size("seq")
        self.far = self.nz - 1 if edge else self.nz // 2
    def line(self, u):
        return line(u, self.nz, self.edge)
    def at(self, i):
        return pl.ds(pl.multiple_of(i * self.p, self.p), self.p)
    def valid(self, i):
        return both(i >= 0, i < self.n)
    def send_in(self, u, i, own, main, short, sems, act):
        dist, below, above, root, inward = self.line(u)
        ss, rr, r2 = sems
        if self.edge:
            act(rc(own, main.at[u, self.at(i)], ss.at[u, i], rr.at[u, i], {"seq": inward}))
            return
        to_short = both(dist == 1, below if u == 0 else above)
        @pl.when(to_short)
        def _():
            act(rc(own, short.at[self.at(i)], ss.at[u, i], r2.at[i], {"seq": inward}))
        @pl.when(jnp.logical_not(to_short))
        def _():
            act(rc(own, main.at[u, self.at(i)], ss.at[u, i], rr.at[u, i], {"seq": inward}))
    def from_main(self, u, i, own, main, sems):
        ss, rr, r2 = sems
        rc(own, main.at[u, self.at(i)], ss.at[u, i], rr.at[u, i], {"seq": self.line(u)[4]}).wait_recv()
    def from_short(self, u, i, own, short, sems):
        ss, rr, r2 = sems
        rc(own, short.at[self.at(i)], ss.at[u, i], r2.at[i], {"seq": self.line(u)[4]}).wait_recv()
    def outward(self, u, i, buf, bs, br, act):
        zi = lax.axis_index("seq")
        dist, below, above, root, inward = self.line(u)
        @pl.when(both(jnp.logical_not(above), zi > 0))
        def _():
            act(rc(buf.at[u, self.at(i)], buf.at[u, self.at(i)], bs.at[0, u, i], br.at[u, i], {"seq": zi - 1}))
        @pl.when(both(jnp.logical_not(below), zi < self.nz - 1))
        def _():
            act(rc(buf.at[u, self.at(i)], buf.at[u, self.at(i)], bs.at[1, u, i], br.at[u, i], {"seq": zi + 1}))
    def has_farther(self, u):
        zi = lax.axis_index("seq")
        dist, below, above, root, inward = self.line(u)
        return jnp.logical_or(both(below, zi > 0), both(above, zi < self.nz - 1))


class HalfFirst(Flow):
    count = 11
    @staticmethod
    def scratch(n, p, C):
        vm = pltpu.VMEM
        dma = pltpu.SemaphoreType.DMA
        Q = n * p
        return [vm((2, Q, C), bf16), vm((2, Q, C), bf16), vm((Q, C), bf16),
                dma((n,)), dma((n,)), dma((2, n)), dma((2, n)), dma((n,)), dma((2, 2, n)), dma((2, n)), dma((2, 2, n))]
    def __init__(self, src, own, out, bufs, osem, n, p, lag, ahead=False):
        self.setup(n, p, lag)
        self.src, self.own, self.out, self.osem = src, own, out, osem
        self.ahead = ahead
        self.RX, self.RZ, self.R2, self.x1s, self.x1r, self.rs, self.rr, self.r2, self.bs, self.br, self.x2 = bufs
        self.ticks = n + lag * (2 * self.far + 2)
    def tick(self, k):
        lag, far, RX, RZ, R2 = self.lag, self.far, self.RX, self.RZ, self.R2
        xi = lax.axis_index("dp")
        ox = 1 - xi
        sems = (self.rs, self.rr, self.r2)
        start = lambda c: c.start()
        def x1(i):
            return rc(self.src.at[ox, :, self.at(i)], RX.at[:, self.at(i)], self.x1s.at[i], self.x1r.at[i], {"dp": ox})
        def x2(u, i):
            return rc(RX.at[u, self.at(i)], self.out.at[xi, u, self.at(i)], self.x2.at[0, u, i], self.x2.at[1, u, i], {"dp": ox})
        @pl.when(k == 0 if self.ahead else self.valid(k))
        def _():
            if self.ahead:
                lax.fori_loop(0, self.n, lambda i, c: (x1(i).start(), c)[1], 0)
            else:
                x1(k).start()
        i1 = k - lag
        @pl.when(self.valid(i1))
        def _():
            x1(i1).wait()
            for u in range(2):
                own = self.own(u).at[self.at(i1)]
                own[...] = add(own, RX.at[u, self.at(i1)])
        for u in range(2):
            dist, below, above, root, inward = self.line(u)
            i = k - lag * (1 + far - dist)
            @pl.when(self.valid(i))
            def _():
                own = self.own(u).at[self.at(i)]
                @pl.when(jnp.logical_not(root))
                def _():
                    @pl.when(self.has_farther(u))
                    def _():
                        self.from_main(u, i, own, RZ, sems)
                        own[...] = add(own, RZ.at[u, self.at(i)])
                    self.send_in(u, i, own, RZ, R2, sems, start)
                @pl.when(root)
                def _():
                    self.from_main(u, i, own, RZ, sems)
                    self.from_short(u, i, own, R2, sems)
                    RX[u, self.at(i)] = add(own, RZ.at[u, self.at(i)], R2.at[self.at(i)])
                    self.outward(u, i, RX, self.bs, self.br, start)
                    x2(u, i).start()
            i = k - lag * (1 + far + dist)
            @pl.when(both(self.valid(i), jnp.logical_not(root)))
            def _():
                rc(RX.at[u, self.at(i)], RX.at[u, self.at(i)], self.bs.at[0, u, i], self.br.at[u, i], {"seq": inward}).wait_recv()
                self.outward(u, i, RX, self.bs, self.br, start)
                x2(u, i).start()
            i = i - lag
            @pl.when(self.valid(i))
            def _():
                x2(u, i).wait()
                @pl.when(jnp.logical_not(root))
                def _():
                    self.send_in(u, i, self.own(u).at[self.at(i)], RZ, R2, sems, lambda c: c.wait_send())
                self.outward(u, i, RX, self.bs, self.br, lambda c: c.wait_send())
                pltpu.make_async_copy(RX.at[u, self.at(i)], self.out.at[xi, u, self.at(i)], self.osem).start()
    def drain(self):
        xi = lax.axis_index("dp")
        pltpu.make_async_copy(self.RX, self.out.at[xi], self.osem).wait()


class LineFirst(Flow):
    count = 10
    @staticmethod
    def scratch(n, p, C):
        vm = pltpu.VMEM
        dma = pltpu.SemaphoreType.DMA
        Q = n * p
        return [vm((2, Q, C), bf16), vm((Q, C), bf16), vm((Q, C), bf16),
                dma((2, n)), dma((2, n)), dma((n,)), dma((2, 2, n)), dma((2, n)), dma((n,)), dma((n,))]
    def __init__(self, W, out, bufs, osem, n, p, lag, edge=False):
        self.setup(n, p, lag, edge)
        self.W, self.out, self.osem = W, out, osem
        self.Z, self.XB, self.R2, self.rs, self.rr, self.r2, self.bs, self.br, self.xs, self.xr = bufs
        self.ticks = n + lag * (2 * self.far + 2)
    def tick(self, k):
        lag, far, W, Z = self.lag, self.far, self.W, self.Z
        ox = 1 - lax.axis_index("dp")
        sems = (self.rs, self.rr, self.r2)
        start = lambda c: c.start()
        def xb(u, i):
            return rc(W.at[u, self.at(i)], self.XB.at[self.at(i)], self.xs.at[i], self.xr.at[i], {"dp": ox})
        for u in range(2):
            dist, below, above, root, inward = self.line(u)
            i = k - lag * (far - dist)
            @pl.when(self.valid(i))
            def _():
                own = W.at[u, self.at(i)]
                @pl.when(jnp.logical_not(root))
                def _():
                    @pl.when(self.has_farther(u))
                    def _():
                        self.from_main(u, i, own, Z, sems)
                        own[...] = add(own, Z.at[u, self.at(i)])
                    self.send_in(u, i, own, Z, self.R2, sems, start)
                @pl.when(root)
                def _():
                    self.from_main(u, i, own, Z, sems)
                    if self.edge:
                        own[...] = add(own, Z.at[u, self.at(i)])
                    else:
                        self.from_short(u, i, own, self.R2, sems)
                        own[...] = add(own, Z.at[u, self.at(i)], self.R2.at[self.at(i)])
                    xb(u, i).start()
            i = k - lag * (far + 1)
            @pl.when(both(self.valid(i), root))
            def _():
                xb(u, i).wait()
                Z[u, self.at(i)] = add(W.at[u, self.at(i)], self.XB.at[self.at(i)])
                self.outward(u, i, Z, self.bs, self.br, start)
            i = k - lag * (far + 1 + dist)
            @pl.when(both(self.valid(i), jnp.logical_not(root)))
            def _():
                rc(Z.at[u, self.at(i)], Z.at[u, self.at(i)], self.bs.at[0, u, i], self.br.at[u, i], {"seq": inward}).wait_recv()
                self.outward(u, i, Z, self.bs, self.br, start)
            i = i - lag
            @pl.when(self.valid(i))
            def _():
                @pl.when(jnp.logical_not(root))
                def _():
                    self.send_in(u, i, W.at[u, self.at(i)], Z, self.R2, sems, lambda c: c.wait_send())
                self.outward(u, i, Z, self.bs, self.br, lambda c: c.wait_send())
                pltpu.make_async_copy(Z.at[u, self.at(i)], self.out.at[u, self.at(i)], self.osem).start()
    def drain(self):
        pltpu.make_async_copy(self.Z, self.out, self.osem).wait()


NO = 192
CROWS = 6 * NO
PHASES = {"dast": 1, "steps": 1, "out": 1, "done": 1, "in": 1}
EARLY = False
PRE = 3
HOP = 1


def backward_kernel(summed, plan, dn_in, q_in, kv_in, att_in, lse, wo_in, wt_in, x1_in, pq, pkv, po, cos, sin, tok, dmid_in, gain1, gp2,
                    g_in, gd_in, ig_out, gains_out, o_gate, o_up, o_down, o_rest, *scr):
    t = lax.axis_index("tensor")
    zi = lax.axis_index("seq")
    nz = lax.axis_size("seq")
    sib, ynb = t ^ 1, t ^ 2
    S, RP, D = tok.shape
    SPAN = 4 * RP
    TQ = 512
    NT = 2 * SPAN // TQ
    HC = D // 4
    QC = CROWS // 4
    scr = list(scr)
    (DB, q, KV, att, wbuf, da, delta, dqT, acc, PB, RB, dqkv, rs1, rs2, W3, heads, GS, GL,
     sKV, rKV, sR1, rR1, sR2, rR2, sG, rG, sDB, rDB, isem, sems_out) = scr[:30]
    scr = scr[30:]
    xi = lax.axis_index("dp")
    rings = []
    loads = [pltpu.make_async_copy(a, b, isem.at[i]) for i, (a, b) in enumerate(
        ((dn_in, DB.at[:, 0]), (wo_in, wbuf.at[pl.ds(0, 512)]), (att_in, att), (q_in, q), (kv_in, KV), (dmid_in, ig_out)))]
    first = []
    if summed:
        def take(cls):
            got = scr[:cls.count]
            del scr[:cls.count]
            return got
        own_g, own_d, WU, WE = (scr.pop(0) for _ in range(4))
        def make(name, cls, *a):
            n, lag, off, pace, *more = plan[name]
            return cls(*a[:-1], take(cls), sems_out.at[len(rings)], n, a[-1] // n, lag, *more), off, pace
        rings.append(make("gate", HalfFirst, g_in.at[0], lambda u: own_g.at[u], o_gate, own_g.shape[1]))
        rings.append(make("down", HalfFirst, gd_in, lambda u: own_d.at[u], o_down, own_d.shape[1]))
        rings.append(make("up", LineFirst, WU, o_up.at[0], WU.shape[1]))
        rings.append(make("up_edge", LineFirst, WE, o_up.at[1], WE.shape[1]))
        rings.append(make("rest", HalfFirst, W3, lambda u: W3.at[xi, u], o_rest, QC))
        first = [pltpu.make_async_copy(a, b, isem.at[13 + i]) for i, (a, b) in enumerate(
            ((gd_in.at[xi], own_d), (g_in.at[0, xi], own_g), (g_in.at[1, 0], WU), (g_in.at[1, 1], WE)))]
    def tick(g):
        for ring, off, pace in rings[:-1]:
            if pace == 1:
                ring.tick(g - off)
            else:
                @pl.when((g - off) % pace == 0)
                def _():
                    ring.tick((g - off) // pace)
    def ptick(phase, it, k):
        mode = PHASES[phase]
        if mode == 1:
            tick(k + it)
        elif mode:
            @pl.when(it % mode == 0)
            def _():
                tick(k + it // mode)
    def after(phase, count, k):
        mode = PHASES[phase]
        return k + (-(-count // mode) if mode else 0)
    wt_load = pltpu.make_async_copy(wt_in, wbuf, isem.at[8])
    x1_loads = [pltpu.make_async_copy(x1_in.at[:, :, pl.ds(c * HC, HC)], PB.at[pl.ds(S * c, S)], isem.at[9 + c]) for c in range(4)]
    for c in loads[:2] + first + loads[2:]:
        c.start()
    devs = [{"tensor": sib}, {"tensor": ynb}]
    if summed:
        devs.append({"dp": 1 - xi})
        b = 2
        while b < nz:
            devs.append({"seq": zi ^ b})
            b *= 2
    entry(devs, True)
    def ga(s):
        return rc(DB.at[s, 0], DB.at[s, 1], sDB.at[0, s], rDB.at[0, s], {"tensor": sib})
    def gb(s):
        return rc(DB.at[s, 0], DB.at[s, 2], sDB.at[1, s], rDB.at[1, s], {"tensor": ynb})
    def gc(s):
        return rc(DB.at[s, 2], DB.at[s, 3], sDB.at[2, s], rDB.at[2, s], {"tensor": sib})
    loads[0].wait()
    for s in range(S):
        gb(s).start()
        ga(s).start()
    for c in first:
        c.wait()
    lax.fori_loop(0, PRE, lambda k, c: (tick(k), c)[1], 0)
    gb(0).wait_recv()
    gc(0).start()
    lax.fori_loop(PRE, 2 * PRE, lambda k, c: (tick(k), c)[1], 0)
    gb(1).wait_recv()
    gc(1).start()
    loads[1].wait()
    for s in range(S):
        ga(s).wait_recv()
        gc(s).wait_recv()

    def dast(it, c):
        s = it // 2
        hb = it % 2
        r = nt(DB[s, pl.ds(2 * hb, 2)].reshape(2 * RP, D), wbuf[0:512, :])
        for h in range(4):
            rows = pl.ds(pl.multiple_of((h % 2) * SPAN + hb * 2 * RP, 2 * RP), 2 * RP)
            da[s, h // 2, rows, :] = r[:, h * 128:(h + 1) * 128].astype(bf16)
        ptick("dast", it, 2 * PRE)
        return c
    lax.fori_loop(0, 2 * S, dast, 0)
    wt_load.start()
    k = after("dast", 2 * S, 2 * PRE)
    loads[2].wait()
    def dlt(it, c):
        s = it // 2
        g = it % 2
        d = da[s, g].astype(f32) * att[s, g].astype(f32)
        delta[s, g] = jnp.sum(d.T, axis=0, keepdims=True)
        dqT[s, g] = jnp.zeros((128, 2 * SPAN), f32)
        return c
    lax.fori_loop(0, 2 * S, dlt, 0)
    for c in loads[3:5]:
        c.wait()

    def put(row, at, value):
        lo = 0
        while lo < value.shape[0]:
            blk, r = (row + lo) // QC, (row + lo) % QC
            cnt = min(value.shape[0] - lo, QC - r)
            W3[blk // 2, blk % 2, r:r + cnt, at] = value[lo:lo + cnt, :]
            lo += cnt
    for s in range(S):
        for r in range(4):
            heads[s * SPAN:(s + 1) * SPAN, r * 128:(r + 1) * 128] = att[s, r // 2, (r % 2) * SPAN:(r % 2 + 1) * SPAN, :]
    def out_grad(k, c, x):
        at = pl.ds(pl.multiple_of(c * HC, HC), HC)
        g0 = nn(heads[...].T, DB[:, :, :, at].reshape(S * SPAN, HC)).astype(bf16)
        put(4 * NO, at, nn(po[...], g0).astype(bf16))
        ptick("out", c, k)
        return x
    if EARLY:
        lax.fori_loop(0, 4, functools.partial(out_grad, k), 0)
        k = after("out", 4, k)

    def unit(s, j, diag):
        lane = lax.broadcasted_iota(jnp.int32, (1, 128), 1)
        acc[...] = jnp.zeros((SPAN, 384), f32)
        for g in range(2):
            fm = in_ranges(lane, F_LANES[g])
            def body(qt, c):
                qa = pl.ds(pl.multiple_of(qt * TQ, TQ), TQ)
                kp = KV[s, j, :, g * 128:(g + 1) * 128]
                kv = jnp.concatenate([kp, KV[s, j, :, 256:384]], axis=1)
                qq = q[s, g, qa, :]
                d = da[s, g, qa, :]
                zero = jnp.zeros_like(d)
                d2 = jnp.concatenate([jnp.where(fm, d, zero), jnp.where(fm, zero, d)], axis=1)
                sT = nt(kp, qq) * (SCALE * LOG2E) - lse[s, g, :, qa]
                if diag:
                    sT = causal(sT, qt, TQ, RP, t)
                p = jnp.exp2(sT)
                ds = (p * (nt(kv, d2) - delta[s, g, :, qa])).astype(bf16)
                dk = nn(ds, qq) * SCALE
                dv = nn(p.astype(bf16), d2)
                acc[:, g * 128:(g + 1) * 128] += dk + dv[:, :128]
                acc[:, 256:384] += dv[:, 128:]
                dqT[s, g, :, qa] += tn(kp, ds)
                return c
            lax.fori_loop(0, NT, body, 0, unroll=2)
        PB[j * S + s] = acc[...].astype(bf16)

    def chain(s, j):
        return rc(RB.at[j, s], RB.at[j, s], sKV.at[j, s], rKV.at[j, s], {"seq": zi - 1})
    def event(e):
        j = e // S
        s = e % S
        @pl.when(both(both(e >= 0, e < nz * S), j <= zi))
        def _():
            acc[...] = PB[e].astype(f32)
            @pl.when(zi < nz - 1)
            def _():
                chain(s, j).wait_recv()
                acc[...] += RB[j, s].astype(f32)
            @pl.when(j < zi)
            def _():
                RB[j, s] = acc[...].astype(bf16)
                chain(s, j).start()
            @pl.when(j == zi)
            def _():
                for g in range(2):
                    u = acc[:, g * 128:(g + 1) * 128]
                    dqkv[s, :, 512 + g * 128:512 + (g + 1) * 128] = (u * cos[g] - pltpu.roll(u, 64, 1) * sin[g]).astype(bf16)
                dqkv[s, :, 768:896] = acc[:, 256:384].astype(bf16)
    def step(m, c):
        j = m // S
        s = m % S
        @pl.when(j < zi)
        def _():
            unit(s, j, False)
        @pl.when(j == zi)
        def _():
            unit(s, j, True)
        event(m - 1 - HOP * (nz - 1 - zi))
        ptick("steps", m, k)
        return c
    steps = nz * S + 1 + HOP * (nz - 1)
    lax.fori_loop(0, steps, step, 0)
    k = after("steps", steps, k)
    for c in x1_loads:
        c.start()

    if not EARLY:
        lax.fori_loop(0, 4, functools.partial(out_grad, k), 0)
        k = after("out", 4, k)
    def rotate(c, x):
        s = c // 2
        for g in range(2):
            @pl.when(c % 2 == g)
            def _():
                for hh in range(2):
                    u = dqT[s, g, :, hh * SPAN:(hh + 1) * SPAN].T * SCALE
                    dqkv[s, :, (2 * g + hh) * 128:(2 * g + hh + 1) * 128] = (u * cos[g] - pltpu.roll(u, 64, 1) * sin[g]).astype(bf16)
        return x
    lax.fori_loop(0, 2 * S, rotate, 0)
    wt_load.wait()
    for s in range(S):
        ga(s).wait_send()
        gb(s).wait_send()
        gc(s).wait_send()

    def ra(s, hb):
        return rc(DB.at[s, 2 + hb], rs1.at[s, hb], sR1.at[s, hb], rR1.at[s, hb], {"tensor": sib})
    def rb(s):
        return rc(DB.at[s, 1], rs2.at[s], sR2.at[s], rR2.at[s], {"tensor": ynb})
    def d_one(it, c):
        s = it // 2
        hb = 1 - it % 2
        rows = pl.ds(pl.multiple_of(hb * 2 * RP, 2 * RP), 2 * RP)
        r = nn(dqkv[s, rows, :], wbuf[...])
        DB[s, hb] = r[:RP].astype(bf16)
        DB[s, 2 + hb] = r[RP:].astype(bf16)
        ra(s, hb).start()
        ptick("done", it, k)
        return c
    lax.fori_loop(0, 2 * S, d_one, 0)
    k = after("done", 2 * S, k)
    for s in range(S):
        ra(s, 1).wait_recv()
        DB[s, 1] = add(DB.at[s, 1], rs1.at[s, 1])
        rb(s).start()
    for c in x1_loads:
        c.wait()
    def in_grad(c, x):
        at = pl.ds(pl.multiple_of(c * HC, HC), HC)
        g0 = nn(dqkv[...].reshape(S * SPAN, 896).T, PB[pl.ds(S * c, S)].reshape(S * SPAN, HC)).astype(bf16)
        gq = tn(pq[...], g0[0:512]).astype(bf16)
        gkv = tn(pkv[...], g0[512:896]).astype(bf16)
        put(0, at, gq)
        put(2 * NO, at, gkv)
        ptick("in", c, k)
        return x
    lax.fori_loop(0, 4, in_grad, 0)
    k = after("in", 4, k)
    if summed:
        start_rest = k
        def joint(g):
            for i, (ring, off, pace) in enumerate(rings):
                kk = g - (start_rest if i == len(rings) - 1 else off)
                if pace == 1:
                    ring.tick(kk)
                else:
                    @pl.when(kk % pace == 0)
                    def _():
                        ring.tick(kk // pace)
    else:
        o3 = pltpu.make_async_copy(W3, o_rest, sems_out.at[4])
        o3.start()
        def joint(g):
            pass
    joint(k)
    joint(k + 1)
    k = k + 2
    loads[5].wait()
    gain = gain1[...].astype(f32).reshape(1, D)
    gp1 = None
    for s in range(S):
        ra(s, 0).wait_recv()
        rb(s).wait_recv()
        e = DB[s, 0].astype(f32) + rs1[s, 0].astype(f32) + rs2[s].astype(f32)
        gp, dv = norm_back_rows(tok[s].astype(f32), e, gain)
        gp1 = gp if gp1 is None else gp1 + gp
        ig_out[s] += dv
    gains_out[...] = jnp.concatenate([gp1, gp2[...], jnp.zeros((6, D), f32)], axis=0)
    if summed:
        peers = [{"tensor": sib}, {"tensor": ynb}, {"dp": 1 - xi}]
        b = 1
        while b < nz:
            peers.append({"seq": zi ^ b})
            b *= 2
        for m, dev in enumerate(peers):
            GS[m] = gains_out[...]
            c = rc(GS.at[m], GL.at[m], sG.at[m], rG.at[m], dev)
            c.start()
            joint(k)
            k = k + 1
            c.wait()
            gains_out[...] += GL[m]
        last = max((start_rest if i == len(rings) - 1 else off) + (ring.ticks - 1) * pace + 1 for i, (ring, off, pace) in enumerate(rings))
        lax.fori_loop(k, last, lambda m, c: (joint(m), c)[1], 0)
    for s in range(S):
        ra(s, 0).wait_send()
        ra(s, 1).wait_send()
        rb(s).wait_send()
        for j in range(nz):
            @pl.when(j < zi)
            def _():
                chain(s, j).wait_send()
    if summed:
        for ring, off, pace in rings:
            ring.drain()
    else:
        o3.wait()


PLAN = {"gate": (6, 1, 0, 2), "down": (16, 2, 12, 1, True), "up": (12, 1, 25, 3), "up_edge": (8, 1, 17, 3, True), "rest": (18, 3, 0, 1)}


def attend_backward(dn, q, KV, att, lse, wo, wt, X1, pq, pkv, po, cos, sin, tok, dmid, gain1, gp2, g, gd, summed, plan=PLAN):
    nz = lax.axis_size("seq")
    S, RP, D = tok.shape
    SPAN = 4 * RP
    FL = g.shape[-1]
    QG, QD, QC = D // 4, FL // 4, CROWS // 4
    V = pl.BlockSpec(memory_space=pltpu.VMEM)
    A = pl.BlockSpec(memory_space=pl.ANY)
    sd = jax.ShapeDtypeStruct
    dma = pltpu.SemaphoreType.DMA
    vm = pltpu.VMEM
    scratch = [vm((S, 4, RP, D), bf16), vm(q.shape, bf16), vm(KV.shape, bf16), vm(att.shape, bf16), vm((896, D), bf16),
               vm(q.shape, bf16), vm((S, 2, 1, 2 * SPAN), f32), vm((S, 2, 128, 2 * SPAN), f32), vm((SPAN, 384), f32),
               vm((nz * S, SPAN, 384), bf16), vm((nz - 1, S, SPAN, 384), bf16), vm((S, SPAN, 896), bf16),
               vm((S, 2, RP, D), bf16), vm((S, RP, D), bf16), vm((2, 2, QC, D), bf16), vm((S * SPAN, 512), bf16),
               vm((6, 8, D), f32), vm((6, 8, D), f32),
               dma((nz, S)), dma((nz, S)), dma((S, 2)), dma((S, 2)), dma((S,)), dma((S,)), dma((6,)), dma((6,)), dma((3, S)), dma((3, S)), dma((17,)), dma((5,))]
    if summed:
        scratch += [vm((2, QG, FL), bf16), vm((2, QD, D), bf16), vm((2, QG, FL), bf16), vm((2, QG, FL), bf16)]
        for name, cls, Q, C in (("gate", HalfFirst, QG, FL), ("down", HalfFirst, QD, D), ("up", LineFirst, QG, FL), ("up_edge", LineFirst, QG, FL), ("rest", HalfFirst, QC, D)):
            n = plan[name][0]
            scratch += cls.scratch(n, Q // n, C)
    return pl.pallas_call(
        functools.partial(backward_kernel, summed, plan),
        out_shape=[sd((S, RP, D), f32), sd((8, D), f32), sd((2, 2, QG, FL), bf16), sd((2, 2, QG, FL), bf16), sd((2, 2, QD, D), bf16),
                   sd((2, 2, QC, D), bf16)],
        in_specs=[A, A, A, A, V, A, A, A, V, V, V, V, V, V, A, V, V, A, A],
        out_specs=[V, V, A, A, A, A],
        scratch_shapes=scratch,
        compiler_params=pltpu.CompilerParams(collective_id=2, has_side_effects=True, vmem_limit_bytes=VMEM_BYTES),
        name="attend_backward")(dn, q, KV, att, lse, wo, wt, X1.reshape(S, SPAN, D), pq, pkv, po, cos, sin, tok, dmid, gain1, gp2,
                                g.reshape(2, 2, 2, QG, FL), gd.reshape(2, 2, QD, D))


def local(
    tokens, attn_gain, w_query, w_key, w_value, w_output, ffn_gain, w_gate, w_up, w_down, cotangent
):
    t = lax.axis_index("tensor")
    zi = lax.axis_index("seq")
    pq, pkv, po = (jnp.asarray(v, bf16) for v in pick_tables())
    tok = jnp.swapaxes(tokens, 0, 1)
    cot = jnp.swapaxes(cotangent, 0, 1)
    S, RP, D = tok.shape
    cos, sin = rope_tables(zi * 4 * RP, 4 * RP, t)
    X1, C, q, KV, att, lse, wqkv, wo, mid, n2 = attend_forward(
        tok, cot, w_query, w_key.T, w_value.T, w_output, pq, pkv, po, cos, sin, attn_gain, ffn_gain)
    summed = lax.axis_size("dp") == 2
    dn, g, gd, down, dmid, gp2 = feed_forward(n2, mid, C, w_gate, w_up, w_down, ffn_gain)
    down_local = lax.psum_scatter(down, "tensor", scatter_dimension=0, tiled=True)[0]
    ig, gains, gate, up, wd, rest = attend_backward(
        dn, q, KV, att, lse, wo, wqkv, X1, pq, pkv, po, cos, sin, tok, dmid, attn_gain, gp2, g, gd, summed)
    if not summed:
        g, wd, rest = lax.psum((g.astype(f32), gd.astype(f32), rest.astype(f32)), ("dp", "seq"))
        gate, up = g[0], g[1]
        gains = lax.psum(gains, ("dp", "seq", "tensor"))
    rest = rest.reshape(-1, D)
    nq, nk = w_query.shape[1], w_key.shape[1]
    activation = (mid + down_local.astype(f32)).astype(bf16)
    return (
        jnp.swapaxes(activation, 0, 1),
        jnp.swapaxes(ig, 0, 1),
        gains[0],
        rest[:nq].astype(f32).T,
        rest[nq:nq + nk].astype(f32).T,
        rest[nq + nk:nq + 2 * nk].astype(f32).T,
        rest[nq + 2 * nk:].astype(f32),
        gains[1],
        gate.reshape(D, -1).astype(f32),
        up.reshape(D, -1).astype(f32),
        wd.reshape(-1, D).astype(f32),
    )


def solution(mesh):
    rows = P(("seq", "tensor"), "dp", None)
    columns = P(None, "tensor")
    placed = (rows, P(), columns, columns, columns, P("tensor", None), P(), columns, columns, P("tensor", None), rows)
    return jax.shard_map(
        local,
        mesh=mesh,
        in_specs=placed,
        out_specs=(rows, rows, P(), columns, columns, columns, P("tensor", None), P(), columns, columns, P("tensor", None)),
        check_vma=False,
    )
```

```python
import functools
import numpy as np
import jax, jax.numpy as jnp
from jax import lax
from jax.sharding import PartitionSpec as P
import jax.experimental.pallas as pl
import jax.experimental.pallas.tpu as pltpu

MESH = pl.DeviceIdType.MESH
bf16 = jnp.bfloat16
f32 = jnp.float32
HEAD_DIM = 96
HALF = 48
epsilon = 1e-05
theta = 100000.0
LOG2E = 1.4426950408889634
SCALE = HEAD_DIM ** -0.5
VMEM_BYTES = 63 << 20

K_LANES = [list(range(0, 48)) + list(range(64, 112)), list(range(16, 64)) + list(range(80, 128))]
F_LANES = [list(range(48, 64)) + list(range(112, 128)), list(range(0, 16)) + list(range(64, 80))]
V_LANES = [list(range(0, 48)) + list(range(64, 80)), list(range(48, 64)) + list(range(80, 128))]


def pick_tables():
    q = np.zeros((512, 384), np.float32)
    kv = np.zeros((384, 384), np.float32)
    o = np.zeros((384, 512), np.float32)
    for h in range(4):
        for d in range(96):
            q[h * 128 + K_LANES[h // 2][d], h * 96 + d] = 1
            lane = F_LANES[h // 2][d] if d < 32 else V_LANES[h // 2][d - 32]
            o[h * 96 + d, h * 128 + lane] = 1
    for g in range(2):
        for d in range(96):
            kv[g * 128 + K_LANES[g][d], g * 96 + d] = 1
            lane = g * 128 + F_LANES[g][d] if d < 32 else 256 + V_LANES[g][d - 32]
            kv[lane, 192 + g * 96 + d] = 1
    return q, kv, o


def in_ranges(lane, lanes):
    mask = None
    lo = prev = lanes[0]
    runs = []
    for x in lanes[1:] + [None]:
        if x is None or x != prev + 1:
            runs.append((lo, prev))
            lo = x
        prev = x
    for a, b in runs:
        m = jnp.logical_and(lane >= a, lane <= b)
        mask = m if mask is None else jnp.logical_or(mask, m)
    return mask


def rope_tables(row_start, span, t):
    rate = np.zeros((2, 128), np.float32)
    sign = np.zeros((2, 128), np.float32)
    for g in range(2):
        for d in range(96):
            rate[g, K_LANES[g][d]] = d % HALF
            sign[g, K_LANES[g][d]] = -1.0 if d < HALF else 1.0
    used = np.abs(sign)
    rates = used * theta ** (-(jnp.asarray(rate) * 2.0 / HEAD_DIM))
    i = jnp.arange(span, dtype=jnp.int32)
    c = span // 4
    places = (row_start + ((i // c) ^ t) * c + i % c).astype(f32)
    angle = places[None, :, None] * rates[:, None, :]
    return jnp.cos(angle), jnp.sin(angle) * sign[:, None, :]


def nt(a, b):
    return lax.dot_general(a, b, (((1,), (1,)), ((), ())), preferred_element_type=f32)


def nn(a, b):
    return jnp.dot(a, b, preferred_element_type=f32)


def tn(a, b):
    return lax.dot_general(a, b, (((0,), (0,)), ((), ())), preferred_element_type=f32)


def rc(src, dst, ss, rr, dev):
    return pltpu.make_async_remote_copy(src, dst, ss, rr, device_id=dev, device_id_type=MESH)


def entry(devs, z_line):
    b = pltpu.get_barrier_semaphore()
    count = len(devs)
    for dev in devs:
        pl.semaphore_signal(b, inc=1, device_id=dev, device_id_type=MESH)
    if z_line:
        zi = lax.axis_index("seq")
        nz = lax.axis_size("seq")
        @pl.when(zi > 0)
        def _():
            pl.semaphore_signal(b, inc=1, device_id={"seq": zi - 1}, device_id_type=MESH)
        @pl.when(zi < nz - 1)
        def _():
            pl.semaphore_signal(b, inc=1, device_id={"seq": zi + 1}, device_id_type=MESH)
        count = count + (zi > 0).astype(jnp.int32) + (zi < nz - 1).astype(jnp.int32)
    pl.semaphore_wait(b, count)


def causal(sT, qt, TQ, RP, t):
    span = sT.shape[0]
    ki = lax.broadcasted_iota(jnp.int32, (span, 1), 0)
    qi = lax.broadcasted_iota(jnp.int32, (1, TQ), 1) + (qt % (span // TQ)) * TQ
    kpos = ((ki // RP) ^ t) * RP + ki % RP
    qpos = ((qi // RP) ^ t) * RP + qi % RP
    return jnp.where(kpos <= qpos, sT, -1e30)


def rms(v, gain):
    return v * lax.rsqrt(jnp.mean(v * v, axis=-1, keepdims=True) + epsilon) * gain


def norm_back_rows(v, e, gain):
    inv = lax.rsqrt(jnp.mean(v * v, axis=-1, keepdims=True) + epsilon)
    part = jnp.sum(e * v * inv, axis=0, keepdims=True)
    sc = e * gain
    return part, inv * sc - v * (inv * inv * inv) * jnp.mean(sc * v, axis=-1, keepdims=True)


def forward_kernel(nz, tok, cot, wq, wk, wv, w_out, pq, pkv, po, cos, sin, gain1, gain2,
                   x1_out, c_out, q_out, kv_out, att_out, lse_out, wqkv_out, wo_out, mid_out, n2_out,
                   xn, X, C, KV, q, att, lse, wqkv, wo, m_s, l_s, o_s, part, rs1, ysend, rs2,
                   sA, rA, sB, rB, sC, rC, sKV, rKV, sR1, rR1, sR2, rR2, osem):
    t = lax.axis_index("tensor")
    zi = lax.axis_index("seq")
    sib, ynb = t ^ 1, t ^ 2
    S, RP, D = tok.shape
    SPAN = 4 * RP
    TQ = 256
    NT = 2 * SPAN // TQ
    g1 = gain1[...].astype(f32).reshape(1, D)
    for s in range(S):
        xn[s] = rms(tok[s].astype(f32), g1).astype(bf16)
    entry([{"tensor": sib}, {"tensor": ynb}], True)

    def ga(w, s):
        return rc((xn, cot)[w].at[s], (X, C)[w].at[s, 1], sA.at[w, s], rA.at[w, s], {"tensor": sib})
    def gb(w, s):
        return rc((xn, cot)[w].at[s], (X, C)[w].at[s, 2], sB.at[w, s], rB.at[w, s], {"tensor": ynb})
    def gc(w, s):
        buf = (X, C)[w]
        return rc(buf.at[s, 2], buf.at[s, 3], sC.at[w, s], rC.at[w, s], {"tensor": sib})
    for s in range(S):
        gb(0, s).start()
        ga(0, s).start()
    wqkv[0:512, :] = nt(pq[...], wq[...]).astype(bf16)
    wqkv[512:896, :] = (nn(pkv[:, 0:192], wk[...]) + nn(pkv[:, 192:384], wv[...])).astype(bf16)
    for s in range(S):
        X[s, 0] = xn[s]

    def kvc(s, j, hb):
        at = pl.ds(hb * 2 * RP, 2 * RP)
        return rc(KV.at[s, j, at], KV.at[s, j, at], sKV.at[s, j, hb], rKV.at[s, j, hb], {"seq": zi + 1})
    def send_own(s, hb):
        @pl.when(zi < nz - 1)
        def _():
            kvc(s, zi, hb).start()
    def arrive(s, h, hb):
        j = zi - 1 - h
        @pl.when(j >= 0)
        def _():
            kvc(s, j, hb).wait_recv()
            @pl.when(zi < nz - 1)
            def _():
                kvc(s, j, hb).start()

    def project(s, hb):
        r = nt(X[s, 2 * hb:2 * hb + 2].reshape(2 * RP, D), wqkv[...])
        base = hb * 2 * RP
        for slot in range(6):
            g = slot // 2 if slot < 4 else slot - 4
            u = r[:, slot * 128:(slot + 1) * 128]
            u = u * cos[g, base:base + 2 * RP, :] + pltpu.roll(u, 64, 1) * sin[g, base:base + 2 * RP, :]
            if slot < 4:
                q[s, g, (slot % 2) * SPAN + base:(slot % 2) * SPAN + base + 2 * RP, :] = u.astype(bf16)
            else:
                KV[s, zi, base:base + 2 * RP, g * 128:(g + 1) * 128] = u.astype(bf16)
        KV[s, zi, base:base + 2 * RP, 256:384] = r[:, 768:896].astype(bf16)

    def unit(s, j, diag):
        def tile(g, qt):
            qa = pl.ds(pl.multiple_of(qt * TQ, TQ), TQ)
            kp = KV[s, j, :, g * 128:(g + 1) * 128]
            sT = nt(kp, q[s, g, qa, :]) * (SCALE * LOG2E)
            if diag:
                sT = causal(sT, qt, TQ, RP, t)
            mx = jnp.max(sT, axis=0, keepdims=True)
            if diag:
                m = mx
            else:
                m0 = m_s[s, g, :, qa]
                m = jnp.maximum(m0, mx)
                al = jnp.exp2(m0 - m)
            p = jnp.exp2(sT - m)
            total = jnp.sum(p, axis=0, keepdims=True)
            kv = jnp.concatenate([kp, KV[s, j, :, 256:384]], axis=1)
            o = tn(kv, p.astype(bf16))
            m_s[s, g, :, qa] = m
            if diag:
                l_s[s, g, :, qa] = total
                o_s[s, g, :, qa] = o
            else:
                l_s[s, g, :, qa] = l_s[s, g, :, qa] * al + total
                o_s[s, g, :, qa] = o_s[s, g, :, qa] * al + o
        def body(qt, c):
            tile(0, qt)
            tile(1, qt)
            return c
        lax.fori_loop(0, NT, body, 0, unroll=2)
    def hop(s, h):
        @pl.when(zi - 1 - h >= 0)
        def _():
            unit(s, zi - 1 - h, False)

    def rs_a(s):
        return rc(part.at[s, 1], rs1.at[s], sR1.at[s], rR1.at[s], {"tensor": sib})
    def rs_b(s):
        return rc(ysend.at[s], rs2.at[s], sR2.at[s], rR2.at[s], {"tensor": ynb})
    def finish(s):
        lane = lax.broadcasted_iota(jnp.int32, (128, 1), 0)
        for g in range(2):
            lse[s, g] = m_s[s, g] + jnp.log2(l_s[s, g])
            fm = in_ranges(lane, F_LANES[g])
            vm = in_ranges(lane, V_LANES[g])
            o = jnp.where(fm, o_s[s, g, 0:128, :], jnp.where(vm, o_s[s, g, 128:256, :], 0.0)) * (1.0 / l_s[s, g])
            att[s, g] = o.T.astype(bf16)
        for par in (1, 0):
            a = jnp.concatenate([jnp.concatenate([att[s, g, hh * SPAN + r * RP:hh * SPAN + (r + 1) * RP, :]
                                                  for g in range(2) for hh in range(2)], axis=1) for r in (par, par + 2)], axis=0)
            part[s, par] = nn(a, wo[...]).astype(bf16).reshape(2, RP, D)
            if par == 1:
                rs_a(s).start()
    def rs_mid(s):
        rs_a(s).wait_recv()
        ysend[s] = (part[s, 0, 1].astype(f32) + rs1[s, 1].astype(f32)).astype(bf16)
        rs_b(s).start()
    def rs_end(s):
        rs_b(s).wait_recv()
        mid = tok[s].astype(f32) + part[s, 0, 0].astype(f32) + rs1[s, 0].astype(f32) + rs2[s].astype(f32)
        mid_out[s] = mid
        n2_out[s] = rms(mid, gain2[...].astype(f32).reshape(1, D)).astype(bf16)

    ga(0, 0).wait_recv()
    project(0, 0)
    send_own(0, 0)
    ga(0, 1).wait_recv()
    project(1, 0)
    wo[...] = tn(po[...], w_out[...]).astype(bf16)
    gb(0, 0).wait_recv()
    gc(0, 0).start()
    arrive(0, 0, 0)
    gc(0, 0).wait_recv()
    project(0, 1)
    send_own(0, 1)
    arrive(0, 1, 0)
    gb(0, 1).wait_recv()
    gc(0, 1).start()
    for s in range(S):
        gb(1, s).start()
        ga(1, s).start()
    unit(0, zi, True)
    arrive(0, 0, 1)
    gc(0, 1).wait_recv()
    project(1, 1)
    arrive(0, 1, 1)
    send_own(1, 0)
    send_own(1, 1)
    hop(0, 0)
    for h in range(2, nz - 1):
        arrive(0, h, 0)
        arrive(0, h, 1)
    for s in range(S):
        C[s, 0] = cot[s]
    def more(h, c):
        hop(0, h)
        return c
    hop(0, 1)
    arrive(1, 0, 0)
    arrive(1, 0, 1)
    lax.fori_loop(2, nz - 1, more, 0)
    finish(0)
    unit(1, zi, True)
    gb(1, 0).wait_recv()
    gc(1, 0).start()
    rs_mid(0)
    arrive(1, 1, 0)
    arrive(1, 1, 1)
    hop(1, 0)
    gb(1, 1).wait_recv()
    gc(1, 1).start()
    hop(1, 1)
    rs_end(0)
    def rest(h, c):
        arrive(1, h, 0)
        arrive(1, h, 1)
        hop(1, h)
        return c
    lax.fori_loop(2, nz - 1, rest, 0)
    finish(1)
    for s in range(S):
        gc(1, s).wait_recv()
        ga(1, s).wait_recv()
    outs = [pltpu.make_async_copy(a, o, osem.at[n]) for n, (a, o) in enumerate(
        ((X, x1_out), (C, c_out), (q, q_out), (KV, kv_out), (att, att_out), (lse, lse_out), (wqkv, wqkv_out), (wo, wo_out)))]
    for o in outs:
        o.start()
    rs_mid(1)
    rs_end(1)
    for s in range(S):
        for w in range(2):
            ga(w, s).wait_send()
            gb(w, s).wait_send()
            gc(w, s).wait_send()
        rs_a(s).wait_send()
        rs_b(s).wait_send()
        for j in range(nz):
            @pl.when(jnp.logical_and(j <= zi, zi < nz - 1))
            def _():
                for hb in range(2):
                    kvc(s, j, hb).wait_send()
    for o in outs:
        o.wait()


def attend_forward(tok, cot, wq, wk, wv, w_out, pq, pkv, po, cos, sin, gain1, gain2):
    nz = lax.axis_size("seq")
    S, RP, D = tok.shape
    SPAN = 4 * RP
    V = pl.BlockSpec(memory_space=pltpu.VMEM)
    A = pl.BlockSpec(memory_space=pl.ANY)
    sd = jax.ShapeDtypeStruct
    dma = pltpu.SemaphoreType.DMA
    vm = pltpu.VMEM
    return pl.pallas_call(
        functools.partial(forward_kernel, nz),
        out_shape=[sd((S, 4, RP, D), bf16), sd((S, 4, RP, D), bf16), sd((S, 2, 2 * SPAN, 128), bf16),
                   sd((S, nz, SPAN, 384), bf16), sd((S, 2, 2 * SPAN, 128), bf16), sd((S, 2, 1, 2 * SPAN), f32),
                   sd((896, D), bf16), sd((512, D), bf16), sd((S, RP, D), f32), sd((S, RP, D), bf16)],
        in_specs=[V] * 13,
        out_specs=[A] * 8 + [V] * 2,
        scratch_shapes=[vm((S, RP, D), bf16), vm((S, 4, RP, D), bf16), vm((S, 4, RP, D), bf16),
                        vm((S, nz, SPAN, 384), bf16), vm((S, 2, 2 * SPAN, 128), bf16),
                        vm((S, 2, 2 * SPAN, 128), bf16), vm((S, 2, 1, 2 * SPAN), f32), vm((896, D), bf16), vm((512, D), bf16),
                        vm((S, 2, 1, 2 * SPAN), f32), vm((S, 2, 1, 2 * SPAN), f32), vm((S, 2, 256, 2 * SPAN), f32),
                        vm((S, 2, 2, RP, D), bf16), vm((S, 2, RP, D), bf16), vm((S, RP, D), bf16), vm((S, RP, D), bf16)]
        + [dma((2, S))] * 6 + [dma((S, nz, 2))] * 2 + [dma((S,))] * 4 + [dma((8,))],
        compiler_params=pltpu.CompilerParams(collective_id=0, has_side_effects=True, vmem_limit_bytes=VMEM_BYTES),
        name="attend_forward")(tok, cot, wq, wk, wv, w_out, pq, pkv, po, cos, sin, gain1, gain2)


def feed_kernel(summed, n2, mid, c_in, wg_in, wu_in, wd_in, gain2,
                dn_out, ga_out, gb_out, down_out, dmid_out, gpart_out,
                X, C, wg, wu, wd, dh, F, G, GD, XR, part, rs1, ysend, rs2, pd,
                sA, rA, sB, rB, sC, rC, sR1, rR1, sR2, rR2, sX, rX, isem, osem):
    t = lax.axis_index("tensor")
    sib, ynb = t ^ 1, t ^ 2
    S, RP, D = n2.shape
    FL = wg.shape[1]
    loads = [pltpu.make_async_copy(a, b, isem.at[i]) for i, (a, b) in enumerate(
        ((wd_in, wd), (c_in, C), (wg_in, wg), (wu_in, wu)))]
    for c in loads:
        c.start()
    xi = lax.axis_index("dp")
    ox = 1 - xi
    entry([{"tensor": sib}, {"tensor": ynb}] + ([{"dp": ox}] if summed else []), False)

    def ga(s):
        return rc(n2.at[s], X.at[s, 1], sA.at[s], rA.at[s], {"tensor": sib})
    def gb(s):
        return rc(n2.at[s], X.at[s, 2], sB.at[s], rB.at[s], {"tensor": ynb})
    def gc(s):
        return rc(X.at[s, 2], X.at[s, 3], sC.at[s], rC.at[s], {"tensor": sib})
    def ra(s, hb):
        return rc(part.at[s, 1, hb], rs1.at[s, hb], sR1.at[s, hb], rR1.at[s, hb], {"tensor": sib})
    def rb(s):
        return rc(ysend.at[s], rs2.at[s], sR2.at[s], rR2.at[s], {"tensor": ynb})
    for s in range(S):
        gb(s).start()
        ga(s).start()
    for s in range(S):
        X[s, 0] = n2[s]
    loads[0].wait()
    loads[1].wait()
    def early(s, c):
        dh[s] = nt(C[s].reshape(4 * RP, D), wd[...])
        return c
    lax.fori_loop(0, S, early, 0)
    loads[2].wait()
    loads[3].wait()

    def mlp(s, hb):
        x = X[s, pl.ds(2 * hb, 2)].reshape(2 * RP, D)
        rows = pl.ds(pl.multiple_of(hb * 2 * RP, 2 * RP), 2 * RP)
        g = nn(x, wg[...])
        u = nn(x, wu[...])
        sg = 1.0 / (1.0 + jnp.exp(-g))
        si = g * sg
        d = dh[s, rows]
        F[2, s, rows] = (si * u).astype(bf16)
        F[0, s, rows] = (d * u * sg * (1.0 + g * (1.0 - sg))).astype(bf16)
        F[1, s, rows] = (d * si).astype(bf16)
        r = nt(F[0, s, rows], wg[...]) + nt(F[1, s, rows], wu[...])
        part[s, 0, hb] = r[:RP].astype(bf16)
        part[s, 1, hb] = r[RP:].astype(bf16)
        ra(s, hb).start()
    def rs_mid(s):
        ra(s, 1).wait_recv()
        ysend[s] = (part[s, 0, 1].astype(f32) + rs1[s, 1].astype(f32)).astype(bf16)
        rb(s).start()
    gain = gain2[...].astype(f32).reshape(1, D)
    def rs_end(s):
        ra(s, 0).wait_recv()
        rb(s).wait_recv()
        e = part[s, 0, 0].astype(f32) + rs1[s, 0].astype(f32) + rs2[s].astype(f32)
        gp, dv = norm_back_rows(mid[s], e, gain)
        if s == 0:
            gpart_out[...] = gp
        else:
            gpart_out[...] += gp
        dm = C[s, 0].astype(f32) + dv
        dmid_out[s] = dm
        dn_out[s] = dm.astype(bf16)

    CH = 512
    def wgrad(a, src, f, c):
        at = pl.ds(pl.multiple_of(c * CH, CH), CH)
        left = src[:, :, :, at].reshape(S * 4 * RP, CH).T
        G[a, at, :] = nn(left, F[f].reshape(S * 4 * RP, FL)).astype(bf16)
    half = FL // 2
    def dgrad(h):
        left = F[2, :, :, pl.ds(pl.multiple_of(h * half, half), half)].reshape(S * 4 * RP, half).T
        for c in range(D // CH):
            at = pl.ds(c * CH, CH)
            GD[h, :, at] = nn(left, C[:, :, :, at].reshape(S * 4 * RP, CH)).astype(bf16)
    def down(s):
        r = nn(F[2, s], wd[...]).astype(bf16)
        for p in range(4):
            pd[t ^ p, s] = r[p * RP:(p + 1) * RP]

    ga(0).wait_recv()
    mlp(0, 0)
    gb(0).wait_recv()
    gc(0).start()
    gc(0).wait_recv()
    mlp(0, 1)
    ga(1).wait_recv()
    gb(1).wait_recv()
    gc(1).start()
    rs_mid(0)
    mlp(1, 0)
    gc(1).wait_recv()
    mlp(1, 1)
    rs_end(0)
    rs_mid(1)
    if summed:
        low, high = pl.ds(0, half // 2), pl.ds(half // 2, half // 2)
        xc = rc(GD.at[ox, low], XR, sX, rX, {"dp": ox})
        def part_of_two(i, x):
            dgrad(jnp.where(i == 0, ox, xi))
            @pl.when(i == 0)
            def _():
                xc.start()
            return x
        lax.fori_loop(0, 2, part_of_two, 0)
        o_down = [pltpu.make_async_copy(GD.at[h, at], gb_out.at[h, at], osem.at[n]) for n, (h, at) in enumerate(((ox, high), (xi, high), (xi, low)))]
    else:
        lax.fori_loop(0, 2, lambda h, x: (dgrad(h), x)[1], 0)
        o_down = [pltpu.make_async_copy(GD, gb_out, osem.at[0])]
    for o in o_down[:2]:
        o.start()
    down(0)
    down(1)
    o_pd = pltpu.make_async_copy(pd, down_out, osem.at[3])
    o_pd.start()
    rs_end(1)
    lax.fori_loop(0, D // CH, lambda c, x: (wgrad(0, X, 0, c), x)[1], 0)
    lax.fori_loop(0, D // CH, lambda c, x: (wgrad(1, X, 1, c), x)[1], 0)
    o_up = pltpu.make_async_copy(G, ga_out, osem.at[4])
    o_up.start()
    if summed:
        xc.wait()
        GD[xi, low] = (GD[xi, low].astype(f32) + XR[...].astype(f32)).astype(bf16)
        o_down[2].start()
    for s in range(S):
        ga(s).wait_send()
        gb(s).wait_send()
        gc(s).wait_send()
        ra(s, 0).wait_send()
        ra(s, 1).wait_send()
        rb(s).wait_send()
    for o in o_down + [o_pd, o_up]:
        o.wait()


def feed_forward(n2, mid, C, wg, wu, wd, gain2, summed):
    S, RP, D = n2.shape
    FL = wg.shape[1]
    V = pl.BlockSpec(memory_space=pltpu.VMEM)
    A = pl.BlockSpec(memory_space=pl.ANY)
    sd = jax.ShapeDtypeStruct
    dma = pltpu.SemaphoreType.DMA
    vm = pltpu.VMEM
    return pl.pallas_call(
        functools.partial(feed_kernel, summed),
        out_shape=[sd((S, RP, D), bf16), sd((2, D, FL), bf16), sd((2, FL // 2, D), bf16), sd((4, S, RP, D), bf16),
                   sd((S, RP, D), f32), sd((1, D), f32)],
        in_specs=[V, V, A, A, A, A, V],
        out_specs=[V, A, A, A, V, V],
        scratch_shapes=[vm((S, 4, RP, D), bf16), vm((S, 4, RP, D), bf16),
                        vm((D, FL), bf16), vm((D, FL), bf16), vm((FL, D), bf16), vm((S, 4 * RP, FL), f32),
                        vm((3, S, 4 * RP, FL), bf16), vm((2, D, FL), bf16), vm((2, FL // 2, D), bf16), vm((FL // 4, D), bf16), vm((S, 2, 2, RP, D), bf16), vm((S, 2, RP, D), bf16),
                        vm((S, RP, D), bf16), vm((S, RP, D), bf16), vm((4, S, RP, D), bf16)]
        + [dma((S,))] * 6 + [dma((S, 2))] * 2 + [dma((S,))] * 2 + [pltpu.SemaphoreType.DMA] * 2 + [dma((4,)), dma((5,))],
        compiler_params=pltpu.CompilerParams(collective_id=1, has_side_effects=True, vmem_limit_bytes=VMEM_BYTES),
        name="feed_forward")(n2, mid, C, wg, wu, wd, gain2)


def line(u, nz, edge=False):
    zi = lax.axis_index("seq")
    root = (nz - 1) * u if edge else nz // 2 - 1 + u
    below, above = zi < root, zi > root
    dist = jnp.where(below, root - zi, zi - root)
    return dist, below, above, zi == root, jnp.where(below, zi + 1, zi - 1)


def both(a, b):
    return jnp.logical_and(a, b)


def add(*refs):
    total = refs[0][...].astype(f32)
    for r in refs[1:]:
        total = total + r[...].astype(f32)
    return total.astype(bf16)


class Flow:
    def setup(self, n, p, lag, edge=False):
        self.n, self.p, self.lag, self.edge = n, p, lag, edge
        self.nz = lax.axis_size("seq")
        self.far = self.nz - 1 if edge else self.nz // 2
    def line(self, u):
        return line(u, self.nz, self.edge)
    def at(self, i):
        return pl.ds(pl.multiple_of(i * self.p, self.p), self.p)
    def valid(self, i):
        return both(i >= 0, i < self.n)
    def send_in(self, u, i, own, main, short, sems, act):
        dist, below, above, root, inward = self.line(u)
        ss, rr, r2 = sems
        if self.edge:
            act(rc(own, main.at[u, self.at(i)], ss.at[u, i], rr.at[u, i], {"seq": inward}))
            return
        to_short = both(dist == 1, below if u == 0 else above)
        @pl.when(to_short)
        def _():
            act(rc(own, short.at[self.at(i)], ss.at[u, i], r2.at[i], {"seq": inward}))
        @pl.when(jnp.logical_not(to_short))
        def _():
            act(rc(own, main.at[u, self.at(i)], ss.at[u, i], rr.at[u, i], {"seq": inward}))
    def from_main(self, u, i, own, main, sems):
        ss, rr, r2 = sems
        rc(own, main.at[u, self.at(i)], ss.at[u, i], rr.at[u, i], {"seq": self.line(u)[4]}).wait_recv()
    def from_short(self, u, i, own, short, sems):
        ss, rr, r2 = sems
        rc(own, short.at[self.at(i)], ss.at[u, i], r2.at[i], {"seq": self.line(u)[4]}).wait_recv()
    def outward(self, u, i, buf, bs, br, act):
        zi = lax.axis_index("seq")
        dist, below, above, root, inward = self.line(u)
        @pl.when(both(jnp.logical_not(above), zi > 0))
        def _():
            act(rc(buf.at[u, self.at(i)], buf.at[u, self.at(i)], bs.at[0, u, i], br.at[u, i], {"seq": zi - 1}))
        @pl.when(both(jnp.logical_not(below), zi < self.nz - 1))
        def _():
            act(rc(buf.at[u, self.at(i)], buf.at[u, self.at(i)], bs.at[1, u, i], br.at[u, i], {"seq": zi + 1}))
    def has_farther(self, u):
        zi = lax.axis_index("seq")
        dist, below, above, root, inward = self.line(u)
        return jnp.logical_or(both(below, zi > 0), both(above, zi < self.nz - 1))


class HalfFirst(Flow):
    count = 11
    @staticmethod
    def scratch(n, p, C):
        vm = pltpu.VMEM
        dma = pltpu.SemaphoreType.DMA
        Q = n * p
        return [vm((2, Q, C), bf16), vm((2, Q, C), bf16), vm((Q, C), bf16),
                dma((n,)), dma((n,)), dma((2, n)), dma((2, n)), dma((n,)), dma((2, 2, n)), dma((2, n)), dma((2, 2, n))]
    def __init__(self, src, own, out, bufs, osem, n, p, lag, ahead=False, halved=(0, 1)):
        self.setup(n, p, lag)
        self.src, self.own, self.out, self.osem = src, own, out, osem
        self.ahead = ahead
        self.halved = halved
        self.RX, self.RZ, self.R2, self.x1s, self.x1r, self.rs, self.rr, self.r2, self.bs, self.br, self.x2 = bufs
        self.ticks = n + lag * (2 * self.far + 2)
    def tick(self, k):
        lag, far, RX, RZ, R2 = self.lag, self.far, self.RX, self.RZ, self.R2
        xi = lax.axis_index("dp")
        ox = 1 - xi
        sems = (self.rs, self.rr, self.r2)
        start = lambda c: c.start()
        def x1(i):
            cls = pl.ds(self.halved[0], len(self.halved))
            return rc(self.src.at[ox, cls, self.at(i)], RX.at[cls, self.at(i)], self.x1s.at[i], self.x1r.at[i], {"dp": ox})
        def x2(u, i):
            return rc(RX.at[u, self.at(i)], self.out.at[xi, u, self.at(i)], self.x2.at[0, u, i], self.x2.at[1, u, i], {"dp": ox})
        @pl.when(k == 0 if self.ahead else self.valid(k))
        def _():
            if self.ahead:
                lax.fori_loop(0, self.n, lambda i, c: (x1(i).start(), c)[1], 0)
            else:
                x1(k).start()
        i1 = k - lag
        @pl.when(self.valid(i1))
        def _():
            x1(i1).wait()
            for u in self.halved:
                own = self.own(u).at[self.at(i1)]
                own[...] = add(own, RX.at[u, self.at(i1)])
        for u in range(2):
            dist, below, above, root, inward = self.line(u)
            i = k - lag * (1 + far - dist)
            @pl.when(self.valid(i))
            def _():
                own = self.own(u).at[self.at(i)]
                @pl.when(jnp.logical_not(root))
                def _():
                    @pl.when(self.has_farther(u))
                    def _():
                        self.from_main(u, i, own, RZ, sems)
                        own[...] = add(own, RZ.at[u, self.at(i)])
                    self.send_in(u, i, own, RZ, R2, sems, start)
                @pl.when(root)
                def _():
                    self.from_main(u, i, own, RZ, sems)
                    self.from_short(u, i, own, R2, sems)
                    RX[u, self.at(i)] = add(own, RZ.at[u, self.at(i)], R2.at[self.at(i)])
                    self.outward(u, i, RX, self.bs, self.br, start)
                    x2(u, i).start()
            i = k - lag * (1 + far + dist)
            @pl.when(both(self.valid(i), jnp.logical_not(root)))
            def _():
                rc(RX.at[u, self.at(i)], RX.at[u, self.at(i)], self.bs.at[0, u, i], self.br.at[u, i], {"seq": inward}).wait_recv()
                self.outward(u, i, RX, self.bs, self.br, start)
                x2(u, i).start()
            i = i - lag
            @pl.when(self.valid(i))
            def _():
                x2(u, i).wait()
                @pl.when(jnp.logical_not(root))
                def _():
                    self.send_in(u, i, self.own(u).at[self.at(i)], RZ, R2, sems, lambda c: c.wait_send())
                self.outward(u, i, RX, self.bs, self.br, lambda c: c.wait_send())
                pltpu.make_async_copy(RX.at[u, self.at(i)], self.out.at[xi, u, self.at(i)], self.osem).start()
    def drain(self):
        xi = lax.axis_index("dp")
        pltpu.make_async_copy(self.RX, self.out.at[xi], self.osem).wait()


class LineFirst(Flow):
    count = 10
    @staticmethod
    def scratch(n, p, C):
        vm = pltpu.VMEM
        dma = pltpu.SemaphoreType.DMA
        Q = n * p
        return [vm((2, Q, C), bf16), vm((Q, C), bf16), vm((Q, C), bf16),
                dma((2, n)), dma((2, n)), dma((n,)), dma((2, 2, n)), dma((2, n)), dma((n,)), dma((n,))]
    def __init__(self, W, out, bufs, osem, n, p, lag, edge=False):
        self.setup(n, p, lag, edge)
        self.W, self.out, self.osem = W, out, osem
        self.Z, self.XB, self.R2, self.rs, self.rr, self.r2, self.bs, self.br, self.xs, self.xr = bufs
        self.ticks = n + lag * (2 * self.far + 2)
    def tick(self, k):
        lag, far, W, Z = self.lag, self.far, self.W, self.Z
        ox = 1 - lax.axis_index("dp")
        sems = (self.rs, self.rr, self.r2)
        start = lambda c: c.start()
        def xb(u, i):
            return rc(W.at[u, self.at(i)], self.XB.at[self.at(i)], self.xs.at[i], self.xr.at[i], {"dp": ox})
        for u in range(2):
            dist, below, above, root, inward = self.line(u)
            i = k - lag * (far - dist)
            @pl.when(self.valid(i))
            def _():
                own = W.at[u, self.at(i)]
                @pl.when(jnp.logical_not(root))
                def _():
                    @pl.when(self.has_farther(u))
                    def _():
                        self.from_main(u, i, own, Z, sems)
                        own[...] = add(own, Z.at[u, self.at(i)])
                    self.send_in(u, i, own, Z, self.R2, sems, start)
                @pl.when(root)
                def _():
                    self.from_main(u, i, own, Z, sems)
                    if self.edge:
                        own[...] = add(own, Z.at[u, self.at(i)])
                    else:
                        self.from_short(u, i, own, self.R2, sems)
                        own[...] = add(own, Z.at[u, self.at(i)], self.R2.at[self.at(i)])
                    xb(u, i).start()
            i = k - lag * (far + 1)
            @pl.when(both(self.valid(i), root))
            def _():
                xb(u, i).wait()
                Z[u, self.at(i)] = add(W.at[u, self.at(i)], self.XB.at[self.at(i)])
                self.outward(u, i, Z, self.bs, self.br, start)
            i = k - lag * (far + 1 + dist)
            @pl.when(both(self.valid(i), jnp.logical_not(root)))
            def _():
                rc(Z.at[u, self.at(i)], Z.at[u, self.at(i)], self.bs.at[0, u, i], self.br.at[u, i], {"seq": inward}).wait_recv()
                self.outward(u, i, Z, self.bs, self.br, start)
            i = i - lag
            @pl.when(self.valid(i))
            def _():
                @pl.when(jnp.logical_not(root))
                def _():
                    self.send_in(u, i, W.at[u, self.at(i)], Z, self.R2, sems, lambda c: c.wait_send())
                self.outward(u, i, Z, self.bs, self.br, lambda c: c.wait_send())
                pltpu.make_async_copy(Z.at[u, self.at(i)], self.out.at[u, self.at(i)], self.osem).start()
    def drain(self):
        pltpu.make_async_copy(self.Z, self.out, self.osem).wait()


NO = 192
CROWS = 6 * NO
PHASES = {"dast": 1, "steps": 2, "out": 2, "done": 1, "in": 1}
EARLY = True
PRE = 4
HOP = 1


def backward_kernel(summed, plan, dn_in, q_in, kv_in, att_in, lse, wo_in, wt_in, x1_in, pq, pkv, po, cos, sin, tok, dmid_in, gain1, gp2,
                    g_in, gd_in, ig_out, gains_out, o_gate, o_up, o_down, o_rest, *scr):
    t = lax.axis_index("tensor")
    zi = lax.axis_index("seq")
    nz = lax.axis_size("seq")
    sib, ynb = t ^ 1, t ^ 2
    S, RP, D = tok.shape
    SPAN = 4 * RP
    TQ = 512
    NT = 2 * SPAN // TQ
    HC = D // 4
    QC = CROWS // 4
    scr = list(scr)
    (DB, q, KV, att, wbuf, da, delta, dqT, acc, PB, RB, dqkv, rs1, rs2, W3, heads, GS, GL,
     sKV, rKV, sR1, rR1, sR2, rR2, sG, rG, sDB, rDB, isem, sems_out) = scr[:30]
    scr = scr[30:]
    xi = lax.axis_index("dp")
    rings = []
    loads = [pltpu.make_async_copy(a, b, isem.at[i]) for i, (a, b) in enumerate(
        ((dn_in, DB.at[:, 0]), (wo_in, wbuf.at[pl.ds(0, 512)]), (att_in, att), (q_in, q), (kv_in, KV), (dmid_in, ig_out)))]
    first = []
    if summed:
        def take(cls):
            got = scr[:cls.count]
            del scr[:cls.count]
            return got
        own_g, own_d, WU, WE = (scr.pop(0) for _ in range(4))
        def make(name, cls, *a):
            n, lag, off, pace, *more = plan[name]
            return cls(*a[:-1], take(cls), sems_out.at[len(rings)], n, a[-1] // n, lag, *more), off, pace
        rings.append(make("gate", HalfFirst, g_in.at[0], lambda u: own_g.at[u], o_gate, own_g.shape[1]))
        rings.append(make("down", HalfFirst, gd_in, lambda u: own_d.at[u], o_down, own_d.shape[1]))
        rings.append(make("up", LineFirst, WU, o_up.at[0], WU.shape[1]))
        rings.append(make("up_edge", LineFirst, WE, o_up.at[1], WE.shape[1]))
        rings.append(make("rest", HalfFirst, W3, lambda u: W3.at[xi, u], o_rest, QC))
        first = [pltpu.make_async_copy(a, b, isem.at[13 + i]) for i, (a, b) in enumerate(
            ((gd_in.at[xi], own_d), (g_in.at[0, xi], own_g), (g_in.at[1, 0], WU), (g_in.at[1, 1], WE)))]
    def tick(g):
        for ring, off, pace in rings[:-1]:
            if pace == 1:
                ring.tick(g - off)
            else:
                @pl.when((g - off) % pace == 0)
                def _():
                    ring.tick((g - off) // pace)
    def ptick(phase, it, k):
        mode = PHASES[phase]
        if mode == 1:
            tick(k + it)
        elif mode:
            @pl.when(it % mode == 0)
            def _():
                tick(k + it // mode)
    def after(phase, count, k):
        mode = PHASES[phase]
        return k + (-(-count // mode) if mode else 0)
    wt_load = pltpu.make_async_copy(wt_in, wbuf, isem.at[8])
    x1_loads = [pltpu.make_async_copy(x1_in.at[:, :, pl.ds(c * HC, HC)], PB.at[pl.ds(S * c, S)], isem.at[9 + c]) for c in range(4)]
    for c in loads[:2] + first + loads[2:]:
        c.start()
    devs = [{"tensor": sib}, {"tensor": ynb}]
    if summed:
        devs.append({"dp": 1 - xi})
        b = 2
        while b < nz:
            devs.append({"seq": zi ^ b})
            b *= 2
    entry(devs, True)
    def ga(s):
        return rc(DB.at[s, 0], DB.at[s, 1], sDB.at[0, s], rDB.at[0, s], {"tensor": sib})
    def gb(s):
        return rc(DB.at[s, 0], DB.at[s, 2], sDB.at[1, s], rDB.at[1, s], {"tensor": ynb})
    def gc(s):
        return rc(DB.at[s, 2], DB.at[s, 3], sDB.at[2, s], rDB.at[2, s], {"tensor": sib})
    loads[0].wait()
    for s in range(S):
        gb(s).start()
        ga(s).start()
    for c in first:
        c.wait()
    lax.fori_loop(0, PRE, lambda k, c: (tick(k), c)[1], 0)
    gb(0).wait_recv()
    gc(0).start()
    lax.fori_loop(PRE, 2 * PRE, lambda k, c: (tick(k), c)[1], 0)
    gb(1).wait_recv()
    gc(1).start()
    loads[1].wait()
    for s in range(S):
        ga(s).wait_recv()
        gc(s).wait_recv()

    def dast(it, c):
        s = it // 2
        hb = it % 2
        r = nt(DB[s, pl.ds(2 * hb, 2)].reshape(2 * RP, D), wbuf[0:512, :])
        for h in range(4):
            rows = pl.ds(pl.multiple_of((h % 2) * SPAN + hb * 2 * RP, 2 * RP), 2 * RP)
            da[s, h // 2, rows, :] = r[:, h * 128:(h + 1) * 128].astype(bf16)
        ptick("dast", it, 2 * PRE)
        return c
    lax.fori_loop(0, 2 * S, dast, 0)
    wt_load.start()
    k = after("dast", 2 * S, 2 * PRE)
    loads[2].wait()
    def dlt(it, c):
        s = it // 2
        g = it % 2
        d = da[s, g].astype(f32) * att[s, g].astype(f32)
        delta[s, g] = jnp.sum(d.T, axis=0, keepdims=True)
        dqT[s, g] = jnp.zeros((128, 2 * SPAN), f32)
        return c
    lax.fori_loop(0, 2 * S, dlt, 0)
    for c in loads[3:5]:
        c.wait()

    def put(row, at, value):
        lo = 0
        while lo < value.shape[0]:
            blk, r = (row + lo) // QC, (row + lo) % QC
            cnt = min(value.shape[0] - lo, QC - r)
            W3[blk // 2, blk % 2, r:r + cnt, at] = value[lo:lo + cnt, :]
            lo += cnt
    for s in range(S):
        for r in range(4):
            heads[s * SPAN:(s + 1) * SPAN, r * 128:(r + 1) * 128] = att[s, r // 2, (r % 2) * SPAN:(r % 2 + 1) * SPAN, :]
    def out_grad(k, c, x):
        at = pl.ds(pl.multiple_of(c * HC, HC), HC)
        g0 = nn(heads[...].T, DB[:, :, :, at].reshape(S * SPAN, HC)).astype(bf16)
        put(4 * NO, at, nn(po[...], g0).astype(bf16))
        ptick("out", c, k)
        return x
    if EARLY:
        lax.fori_loop(0, 4, functools.partial(out_grad, k), 0)
        k = after("out", 4, k)

    def unit(s, j, diag):
        lane = lax.broadcasted_iota(jnp.int32, (1, 128), 1)
        acc[...] = jnp.zeros((SPAN, 384), f32)
        for g in range(2):
            fm = in_ranges(lane, F_LANES[g])
            def body(qt, c):
                qa = pl.ds(pl.multiple_of(qt * TQ, TQ), TQ)
                kp = KV[s, j, :, g * 128:(g + 1) * 128]
                kv = jnp.concatenate([kp, KV[s, j, :, 256:384]], axis=1)
                qq = q[s, g, qa, :]
                d = da[s, g, qa, :]
                zero = jnp.zeros_like(d)
                d2 = jnp.concatenate([jnp.where(fm, d, zero), jnp.where(fm, zero, d)], axis=1)
                sT = nt(kp, qq) * (SCALE * LOG2E) - lse[s, g, :, qa]
                if diag:
                    sT = causal(sT, qt, TQ, RP, t)
                p = jnp.exp2(sT)
                ds = (p * (nt(kv, d2) - delta[s, g, :, qa])).astype(bf16)
                dk = nn(ds, qq) * SCALE
                dv = nn(p.astype(bf16), d2)
                acc[:, g * 128:(g + 1) * 128] += dk + dv[:, :128]
                acc[:, 256:384] += dv[:, 128:]
                dqT[s, g, :, qa] += tn(kp, ds)
                return c
            lax.fori_loop(0, NT, body, 0, unroll=2)
        PB[j * S + s] = acc[...].astype(bf16)

    def chain(s, j):
        return rc(RB.at[j, s], RB.at[j, s], sKV.at[j, s], rKV.at[j, s], {"seq": zi - 1})
    def event(e):
        j = e // S
        s = e % S
        @pl.when(both(both(e >= 0, e < nz * S), j <= zi))
        def _():
            acc[...] = PB[e].astype(f32)
            @pl.when(zi < nz - 1)
            def _():
                chain(s, j).wait_recv()
                acc[...] += RB[j, s].astype(f32)
            @pl.when(j < zi)
            def _():
                RB[j, s] = acc[...].astype(bf16)
                chain(s, j).start()
            @pl.when(j == zi)
            def _():
                for g in range(2):
                    u = acc[:, g * 128:(g + 1) * 128]
                    dqkv[s, :, 512 + g * 128:512 + (g + 1) * 128] = (u * cos[g] - pltpu.roll(u, 64, 1) * sin[g]).astype(bf16)
                dqkv[s, :, 768:896] = acc[:, 256:384].astype(bf16)
    def step(m, c):
        j = m // S
        s = m % S
        @pl.when(j < zi)
        def _():
            unit(s, j, False)
        @pl.when(j == zi)
        def _():
            unit(s, j, True)
        event(m - 1 - HOP * (nz - 1 - zi))
        ptick("steps", m, k)
        return c
    steps = nz * S + 1 + HOP * (nz - 1)
    lax.fori_loop(0, steps, step, 0)
    k = after("steps", steps, k)
    for c in x1_loads:
        c.start()

    if not EARLY:
        lax.fori_loop(0, 4, functools.partial(out_grad, k), 0)
        k = after("out", 4, k)
    def rotate(c, x):
        s = c // 2
        for g in range(2):
            @pl.when(c % 2 == g)
            def _():
                for hh in range(2):
                    u = dqT[s, g, :, hh * SPAN:(hh + 1) * SPAN].T * SCALE
                    dqkv[s, :, (2 * g + hh) * 128:(2 * g + hh + 1) * 128] = (u * cos[g] - pltpu.roll(u, 64, 1) * sin[g]).astype(bf16)
        return x
    lax.fori_loop(0, 2 * S, rotate, 0)
    wt_load.wait()
    for s in range(S):
        ga(s).wait_send()
        gb(s).wait_send()
        gc(s).wait_send()

    def ra(s, hb):
        return rc(DB.at[s, 2 + hb], rs1.at[s, hb], sR1.at[s, hb], rR1.at[s, hb], {"tensor": sib})
    def rb(s):
        return rc(DB.at[s, 1], rs2.at[s], sR2.at[s], rR2.at[s], {"tensor": ynb})
    def d_one(it, c):
        s = it // 2
        hb = 1 - it % 2
        rows = pl.ds(pl.multiple_of(hb * 2 * RP, 2 * RP), 2 * RP)
        r = nn(dqkv[s, rows, :], wbuf[...])
        DB[s, hb] = r[:RP].astype(bf16)
        DB[s, 2 + hb] = r[RP:].astype(bf16)
        ra(s, hb).start()
        ptick("done", it, k)
        return c
    lax.fori_loop(0, 2 * S, d_one, 0)
    k = after("done", 2 * S, k)
    for s in range(S):
        ra(s, 1).wait_recv()
        DB[s, 1] = add(DB.at[s, 1], rs1.at[s, 1])
        rb(s).start()
    for c in x1_loads:
        c.wait()
    def in_grad(c, x):
        at = pl.ds(pl.multiple_of(c * HC, HC), HC)
        g0 = nn(dqkv[...].reshape(S * SPAN, 896).T, PB[pl.ds(S * c, S)].reshape(S * SPAN, HC)).astype(bf16)
        gq = tn(pq[...], g0[0:512]).astype(bf16)
        gkv = tn(pkv[...], g0[512:896]).astype(bf16)
        put(0, at, gq)
        put(2 * NO, at, gkv)
        ptick("in", c, k)
        return x
    lax.fori_loop(0, 4, in_grad, 0)
    k = after("in", 4, k)
    if summed:
        start_rest = k
        def joint(g):
            for i, (ring, off, pace) in enumerate(rings):
                kk = g - (start_rest if i == len(rings) - 1 else off)
                if pace == 1:
                    ring.tick(kk)
                else:
                    @pl.when(kk % pace == 0)
                    def _():
                        ring.tick(kk // pace)
    else:
        o3 = pltpu.make_async_copy(W3, o_rest, sems_out.at[4])
        o3.start()
        def joint(g):
            pass
    joint(k)
    joint(k + 1)
    k = k + 2
    loads[5].wait()
    gain = gain1[...].astype(f32).reshape(1, D)
    gp1 = None
    for s in range(S):
        ra(s, 0).wait_recv()
        rb(s).wait_recv()
        e = DB[s, 0].astype(f32) + rs1[s, 0].astype(f32) + rs2[s].astype(f32)
        gp, dv = norm_back_rows(tok[s].astype(f32), e, gain)
        gp1 = gp if gp1 is None else gp1 + gp
        ig_out[s] += dv
    gains_out[...] = jnp.concatenate([gp1, gp2[...], jnp.zeros((6, D), f32)], axis=0)
    if summed:
        peers = [{"tensor": sib}, {"tensor": ynb}, {"dp": 1 - xi}]
        b = 1
        while b < nz:
            peers.append({"seq": zi ^ b})
            b *= 2
        for m, dev in enumerate(peers):
            GS[m] = gains_out[...]
            c = rc(GS.at[m], GL.at[m], sG.at[m], rG.at[m], dev)
            c.start()
            joint(k)
            k = k + 1
            c.wait()
            gains_out[...] += GL[m]
        last = max((start_rest if i == len(rings) - 1 else off) + (ring.ticks - 1) * pace + 1 for i, (ring, off, pace) in enumerate(rings))
        lax.fori_loop(k, last, lambda m, c: (joint(m), c)[1], 0)
    for s in range(S):
        ra(s, 0).wait_send()
        ra(s, 1).wait_send()
        rb(s).wait_send()
        for j in range(nz):
            @pl.when(j < zi)
            def _():
                chain(s, j).wait_send()
    if summed:
        for ring, off, pace in rings:
            ring.drain()
    else:
        o3.wait()


PLAN = {"gate": (12, 2, 7, 1), "down": (8, 2, 0, 1, False, (1,)), "up": (8, 1, 21, 3), "up_edge": (24, 3, 2, 1, True), "rest": (18, 3, 0, 1)}


def attend_backward(dn, q, KV, att, lse, wo, wt, X1, pq, pkv, po, cos, sin, tok, dmid, gain1, gp2, g, gd, summed, plan=PLAN):
    nz = lax.axis_size("seq")
    S, RP, D = tok.shape
    SPAN = 4 * RP
    FL = g.shape[-1]
    QG, QD, QC = D // 4, FL // 4, CROWS // 4
    V = pl.BlockSpec(memory_space=pltpu.VMEM)
    A = pl.BlockSpec(memory_space=pl.ANY)
    sd = jax.ShapeDtypeStruct
    dma = pltpu.SemaphoreType.DMA
    vm = pltpu.VMEM
    scratch = [vm((S, 4, RP, D), bf16), vm(q.shape, bf16), vm(KV.shape, bf16), vm(att.shape, bf16), vm((896, D), bf16),
               vm(q.shape, bf16), vm((S, 2, 1, 2 * SPAN), f32), vm((S, 2, 128, 2 * SPAN), f32), vm((SPAN, 384), f32),
               vm((nz * S, SPAN, 384), bf16), vm((nz - 1, S, SPAN, 384), bf16), vm((S, SPAN, 896), bf16),
               vm((S, 2, RP, D), bf16), vm((S, RP, D), bf16), vm((2, 2, QC, D), bf16), vm((S * SPAN, 512), bf16),
               vm((6, 8, D), f32), vm((6, 8, D), f32),
               dma((nz, S)), dma((nz, S)), dma((S, 2)), dma((S, 2)), dma((S,)), dma((S,)), dma((6,)), dma((6,)), dma((3, S)), dma((3, S)), dma((17,)), dma((5,))]
    if summed:
        scratch += [vm((2, QG, FL), bf16), vm((2, QD, D), bf16), vm((2, QG, FL), bf16), vm((2, QG, FL), bf16)]
        for name, cls, Q, C in (("gate", HalfFirst, QG, FL), ("down", HalfFirst, QD, D), ("up", LineFirst, QG, FL), ("up_edge", LineFirst, QG, FL), ("rest", HalfFirst, QC, D)):
            n = plan[name][0]
            scratch += cls.scratch(n, Q // n, C)
    return pl.pallas_call(
        functools.partial(backward_kernel, summed, plan),
        out_shape=[sd((S, RP, D), f32), sd((8, D), f32), sd((2, 2, QG, FL), bf16), sd((2, 2, QG, FL), bf16), sd((2, 2, QD, D), bf16),
                   sd((2, 2, QC, D), bf16)],
        in_specs=[A, A, A, A, V, A, A, A, V, V, V, V, V, V, A, V, V, A, A],
        out_specs=[V, V, A, A, A, A],
        scratch_shapes=scratch,
        compiler_params=pltpu.CompilerParams(collective_id=2, has_side_effects=True, vmem_limit_bytes=VMEM_BYTES),
        name="attend_backward")(dn, q, KV, att, lse, wo, wt, X1.reshape(S, SPAN, D), pq, pkv, po, cos, sin, tok, dmid, gain1, gp2,
                                g.reshape(2, 2, 2, QG, FL), gd.reshape(2, 2, QD, D))


def local(
    tokens, attn_gain, w_query, w_key, w_value, w_output, ffn_gain, w_gate, w_up, w_down, cotangent
):
    t = lax.axis_index("tensor")
    zi = lax.axis_index("seq")
    pq, pkv, po = (jnp.asarray(v, bf16) for v in pick_tables())
    tok = jnp.swapaxes(tokens, 0, 1)
    cot = jnp.swapaxes(cotangent, 0, 1)
    S, RP, D = tok.shape
    cos, sin = rope_tables(zi * 4 * RP, 4 * RP, t)
    X1, C, q, KV, att, lse, wqkv, wo, mid, n2 = attend_forward(
        tok, cot, w_query, w_key.T, w_value.T, w_output, pq, pkv, po, cos, sin, attn_gain, ffn_gain)
    summed = lax.axis_size("dp") == 2
    dn, g, gd, down, dmid, gp2 = feed_forward(n2, mid, C, w_gate, w_up, w_down, ffn_gain, summed)
    down_local = lax.psum_scatter(down, "tensor", scatter_dimension=0, tiled=True)[0]
    ig, gains, gate, up, wd, rest = attend_backward(
        dn, q, KV, att, lse, wo, wqkv, X1, pq, pkv, po, cos, sin, tok, dmid, attn_gain, gp2, g, gd, summed)
    if not summed:
        g, wd, rest = lax.psum((g.astype(f32), gd.astype(f32), rest.astype(f32)), ("dp", "seq"))
        gate, up = g[0], g[1]
        gains = lax.psum(gains, ("dp", "seq", "tensor"))
    rest = rest.reshape(-1, D)
    nq, nk = w_query.shape[1], w_key.shape[1]
    activation = (mid + down_local.astype(f32)).astype(bf16)
    return (
        jnp.swapaxes(activation, 0, 1),
        jnp.swapaxes(ig, 0, 1),
        gains[0],
        rest[:nq].astype(f32).T,
        rest[nq:nq + nk].astype(f32).T,
        rest[nq + nk:nq + 2 * nk].astype(f32).T,
        rest[nq + 2 * nk:].astype(f32),
        gains[1],
        gate.reshape(D, -1).astype(f32),
        up.reshape(D, -1).astype(f32),
        wd.reshape(-1, D).astype(f32),
    )


def solution(mesh):
    rows = P(("seq", "tensor"), "dp", None)
    columns = P(None, "tensor")
    placed = (rows, P(), columns, columns, columns, P("tensor", None), P(), columns, columns, P("tensor", None), rows)
    return jax.shard_map(
        local,
        mesh=mesh,
        in_specs=placed,
        out_specs=(rows, rows, P(), columns, columns, columns, P("tensor", None), P(), columns, columns, P("tensor", None)),
        check_vma=False,
    )
```

```python
import functools
import numpy as np
import jax, jax.numpy as jnp
from jax import lax
from jax.sharding import PartitionSpec as P
import jax.experimental.pallas as pl
import jax.experimental.pallas.tpu as pltpu

MESH = pl.DeviceIdType.MESH
bf16 = jnp.bfloat16
f32 = jnp.float32
HEAD_DIM = 96
HALF = 48
epsilon = 1e-05
theta = 100000.0
LOG2E = 1.4426950408889634
SCALE = HEAD_DIM ** -0.5
VMEM_BYTES = 63 << 20

K_LANES = [list(range(0, 48)) + list(range(64, 112)), list(range(16, 64)) + list(range(80, 128))]
F_LANES = [list(range(48, 64)) + list(range(112, 128)), list(range(0, 16)) + list(range(64, 80))]
V_LANES = [list(range(0, 48)) + list(range(64, 80)), list(range(48, 64)) + list(range(80, 128))]


def pick_tables():
    q = np.zeros((512, 384), np.float32)
    kv = np.zeros((384, 384), np.float32)
    o = np.zeros((384, 512), np.float32)
    for h in range(4):
        for d in range(96):
            q[h * 128 + K_LANES[h // 2][d], h * 96 + d] = 1
            lane = F_LANES[h // 2][d] if d < 32 else V_LANES[h // 2][d - 32]
            o[h * 96 + d, h * 128 + lane] = 1
    for g in range(2):
        for d in range(96):
            kv[g * 128 + K_LANES[g][d], g * 96 + d] = 1
            lane = g * 128 + F_LANES[g][d] if d < 32 else 256 + V_LANES[g][d - 32]
            kv[lane, 192 + g * 96 + d] = 1
    return q, kv, o


def in_ranges(lane, lanes):
    mask = None
    lo = prev = lanes[0]
    runs = []
    for x in lanes[1:] + [None]:
        if x is None or x != prev + 1:
            runs.append((lo, prev))
            lo = x
        prev = x
    for a, b in runs:
        m = jnp.logical_and(lane >= a, lane <= b)
        mask = m if mask is None else jnp.logical_or(mask, m)
    return mask


def rope_tables(row_start, span, t):
    rate = np.zeros((2, 128), np.float32)
    sign = np.zeros((2, 128), np.float32)
    for g in range(2):
        for d in range(96):
            rate[g, K_LANES[g][d]] = d % HALF
            sign[g, K_LANES[g][d]] = -1.0 if d < HALF else 1.0
    used = np.abs(sign)
    rates = used * theta ** (-(jnp.asarray(rate) * 2.0 / HEAD_DIM))
    i = jnp.arange(span, dtype=jnp.int32)
    c = span // 4
    places = (row_start + ((i // c) ^ t) * c + i % c).astype(f32)
    angle = places[None, :, None] * rates[:, None, :]
    return jnp.cos(angle), jnp.sin(angle) * sign[:, None, :]


def nt(a, b):
    return lax.dot_general(a, b, (((1,), (1,)), ((), ())), preferred_element_type=f32)


def nn(a, b):
    return jnp.dot(a, b, preferred_element_type=f32)


def tn(a, b):
    return lax.dot_general(a, b, (((0,), (0,)), ((), ())), preferred_element_type=f32)


def rc(src, dst, ss, rr, dev):
    return pltpu.make_async_remote_copy(src, dst, ss, rr, device_id=dev, device_id_type=MESH)


def entry(devs, z_line):
    b = pltpu.get_barrier_semaphore()
    count = len(devs)
    for dev in devs:
        pl.semaphore_signal(b, inc=1, device_id=dev, device_id_type=MESH)
    if z_line:
        zi = lax.axis_index("seq")
        nz = lax.axis_size("seq")
        @pl.when(zi > 0)
        def _():
            pl.semaphore_signal(b, inc=1, device_id={"seq": zi - 1}, device_id_type=MESH)
        @pl.when(zi < nz - 1)
        def _():
            pl.semaphore_signal(b, inc=1, device_id={"seq": zi + 1}, device_id_type=MESH)
        count = count + (zi > 0).astype(jnp.int32) + (zi < nz - 1).astype(jnp.int32)
    pl.semaphore_wait(b, count)


def causal(sT, qt, TQ, RP, t):
    span = sT.shape[0]
    ki = lax.broadcasted_iota(jnp.int32, (span, 1), 0)
    qi = lax.broadcasted_iota(jnp.int32, (1, TQ), 1) + (qt % (span // TQ)) * TQ
    kpos = ((ki // RP) ^ t) * RP + ki % RP
    qpos = ((qi // RP) ^ t) * RP + qi % RP
    return jnp.where(kpos <= qpos, sT, -1e30)


def rms(v, gain):
    return v * lax.rsqrt(jnp.mean(v * v, axis=-1, keepdims=True) + epsilon) * gain


def norm_back_rows(v, e, gain):
    inv = lax.rsqrt(jnp.mean(v * v, axis=-1, keepdims=True) + epsilon)
    part = jnp.sum(e * v * inv, axis=0, keepdims=True)
    sc = e * gain
    return part, inv * sc - v * (inv * inv * inv) * jnp.mean(sc * v, axis=-1, keepdims=True)


def forward_kernel(nz, tok, cot, wq, wk, wv, w_out, pq, pkv, po, cos, sin, gain1, gain2,
                   x1_out, c_out, q_out, kv_out, att_out, lse_out, wqkv_out, wo_out, mid_out, n2_out,
                   xn, X, C, KV, q, att, lse, wqkv, wo, m_s, l_s, o_s, part, rs1, ysend, rs2,
                   sA, rA, sB, rB, sC, rC, sKV, rKV, sR1, rR1, sR2, rR2, osem):
    t = lax.axis_index("tensor")
    zi = lax.axis_index("seq")
    sib, ynb = t ^ 1, t ^ 2
    S, RP, D = tok.shape
    SPAN = 4 * RP
    TQ = 256
    NT = 2 * SPAN // TQ
    g1 = gain1[...].astype(f32).reshape(1, D)
    for s in range(S):
        xn[s] = rms(tok[s].astype(f32), g1).astype(bf16)
    entry([{"tensor": sib}, {"tensor": ynb}], True)

    def ga(w, s):
        return rc((xn, cot)[w].at[s], (X, C)[w].at[s, 1], sA.at[w, s], rA.at[w, s], {"tensor": sib})
    def gb(w, s):
        return rc((xn, cot)[w].at[s], (X, C)[w].at[s, 2], sB.at[w, s], rB.at[w, s], {"tensor": ynb})
    def gc(w, s):
        buf = (X, C)[w]
        return rc(buf.at[s, 2], buf.at[s, 3], sC.at[w, s], rC.at[w, s], {"tensor": sib})
    for s in range(S):
        gb(0, s).start()
        ga(0, s).start()
    wqkv[0:512, :] = nt(pq[...], wq[...]).astype(bf16)
    wqkv[512:896, :] = (nn(pkv[:, 0:192], wk[...]) + nn(pkv[:, 192:384], wv[...])).astype(bf16)
    for s in range(S):
        X[s, 0] = xn[s]

    def kvc(s, j, hb):
        at = pl.ds(hb * 2 * RP, 2 * RP)
        return rc(KV.at[s, j, at], KV.at[s, j, at], sKV.at[s, j, hb], rKV.at[s, j, hb], {"seq": zi + 1})
    def send_own(s, hb):
        @pl.when(zi < nz - 1)
        def _():
            kvc(s, zi, hb).start()
    def arrive(s, h, hb):
        j = zi - 1 - h
        @pl.when(j >= 0)
        def _():
            kvc(s, j, hb).wait_recv()
            @pl.when(zi < nz - 1)
            def _():
                kvc(s, j, hb).start()

    def project(s, hb):
        r = nt(X[s, 2 * hb:2 * hb + 2].reshape(2 * RP, D), wqkv[...])
        base = hb * 2 * RP
        for slot in range(6):
            g = slot // 2 if slot < 4 else slot - 4
            u = r[:, slot * 128:(slot + 1) * 128]
            u = u * cos[g, base:base + 2 * RP, :] + pltpu.roll(u, 64, 1) * sin[g, base:base + 2 * RP, :]
            if slot < 4:
                q[s, g, (slot % 2) * SPAN + base:(slot % 2) * SPAN + base + 2 * RP, :] = u.astype(bf16)
            else:
                KV[s, zi, base:base + 2 * RP, g * 128:(g + 1) * 128] = u.astype(bf16)
        KV[s, zi, base:base + 2 * RP, 256:384] = r[:, 768:896].astype(bf16)

    def unit(s, j, diag):
        def tile(g, qt):
            qa = pl.ds(pl.multiple_of(qt * TQ, TQ), TQ)
            kp = KV[s, j, :, g * 128:(g + 1) * 128]
            sT = nt(kp, q[s, g, qa, :]) * (SCALE * LOG2E)
            if diag:
                sT = causal(sT, qt, TQ, RP, t)
            mx = jnp.max(sT, axis=0, keepdims=True)
            if diag:
                m = mx
            else:
                m0 = m_s[s, g, :, qa]
                m = jnp.maximum(m0, mx)
                al = jnp.exp2(m0 - m)
            p = jnp.exp2(sT - m)
            total = jnp.sum(p, axis=0, keepdims=True)
            kv = jnp.concatenate([kp, KV[s, j, :, 256:384]], axis=1)
            o = tn(kv, p.astype(bf16))
            m_s[s, g, :, qa] = m
            if diag:
                l_s[s, g, :, qa] = total
                o_s[s, g, :, qa] = o
            else:
                l_s[s, g, :, qa] = l_s[s, g, :, qa] * al + total
                o_s[s, g, :, qa] = o_s[s, g, :, qa] * al + o
        def body(qt, c):
            tile(0, qt)
            tile(1, qt)
            return c
        lax.fori_loop(0, NT, body, 0, unroll=2)
    def hop(s, h):
        @pl.when(zi - 1 - h >= 0)
        def _():
            unit(s, zi - 1 - h, False)

    def rs_a(s):
        return rc(part.at[s, 1], rs1.at[s], sR1.at[s], rR1.at[s], {"tensor": sib})
    def rs_b(s):
        return rc(ysend.at[s], rs2.at[s], sR2.at[s], rR2.at[s], {"tensor": ynb})
    def finish(s):
        lane = lax.broadcasted_iota(jnp.int32, (128, 1), 0)
        for g in range(2):
            lse[s, g] = m_s[s, g] + jnp.log2(l_s[s, g])
            fm = in_ranges(lane, F_LANES[g])
            vm = in_ranges(lane, V_LANES[g])
            o = jnp.where(fm, o_s[s, g, 0:128, :], jnp.where(vm, o_s[s, g, 128:256, :], 0.0)) * (1.0 / l_s[s, g])
            att[s, g] = o.T.astype(bf16)
        for par in (1, 0):
            a = jnp.concatenate([jnp.concatenate([att[s, g, hh * SPAN + r * RP:hh * SPAN + (r + 1) * RP, :]
                                                  for g in range(2) for hh in range(2)], axis=1) for r in (par, par + 2)], axis=0)
            part[s, par] = nn(a, wo[...]).astype(bf16).reshape(2, RP, D)
            if par == 1:
                rs_a(s).start()
    def rs_mid(s):
        rs_a(s).wait_recv()
        ysend[s] = (part[s, 0, 1].astype(f32) + rs1[s, 1].astype(f32)).astype(bf16)
        rs_b(s).start()
    def rs_end(s):
        rs_b(s).wait_recv()
        mid = tok[s].astype(f32) + part[s, 0, 0].astype(f32) + rs1[s, 0].astype(f32) + rs2[s].astype(f32)
        mid_out[s] = mid
        n2_out[s] = rms(mid, gain2[...].astype(f32).reshape(1, D)).astype(bf16)

    ga(0, 0).wait_recv()
    project(0, 0)
    send_own(0, 0)
    ga(0, 1).wait_recv()
    project(1, 0)
    wo[...] = tn(po[...], w_out[...]).astype(bf16)
    gb(0, 0).wait_recv()
    gc(0, 0).start()
    arrive(0, 0, 0)
    gc(0, 0).wait_recv()
    project(0, 1)
    send_own(0, 1)
    arrive(0, 1, 0)
    gb(0, 1).wait_recv()
    gc(0, 1).start()
    for s in range(S):
        gb(1, s).start()
        ga(1, s).start()
    unit(0, zi, True)
    arrive(0, 0, 1)
    gc(0, 1).wait_recv()
    project(1, 1)
    arrive(0, 1, 1)
    send_own(1, 0)
    send_own(1, 1)
    hop(0, 0)
    for h in range(2, nz - 1):
        arrive(0, h, 0)
        arrive(0, h, 1)
    for s in range(S):
        C[s, 0] = cot[s]
    def more(h, c):
        hop(0, h)
        return c
    hop(0, 1)
    arrive(1, 0, 0)
    arrive(1, 0, 1)
    lax.fori_loop(2, nz - 1, more, 0)
    finish(0)
    unit(1, zi, True)
    gb(1, 0).wait_recv()
    gc(1, 0).start()
    rs_mid(0)
    arrive(1, 1, 0)
    arrive(1, 1, 1)
    hop(1, 0)
    gb(1, 1).wait_recv()
    gc(1, 1).start()
    hop(1, 1)
    rs_end(0)
    def rest(h, c):
        arrive(1, h, 0)
        arrive(1, h, 1)
        hop(1, h)
        return c
    lax.fori_loop(2, nz - 1, rest, 0)
    finish(1)
    for s in range(S):
        gc(1, s).wait_recv()
        ga(1, s).wait_recv()
    outs = [pltpu.make_async_copy(a, o, osem.at[n]) for n, (a, o) in enumerate(
        ((X, x1_out), (C, c_out), (q, q_out), (KV, kv_out), (att, att_out), (lse, lse_out), (wqkv, wqkv_out), (wo, wo_out)))]
    for o in outs:
        o.start()
    rs_mid(1)
    rs_end(1)
    for s in range(S):
        for w in range(2):
            ga(w, s).wait_send()
            gb(w, s).wait_send()
            gc(w, s).wait_send()
        rs_a(s).wait_send()
        rs_b(s).wait_send()
        for j in range(nz):
            @pl.when(jnp.logical_and(j <= zi, zi < nz - 1))
            def _():
                for hb in range(2):
                    kvc(s, j, hb).wait_send()
    for o in outs:
        o.wait()


def attend_forward(tok, cot, wq, wk, wv, w_out, pq, pkv, po, cos, sin, gain1, gain2):
    nz = lax.axis_size("seq")
    S, RP, D = tok.shape
    SPAN = 4 * RP
    V = pl.BlockSpec(memory_space=pltpu.VMEM)
    A = pl.BlockSpec(memory_space=pl.ANY)
    sd = jax.ShapeDtypeStruct
    dma = pltpu.SemaphoreType.DMA
    vm = pltpu.VMEM
    return pl.pallas_call(
        functools.partial(forward_kernel, nz),
        out_shape=[sd((S, 4, RP, D), bf16), sd((S, 4, RP, D), bf16), sd((S, 2, 2 * SPAN, 128), bf16),
                   sd((S, nz, SPAN, 384), bf16), sd((S, 2, 2 * SPAN, 128), bf16), sd((S, 2, 1, 2 * SPAN), f32),
                   sd((896, D), bf16), sd((512, D), bf16), sd((S, RP, D), f32), sd((S, RP, D), bf16)],
        in_specs=[V] * 13,
        out_specs=[A] * 8 + [V] * 2,
        scratch_shapes=[vm((S, RP, D), bf16), vm((S, 4, RP, D), bf16), vm((S, 4, RP, D), bf16),
                        vm((S, nz, SPAN, 384), bf16), vm((S, 2, 2 * SPAN, 128), bf16),
                        vm((S, 2, 2 * SPAN, 128), bf16), vm((S, 2, 1, 2 * SPAN), f32), vm((896, D), bf16), vm((512, D), bf16),
                        vm((S, 2, 1, 2 * SPAN), f32), vm((S, 2, 1, 2 * SPAN), f32), vm((S, 2, 256, 2 * SPAN), f32),
                        vm((S, 2, 2, RP, D), bf16), vm((S, 2, RP, D), bf16), vm((S, RP, D), bf16), vm((S, RP, D), bf16)]
        + [dma((2, S))] * 6 + [dma((S, nz, 2))] * 2 + [dma((S,))] * 4 + [dma((8,))],
        compiler_params=pltpu.CompilerParams(collective_id=0, has_side_effects=True, vmem_limit_bytes=VMEM_BYTES),
        name="attend_forward")(tok, cot, wq, wk, wv, w_out, pq, pkv, po, cos, sin, gain1, gain2)


def feed_kernel(summed, n2, mid, c_in, wg_in, wu_in, wd_in, gain2,
                dn_out, ga_out, gb_out, down_out, dmid_out, gpart_out,
                X, C, wg, wu, wd, dh, F, G, GD, XR, part, rs1, ysend, rs2, pd,
                sA, rA, sB, rB, sC, rC, sR1, rR1, sR2, rR2, sX, rX, isem, osem):
    t = lax.axis_index("tensor")
    sib, ynb = t ^ 1, t ^ 2
    S, RP, D = n2.shape
    FL = wg.shape[1]
    loads = [pltpu.make_async_copy(a, b, isem.at[i]) for i, (a, b) in enumerate(
        ((wd_in, wd), (c_in, C), (wg_in, wg), (wu_in, wu)))]
    for c in loads:
        c.start()
    xi = lax.axis_index("dp")
    ox = 1 - xi
    entry([{"tensor": sib}, {"tensor": ynb}] + ([{"dp": ox}] if summed else []), False)

    def ga(s):
        return rc(n2.at[s], X.at[s, 1], sA.at[s], rA.at[s], {"tensor": sib})
    def gb(s):
        return rc(n2.at[s], X.at[s, 2], sB.at[s], rB.at[s], {"tensor": ynb})
    def gc(s):
        return rc(X.at[s, 2], X.at[s, 3], sC.at[s], rC.at[s], {"tensor": sib})
    def ra(s, hb):
        return rc(part.at[s, 1, hb], rs1.at[s, hb], sR1.at[s, hb], rR1.at[s, hb], {"tensor": sib})
    def rb(s):
        return rc(ysend.at[s], rs2.at[s], sR2.at[s], rR2.at[s], {"tensor": ynb})
    for s in range(S):
        gb(s).start()
        ga(s).start()
    for s in range(S):
        X[s, 0] = n2[s]
    loads[0].wait()
    loads[1].wait()
    def early(s, c):
        dh[s] = nt(C[s].reshape(4 * RP, D), wd[...])
        return c
    lax.fori_loop(0, S, early, 0)
    loads[2].wait()
    loads[3].wait()

    def mlp(s, hb):
        x = X[s, pl.ds(2 * hb, 2)].reshape(2 * RP, D)
        rows = pl.ds(pl.multiple_of(hb * 2 * RP, 2 * RP), 2 * RP)
        g = nn(x, wg[...])
        u = nn(x, wu[...])
        sg = 1.0 / (1.0 + jnp.exp(-g))
        si = g * sg
        d = dh[s, rows]
        F[2, s, rows] = (si * u).astype(bf16)
        F[0, s, rows] = (d * u * sg * (1.0 + g * (1.0 - sg))).astype(bf16)
        F[1, s, rows] = (d * si).astype(bf16)
        r = nt(F[0, s, rows], wg[...]) + nt(F[1, s, rows], wu[...])
        part[s, 0, hb] = r[:RP].astype(bf16)
        part[s, 1, hb] = r[RP:].astype(bf16)
        ra(s, hb).start()
    def rs_mid(s):
        ra(s, 1).wait_recv()
        ysend[s] = (part[s, 0, 1].astype(f32) + rs1[s, 1].astype(f32)).astype(bf16)
        rb(s).start()
    gain = gain2[...].astype(f32).reshape(1, D)
    def rs_end(s):
        ra(s, 0).wait_recv()
        rb(s).wait_recv()
        e = part[s, 0, 0].astype(f32) + rs1[s, 0].astype(f32) + rs2[s].astype(f32)
        gp, dv = norm_back_rows(mid[s], e, gain)
        if s == 0:
            gpart_out[...] = gp
        else:
            gpart_out[...] += gp
        dm = C[s, 0].astype(f32) + dv
        dmid_out[s] = dm
        dn_out[s] = dm.astype(bf16)

    CH = 512
    def wgrad(a, src, f, c):
        at = pl.ds(pl.multiple_of(c * CH, CH), CH)
        left = src[:, :, :, at].reshape(S * 4 * RP, CH).T
        G[a, at, :] = nn(left, F[f].reshape(S * 4 * RP, FL)).astype(bf16)
    half = FL // 2
    def dgrad(h):
        left = F[2, :, :, pl.ds(pl.multiple_of(h * half, half), half)].reshape(S * 4 * RP, half).T
        for c in range(D // CH):
            at = pl.ds(c * CH, CH)
            GD[h, :, at] = nn(left, C[:, :, :, at].reshape(S * 4 * RP, CH)).astype(bf16)
    def down(s):
        r = nn(F[2, s], wd[...]).astype(bf16)
        for p in range(4):
            pd[t ^ p, s] = r[p * RP:(p + 1) * RP]

    ga(0).wait_recv()
    mlp(0, 0)
    gb(0).wait_recv()
    gc(0).start()
    gc(0).wait_recv()
    mlp(0, 1)
    ga(1).wait_recv()
    gb(1).wait_recv()
    gc(1).start()
    rs_mid(0)
    mlp(1, 0)
    gc(1).wait_recv()
    mlp(1, 1)
    rs_end(0)
    rs_mid(1)
    if summed:
        low, high = pl.ds(0, half // 2), pl.ds(half // 2, half // 2)
        xc = rc(GD.at[ox, low], XR, sX, rX, {"dp": ox})
        def part_of_two(i, x):
            dgrad(jnp.where(i == 0, ox, xi))
            @pl.when(i == 0)
            def _():
                xc.start()
            return x
        lax.fori_loop(0, 2, part_of_two, 0)
        o_down = [pltpu.make_async_copy(GD.at[h, at], gb_out.at[h, at], osem.at[n]) for n, (h, at) in enumerate(((ox, high), (xi, high), (xi, low)))]
    else:
        lax.fori_loop(0, 2, lambda h, x: (dgrad(h), x)[1], 0)
        o_down = [pltpu.make_async_copy(GD, gb_out, osem.at[0])]
    for o in o_down[:2]:
        o.start()
    down(0)
    down(1)
    o_pd = pltpu.make_async_copy(pd, down_out, osem.at[3])
    o_pd.start()
    rs_end(1)
    lax.fori_loop(0, D // CH, lambda c, x: (wgrad(0, X, 0, c), x)[1], 0)
    lax.fori_loop(0, D // CH, lambda c, x: (wgrad(1, X, 1, c), x)[1], 0)
    o_up = pltpu.make_async_copy(G, ga_out, osem.at[4])
    o_up.start()
    if summed:
        xc.wait()
        GD[xi, low] = (GD[xi, low].astype(f32) + XR[...].astype(f32)).astype(bf16)
        o_down[2].start()
    for s in range(S):
        ga(s).wait_send()
        gb(s).wait_send()
        gc(s).wait_send()
        ra(s, 0).wait_send()
        ra(s, 1).wait_send()
        rb(s).wait_send()
    for o in o_down + [o_pd, o_up]:
        o.wait()


def feed_forward(n2, mid, C, wg, wu, wd, gain2, summed):
    S, RP, D = n2.shape
    FL = wg.shape[1]
    V = pl.BlockSpec(memory_space=pltpu.VMEM)
    A = pl.BlockSpec(memory_space=pl.ANY)
    sd = jax.ShapeDtypeStruct
    dma = pltpu.SemaphoreType.DMA
    vm = pltpu.VMEM
    return pl.pallas_call(
        functools.partial(feed_kernel, summed),
        out_shape=[sd((S, RP, D), bf16), sd((2, D, FL), bf16), sd((2, FL // 2, D), bf16), sd((4, S, RP, D), bf16),
                   sd((S, RP, D), f32), sd((1, D), f32)],
        in_specs=[V, V, A, A, A, A, V],
        out_specs=[V, A, A, A, V, V],
        scratch_shapes=[vm((S, 4, RP, D), bf16), vm((S, 4, RP, D), bf16),
                        vm((D, FL), bf16), vm((D, FL), bf16), vm((FL, D), bf16), vm((S, 4 * RP, FL), f32),
                        vm((3, S, 4 * RP, FL), bf16), vm((2, D, FL), bf16), vm((2, FL // 2, D), bf16), vm((FL // 4, D), bf16), vm((S, 2, 2, RP, D), bf16), vm((S, 2, RP, D), bf16),
                        vm((S, RP, D), bf16), vm((S, RP, D), bf16), vm((4, S, RP, D), bf16)]
        + [dma((S,))] * 6 + [dma((S, 2))] * 2 + [dma((S,))] * 2 + [pltpu.SemaphoreType.DMA] * 2 + [dma((4,)), dma((5,))],
        compiler_params=pltpu.CompilerParams(collective_id=1, has_side_effects=True, vmem_limit_bytes=VMEM_BYTES),
        name="feed_forward")(n2, mid, C, wg, wu, wd, gain2)


def line(u, nz, edge=False):
    zi = lax.axis_index("seq")
    root = (nz - 1) * u if edge else nz // 2 - 1 + u
    below, above = zi < root, zi > root
    dist = jnp.where(below, root - zi, zi - root)
    return dist, below, above, zi == root, jnp.where(below, zi + 1, zi - 1)


def both(a, b):
    return jnp.logical_and(a, b)


def add(*refs):
    total = refs[0][...].astype(f32)
    for r in refs[1:]:
        total = total + r[...].astype(f32)
    return total.astype(bf16)


class Flow:
    def setup(self, n, p, lag, edge=False):
        self.n, self.p, self.lag, self.edge = n, p, lag, edge
        self.nz = lax.axis_size("seq")
        self.far = self.nz - 1 if edge else self.nz // 2
    def line(self, u):
        return line(u, self.nz, self.edge)
    def at(self, i):
        return pl.ds(pl.multiple_of(i * self.p, self.p), self.p)
    def valid(self, i):
        return both(i >= 0, i < self.n)
    def send_in(self, u, i, own, main, short, sems, act):
        dist, below, above, root, inward = self.line(u)
        ss, rr, r2 = sems
        if self.edge:
            act(rc(own, main.at[u, self.at(i)], ss.at[u, i], rr.at[u, i], {"seq": inward}))
            return
        to_short = both(dist == 1, below if u == 0 else above)
        @pl.when(to_short)
        def _():
            act(rc(own, short.at[self.at(i)], ss.at[u, i], r2.at[i], {"seq": inward}))
        @pl.when(jnp.logical_not(to_short))
        def _():
            act(rc(own, main.at[u, self.at(i)], ss.at[u, i], rr.at[u, i], {"seq": inward}))
    def from_main(self, u, i, own, main, sems):
        ss, rr, r2 = sems
        rc(own, main.at[u, self.at(i)], ss.at[u, i], rr.at[u, i], {"seq": self.line(u)[4]}).wait_recv()
    def from_short(self, u, i, own, short, sems):
        ss, rr, r2 = sems
        rc(own, short.at[self.at(i)], ss.at[u, i], r2.at[i], {"seq": self.line(u)[4]}).wait_recv()
    def outward(self, u, i, buf, bs, br, act):
        zi = lax.axis_index("seq")
        dist, below, above, root, inward = self.line(u)
        @pl.when(both(jnp.logical_not(above), zi > 0))
        def _():
            act(rc(buf.at[u, self.at(i)], buf.at[u, self.at(i)], bs.at[0, u, i], br.at[u, i], {"seq": zi - 1}))
        @pl.when(both(jnp.logical_not(below), zi < self.nz - 1))
        def _():
            act(rc(buf.at[u, self.at(i)], buf.at[u, self.at(i)], bs.at[1, u, i], br.at[u, i], {"seq": zi + 1}))
    def has_farther(self, u):
        zi = lax.axis_index("seq")
        dist, below, above, root, inward = self.line(u)
        return jnp.logical_or(both(below, zi > 0), both(above, zi < self.nz - 1))


class HalfFirst(Flow):
    count = 11
    @staticmethod
    def scratch(n, p, C):
        vm = pltpu.VMEM
        dma = pltpu.SemaphoreType.DMA
        Q = n * p
        return [vm((2, Q, C), bf16), vm((2, Q, C), bf16), vm((Q, C), bf16),
                dma((n,)), dma((n,)), dma((2, n)), dma((2, n)), dma((n,)), dma((2, 2, n)), dma((2, n)), dma((2, 2, n))]
    def __init__(self, src, own, out, bufs, osem, n, p, lag, ahead=False, halved=(0, 1)):
        self.setup(n, p, lag)
        self.src, self.own, self.out, self.osem = src, own, out, osem
        self.ahead = ahead
        self.halved = halved
        self.RX, self.RZ, self.R2, self.x1s, self.x1r, self.rs, self.rr, self.r2, self.bs, self.br, self.x2 = bufs
        self.ticks = n + lag * (2 * self.far + 2)
    def tick(self, k):
        lag, far, RX, RZ, R2 = self.lag, self.far, self.RX, self.RZ, self.R2
        xi = lax.axis_index("dp")
        ox = 1 - xi
        sems = (self.rs, self.rr, self.r2)
        start = lambda c: c.start()
        def x1(i):
            cls = pl.ds(self.halved[0], len(self.halved))
            return rc(self.src.at[ox, cls, self.at(i)], RX.at[cls, self.at(i)], self.x1s.at[i], self.x1r.at[i], {"dp": ox})
        def x2(u, i):
            return rc(RX.at[u, self.at(i)], self.out.at[xi, u, self.at(i)], self.x2.at[0, u, i], self.x2.at[1, u, i], {"dp": ox})
        @pl.when(k == 0 if self.ahead else self.valid(k))
        def _():
            if self.ahead:
                lax.fori_loop(0, self.n, lambda i, c: (x1(i).start(), c)[1], 0)
            else:
                x1(k).start()
        i1 = k - lag
        @pl.when(self.valid(i1))
        def _():
            x1(i1).wait()
            for u in self.halved:
                own = self.own(u).at[self.at(i1)]
                own[...] = add(own, RX.at[u, self.at(i1)])
        for u in range(2):
            dist, below, above, root, inward = self.line(u)
            i = k - lag * (1 + far - dist)
            @pl.when(self.valid(i))
            def _():
                own = self.own(u).at[self.at(i)]
                @pl.when(jnp.logical_not(root))
                def _():
                    @pl.when(self.has_farther(u))
                    def _():
                        self.from_main(u, i, own, RZ, sems)
                        own[...] = add(own, RZ.at[u, self.at(i)])
                    self.send_in(u, i, own, RZ, R2, sems, start)
                @pl.when(root)
                def _():
                    self.from_main(u, i, own, RZ, sems)
                    self.from_short(u, i, own, R2, sems)
                    RX[u, self.at(i)] = add(own, RZ.at[u, self.at(i)], R2.at[self.at(i)])
                    self.outward(u, i, RX, self.bs, self.br, start)
                    x2(u, i).start()
            i = k - lag * (1 + far + dist)
            @pl.when(both(self.valid(i), jnp.logical_not(root)))
            def _():
                rc(RX.at[u, self.at(i)], RX.at[u, self.at(i)], self.bs.at[0, u, i], self.br.at[u, i], {"seq": inward}).wait_recv()
                self.outward(u, i, RX, self.bs, self.br, start)
                x2(u, i).start()
            i = i - lag
            @pl.when(self.valid(i))
            def _():
                x2(u, i).wait()
                @pl.when(jnp.logical_not(root))
                def _():
                    self.send_in(u, i, self.own(u).at[self.at(i)], RZ, R2, sems, lambda c: c.wait_send())
                self.outward(u, i, RX, self.bs, self.br, lambda c: c.wait_send())
                pltpu.make_async_copy(RX.at[u, self.at(i)], self.out.at[xi, u, self.at(i)], self.osem).start()
    def drain(self):
        xi = lax.axis_index("dp")
        pltpu.make_async_copy(self.RX, self.out.at[xi], self.osem).wait()


class LineFirst(Flow):
    count = 10
    @staticmethod
    def scratch(n, p, C):
        vm = pltpu.VMEM
        dma = pltpu.SemaphoreType.DMA
        Q = n * p
        return [vm((2, Q, C), bf16), vm((Q, C), bf16), vm((Q, C), bf16),
                dma((2, n)), dma((2, n)), dma((n,)), dma((2, 2, n)), dma((2, n)), dma((n,)), dma((n,))]
    def __init__(self, W, out, bufs, osem, n, p, lag, edge=False):
        self.setup(n, p, lag, edge)
        self.W, self.out, self.osem = W, out, osem
        self.Z, self.XB, self.R2, self.rs, self.rr, self.r2, self.bs, self.br, self.xs, self.xr = bufs
        self.ticks = n + lag * (2 * self.far + 2)
    def tick(self, k):
        lag, far, W, Z = self.lag, self.far, self.W, self.Z
        ox = 1 - lax.axis_index("dp")
        sems = (self.rs, self.rr, self.r2)
        start = lambda c: c.start()
        def xb(u, i):
            return rc(W.at[u, self.at(i)], self.XB.at[self.at(i)], self.xs.at[i], self.xr.at[i], {"dp": ox})
        for u in range(2):
            dist, below, above, root, inward = self.line(u)
            i = k - lag * (far - dist)
            @pl.when(self.valid(i))
            def _():
                own = W.at[u, self.at(i)]
                @pl.when(jnp.logical_not(root))
                def _():
                    @pl.when(self.has_farther(u))
                    def _():
                        self.from_main(u, i, own, Z, sems)
                        own[...] = add(own, Z.at[u, self.at(i)])
                    self.send_in(u, i, own, Z, self.R2, sems, start)
                @pl.when(root)
                def _():
                    self.from_main(u, i, own, Z, sems)
                    if self.edge:
                        own[...] = add(own, Z.at[u, self.at(i)])
                    else:
                        self.from_short(u, i, own, self.R2, sems)
                        own[...] = add(own, Z.at[u, self.at(i)], self.R2.at[self.at(i)])
                    xb(u, i).start()
            i = k - lag * (far + 1)
            @pl.when(both(self.valid(i), root))
            def _():
                xb(u, i).wait()
                Z[u, self.at(i)] = add(W.at[u, self.at(i)], self.XB.at[self.at(i)])
                self.outward(u, i, Z, self.bs, self.br, start)
            i = k - lag * (far + 1 + dist)
            @pl.when(both(self.valid(i), jnp.logical_not(root)))
            def _():
                rc(Z.at[u, self.at(i)], Z.at[u, self.at(i)], self.bs.at[0, u, i], self.br.at[u, i], {"seq": inward}).wait_recv()
                self.outward(u, i, Z, self.bs, self.br, start)
            i = i - lag
            @pl.when(self.valid(i))
            def _():
                @pl.when(jnp.logical_not(root))
                def _():
                    self.send_in(u, i, W.at[u, self.at(i)], Z, self.R2, sems, lambda c: c.wait_send())
                self.outward(u, i, Z, self.bs, self.br, lambda c: c.wait_send())
                pltpu.make_async_copy(Z.at[u, self.at(i)], self.out.at[u, self.at(i)], self.osem).start()
    def drain(self):
        pltpu.make_async_copy(self.Z, self.out, self.osem).wait()


NO = 192
WROWS = 384
CROWS = 4 * NO
PHASES = {"dast": 1, "steps": 2, "out": 2, "done": 1, "in": 1}
PRE = 4
HOP = 2


def backward_kernel(summed, plan, dn_in, q_in, kv_in, att_in, lse, wo_in, wt_in, x1_in, pq, pkv, po, cos, sin, tok, dmid_in, gain1, gp2,
                    g_in, gd_in, ig_out, gains_out, o_gate, o_up, o_down, o_wo, o_rest, *scr):
    t = lax.axis_index("tensor")
    zi = lax.axis_index("seq")
    nz = lax.axis_size("seq")
    sib, ynb = t ^ 1, t ^ 2
    S, RP, D = tok.shape
    SPAN = 4 * RP
    TQ = 512
    NT = 2 * SPAN // TQ
    HC = D // 4
    QC = CROWS // 4
    scr = list(scr)
    (DB, q, KV, att, wbuf, da, delta, dqT, acc, PB, RB, dqkv, rs1, rs2, W3, WO, heads, GS, GL,
     sKV, rKV, sR1, rR1, sR2, rR2, sG, rG, sDB, rDB, isem, sems_out) = scr[:31]
    scr = scr[31:]
    xi = lax.axis_index("dp")
    rings = []
    def sites(phase, count):
        mode = PHASES[phase]
        return -(-count // mode) if mode else 0
    loads = [pltpu.make_async_copy(a, b, isem.at[i]) for i, (a, b) in enumerate(
        ((dn_in, DB.at[:, 0]), (wo_in, wbuf.at[pl.ds(0, 512)]), (att_in, att), (q_in, q), (kv_in, KV), (dmid_in, ig_out)))]
    first = []
    if summed:
        def take(cls):
            got = scr[:cls.count]
            del scr[:cls.count]
            return got
        own_g, own_d, WU, WE = (scr.pop(0) for _ in range(4))
        def make(name, cls, *a):
            n, lag, off, pace, *more = plan[name]
            return cls(*a[:-1], take(cls), sems_out.at[len(rings)], n, a[-1] // n, lag, *more), off, pace
        rings.append(make("gate", HalfFirst, g_in.at[0], lambda u: own_g.at[u], o_gate, own_g.shape[1]))
        rings.append(make("down", HalfFirst, gd_in, lambda u: own_d.at[u], o_down, own_d.shape[1]))
        rings.append(make("up", LineFirst, WU, o_up.at[0], WU.shape[1]))
        rings.append(make("up_edge", LineFirst, WE, o_up.at[1], WE.shape[1]))
        rings.append(make("wo", HalfFirst, WO, lambda u: WO.at[xi, u], o_wo, WROWS // 4))
        ring, off, pace = rings.pop()
        rings.append((ring, off + 2 * PRE + sites("dast", 2 * S) + sites("out", 4), pace))
        rings.append(make("rest", HalfFirst, W3, lambda u: W3.at[xi, u], o_rest, QC))
        first = [pltpu.make_async_copy(a, b, isem.at[13 + i]) for i, (a, b) in enumerate(
            ((gd_in.at[xi], own_d), (g_in.at[0, xi], own_g), (g_in.at[1, 0], WU), (g_in.at[1, 1], WE)))]
    def tick(g):
        for ring, off, pace in rings[:-1]:
            if pace == 1:
                ring.tick(g - off)
            else:
                @pl.when((g - off) % pace == 0)
                def _():
                    ring.tick((g - off) // pace)
    def ptick(phase, it, k):
        mode = PHASES[phase]
        if mode == 1:
            tick(k + it)
        elif mode:
            @pl.when(it % mode == 0)
            def _():
                tick(k + it // mode)
    def after(phase, count, k):
        return k + sites(phase, count)
    wt_load = pltpu.make_async_copy(wt_in, wbuf, isem.at[8])
    x1_loads = [pltpu.make_async_copy(x1_in.at[:, :, pl.ds(c * HC, HC)], PB.at[pl.ds(S * c, S)], isem.at[9 + c]) for c in range(4)]
    for c in loads[:2] + first + loads[2:]:
        c.start()
    devs = [{"tensor": sib}, {"tensor": ynb}]
    if summed:
        devs.append({"dp": 1 - xi})
        b = 2
        while b < nz:
            devs.append({"seq": zi ^ b})
            b *= 2
    entry(devs, True)
    def ga(s):
        return rc(DB.at[s, 0], DB.at[s, 1], sDB.at[0, s], rDB.at[0, s], {"tensor": sib})
    def gb(s):
        return rc(DB.at[s, 0], DB.at[s, 2], sDB.at[1, s], rDB.at[1, s], {"tensor": ynb})
    def gc(s):
        return rc(DB.at[s, 2], DB.at[s, 3], sDB.at[2, s], rDB.at[2, s], {"tensor": sib})
    loads[0].wait()
    for s in range(S):
        gb(s).start()
        ga(s).start()
    for c in first:
        c.wait()
    lax.fori_loop(0, PRE, lambda k, c: (tick(k), c)[1], 0)
    gb(0).wait_recv()
    gc(0).start()
    lax.fori_loop(PRE, 2 * PRE, lambda k, c: (tick(k), c)[1], 0)
    gb(1).wait_recv()
    gc(1).start()
    loads[1].wait()
    for s in range(S):
        ga(s).wait_recv()
        gc(s).wait_recv()

    def dast(it, c):
        s = it // 2
        hb = it % 2
        r = nt(DB[s, pl.ds(2 * hb, 2)].reshape(2 * RP, D), wbuf[0:512, :])
        for h in range(4):
            rows = pl.ds(pl.multiple_of((h % 2) * SPAN + hb * 2 * RP, 2 * RP), 2 * RP)
            da[s, h // 2, rows, :] = r[:, h * 128:(h + 1) * 128].astype(bf16)
        ptick("dast", it, 2 * PRE)
        return c
    lax.fori_loop(0, 2 * S, dast, 0)
    wt_load.start()
    k = after("dast", 2 * S, 2 * PRE)
    loads[2].wait()
    def dlt(it, c):
        s = it // 2
        g = it % 2
        d = da[s, g].astype(f32) * att[s, g].astype(f32)
        delta[s, g] = jnp.sum(d.T, axis=0, keepdims=True)
        dqT[s, g] = jnp.zeros((128, 2 * SPAN), f32)
        return c
    lax.fori_loop(0, 2 * S, dlt, 0)
    for c in loads[3:5]:
        c.wait()

    def put(row, at, value):
        lo = 0
        while lo < value.shape[0]:
            blk, r = (row + lo) // QC, (row + lo) % QC
            cnt = min(value.shape[0] - lo, QC - r)
            W3[blk // 2, blk % 2, r:r + cnt, at] = value[lo:lo + cnt, :]
            lo += cnt
    for s in range(S):
        for r in range(4):
            heads[s * SPAN:(s + 1) * SPAN, r * 128:(r + 1) * 128] = att[s, r // 2, (r % 2) * SPAN:(r % 2 + 1) * SPAN, :]
    def out_grad(k, c, x):
        at = pl.ds(pl.multiple_of(c * HC, HC), HC)
        g0 = nn(heads[...].T, DB[:, :, :, at].reshape(S * SPAN, HC)).astype(bf16)
        g0 = nn(po[...], g0).astype(bf16)
        for b in range(4):
            WO[b // 2, b % 2, :, at] = g0[b * (WROWS // 4):(b + 1) * (WROWS // 4), :]
        ptick("out", c, k)
        return x
    lax.fori_loop(0, 4, functools.partial(out_grad, k), 0)
    k = after("out", 4, k)

    def unit(s, j, diag):
        lane = lax.broadcasted_iota(jnp.int32, (1, 128), 1)
        acc[...] = jnp.zeros((SPAN, 384), f32)
        for g in range(2):
            fm = in_ranges(lane, F_LANES[g])
            def body(qt, c):
                qa = pl.ds(pl.multiple_of(qt * TQ, TQ), TQ)
                kp = KV[s, j, :, g * 128:(g + 1) * 128]
                kv = jnp.concatenate([kp, KV[s, j, :, 256:384]], axis=1)
                qq = q[s, g, qa, :]
                d = da[s, g, qa, :]
                zero = jnp.zeros_like(d)
                d2 = jnp.concatenate([jnp.where(fm, d, zero), jnp.where(fm, zero, d)], axis=1)
                sT = nt(kp, qq) * (SCALE * LOG2E) - lse[s, g, :, qa]
                if diag:
                    sT = causal(sT, qt, TQ, RP, t)
                p = jnp.exp2(sT)
                ds = (p * (nt(kv, d2) - delta[s, g, :, qa])).astype(bf16)
                dk = nn(ds, qq) * SCALE
                dv = nn(p.astype(bf16), d2)
                acc[:, g * 128:(g + 1) * 128] += dk + dv[:, :128]
                acc[:, 256:384] += dv[:, 128:]
                dqT[s, g, :, qa] += tn(kp, ds)
                return c
            lax.fori_loop(0, NT, body, 0, unroll=2)
        PB[j * S + s] = acc[...].astype(bf16)

    def chain(s, j):
        return rc(RB.at[j, s], RB.at[j, s], sKV.at[j, s], rKV.at[j, s], {"seq": zi - 1})
    def event(e):
        j = e // S
        s = e % S
        @pl.when(both(both(e >= 0, e < nz * S), j <= zi))
        def _():
            acc[...] = PB[e].astype(f32)
            @pl.when(zi < nz - 1)
            def _():
                chain(s, j).wait_recv()
                acc[...] += RB[j, s].astype(f32)
            @pl.when(j < zi)
            def _():
                RB[j, s] = acc[...].astype(bf16)
                chain(s, j).start()
            @pl.when(j == zi)
            def _():
                for g in range(2):
                    u = acc[:, g * 128:(g + 1) * 128]
                    dqkv[s, :, 512 + g * 128:512 + (g + 1) * 128] = (u * cos[g] - pltpu.roll(u, 64, 1) * sin[g]).astype(bf16)
                dqkv[s, :, 768:896] = acc[:, 256:384].astype(bf16)
    def step(m, c):
        j = m // S
        s = m % S
        @pl.when(j < zi)
        def _():
            unit(s, j, False)
        @pl.when(j == zi)
        def _():
            unit(s, j, True)
        event(m - 1 - HOP * (nz - 1 - zi))
        ptick("steps", m, k)
        return c
    steps = nz * S + 1 + HOP * (nz - 1)
    lax.fori_loop(0, steps, step, 0)
    k = after("steps", steps, k)
    for c in x1_loads:
        c.start()

    def rotate(c, x):
        s = c // 2
        for g in range(2):
            @pl.when(c % 2 == g)
            def _():
                for hh in range(2):
                    u = dqT[s, g, :, hh * SPAN:(hh + 1) * SPAN].T * SCALE
                    dqkv[s, :, (2 * g + hh) * 128:(2 * g + hh + 1) * 128] = (u * cos[g] - pltpu.roll(u, 64, 1) * sin[g]).astype(bf16)
        return x
    lax.fori_loop(0, 2 * S, rotate, 0)
    wt_load.wait()
    for s in range(S):
        ga(s).wait_send()
        gb(s).wait_send()
        gc(s).wait_send()

    def ra(s, hb):
        return rc(DB.at[s, 2 + hb], rs1.at[s, hb], sR1.at[s, hb], rR1.at[s, hb], {"tensor": sib})
    def rb(s):
        return rc(DB.at[s, 1], rs2.at[s], sR2.at[s], rR2.at[s], {"tensor": ynb})
    def d_one(it, c):
        s = it // 2
        hb = 1 - it % 2
        rows = pl.ds(pl.multiple_of(hb * 2 * RP, 2 * RP), 2 * RP)
        r = nn(dqkv[s, rows, :], wbuf[...])
        DB[s, hb] = r[:RP].astype(bf16)
        DB[s, 2 + hb] = r[RP:].astype(bf16)
        ra(s, hb).start()
        ptick("done", it, k)
        return c
    lax.fori_loop(0, 2 * S, d_one, 0)
    k = after("done", 2 * S, k)
    for s in range(S):
        ra(s, 1).wait_recv()
        DB[s, 1] = add(DB.at[s, 1], rs1.at[s, 1])
        rb(s).start()
    for c in x1_loads:
        c.wait()
    def in_grad(c, x):
        at = pl.ds(pl.multiple_of(c * HC, HC), HC)
        g0 = nn(dqkv[...].reshape(S * SPAN, 896).T, PB[pl.ds(S * c, S)].reshape(S * SPAN, HC)).astype(bf16)
        gq = tn(pq[...], g0[0:512]).astype(bf16)
        gkv = tn(pkv[...], g0[512:896]).astype(bf16)
        put(0, at, gq)
        put(2 * NO, at, gkv)
        ptick("in", c, k)
        return x
    lax.fori_loop(0, 4, in_grad, 0)
    k = after("in", 4, k)
    if summed:
        start_rest = k
        def joint(g):
            for i, (ring, off, pace) in enumerate(rings):
                kk = g - (start_rest if i == len(rings) - 1 else off)
                if pace == 1:
                    ring.tick(kk)
                else:
                    @pl.when(kk % pace == 0)
                    def _():
                        ring.tick(kk // pace)
    else:
        o3 = [pltpu.make_async_copy(W3, o_rest, sems_out.at[5]), pltpu.make_async_copy(WO, o_wo, sems_out.at[4])]
        for o in o3:
            o.start()
        def joint(g):
            pass
    joint(k)
    joint(k + 1)
    k = k + 2
    loads[5].wait()
    gain = gain1[...].astype(f32).reshape(1, D)
    gp1 = None
    for s in range(S):
        ra(s, 0).wait_recv()
        rb(s).wait_recv()
        e = DB[s, 0].astype(f32) + rs1[s, 0].astype(f32) + rs2[s].astype(f32)
        gp, dv = norm_back_rows(tok[s].astype(f32), e, gain)
        gp1 = gp if gp1 is None else gp1 + gp
        ig_out[s] += dv
    gains_out[...] = jnp.concatenate([gp1, gp2[...], jnp.zeros((6, D), f32)], axis=0)
    if summed:
        peers = [{"tensor": sib}, {"tensor": ynb}, {"dp": 1 - xi}]
        b = 1
        while b < nz:
            peers.append({"seq": zi ^ b})
            b *= 2
        for m, dev in enumerate(peers):
            GS[m] = gains_out[...]
            c = rc(GS.at[m], GL.at[m], sG.at[m], rG.at[m], dev)
            c.start()
            joint(k)
            k = k + 1
            c.wait()
            gains_out[...] += GL[m]
        last = max((start_rest if i == len(rings) - 1 else off) + (ring.ticks - 1) * pace + 1 for i, (ring, off, pace) in enumerate(rings))
        lax.fori_loop(k, last, lambda m, c: (joint(m), c)[1], 0)
    for s in range(S):
        ra(s, 0).wait_send()
        ra(s, 1).wait_send()
        rb(s).wait_send()
        for j in range(nz):
            @pl.when(j < zi)
            def _():
                chain(s, j).wait_send()
    if summed:
        for ring, off, pace in rings:
            ring.drain()
    else:
        for o in o3:
            o.wait()


PLAN = {"gate": (12, 2, 6, 1), "down": (8, 2, 0, 1, False, (1,)), "up": (12, 1, 23, 2), "up_edge": (24, 2, 7, 1, True), "wo": (6, 2, 2, 1), "rest": (12, 2, 0, 1)}


def attend_backward(dn, q, KV, att, lse, wo, wt, X1, pq, pkv, po, cos, sin, tok, dmid, gain1, gp2, g, gd, summed, plan=PLAN):
    nz = lax.axis_size("seq")
    S, RP, D = tok.shape
    SPAN = 4 * RP
    FL = g.shape[-1]
    QG, QD, QC = D // 4, FL // 4, CROWS // 4
    V = pl.BlockSpec(memory_space=pltpu.VMEM)
    A = pl.BlockSpec(memory_space=pl.ANY)
    sd = jax.ShapeDtypeStruct
    dma = pltpu.SemaphoreType.DMA
    vm = pltpu.VMEM
    scratch = [vm((S, 4, RP, D), bf16), vm(q.shape, bf16), vm(KV.shape, bf16), vm(att.shape, bf16), vm((896, D), bf16),
               vm(q.shape, bf16), vm((S, 2, 1, 2 * SPAN), f32), vm((S, 2, 128, 2 * SPAN), f32), vm((SPAN, 384), f32),
               vm((nz * S, SPAN, 384), bf16), vm((nz - 1, S, SPAN, 384), bf16), vm((S, SPAN, 896), bf16),
               vm((S, 2, RP, D), bf16), vm((S, RP, D), bf16), vm((2, 2, QC, D), bf16), vm((2, 2, WROWS // 4, D), bf16), vm((S * SPAN, 512), bf16),
               vm((6, 8, D), f32), vm((6, 8, D), f32),
               dma((nz, S)), dma((nz, S)), dma((S, 2)), dma((S, 2)), dma((S,)), dma((S,)), dma((6,)), dma((6,)), dma((3, S)), dma((3, S)), dma((17,)), dma((6,))]
    if summed:
        scratch += [vm((2, QG, FL), bf16), vm((2, QD, D), bf16), vm((2, QG, FL), bf16), vm((2, QG, FL), bf16)]
        for name, cls, Q, C in (("gate", HalfFirst, QG, FL), ("down", HalfFirst, QD, D), ("up", LineFirst, QG, FL), ("up_edge", LineFirst, QG, FL), ("wo", HalfFirst, WROWS // 4, D), ("rest", HalfFirst, QC, D)):
            n = plan[name][0]
            scratch += cls.scratch(n, Q // n, C)
    return pl.pallas_call(
        functools.partial(backward_kernel, summed, plan),
        out_shape=[sd((S, RP, D), f32), sd((8, D), f32), sd((2, 2, QG, FL), bf16), sd((2, 2, QG, FL), bf16), sd((2, 2, QD, D), bf16),
                   sd((2, 2, WROWS // 4, D), bf16), sd((2, 2, QC, D), bf16)],
        in_specs=[A, A, A, A, V, A, A, A, V, V, V, V, V, V, A, V, V, A, A],
        out_specs=[V, V, A, A, A, A, A],
        scratch_shapes=scratch,
        compiler_params=pltpu.CompilerParams(collective_id=2, has_side_effects=True, vmem_limit_bytes=VMEM_BYTES),
        name="attend_backward")(dn, q, KV, att, lse, wo, wt, X1.reshape(S, SPAN, D), pq, pkv, po, cos, sin, tok, dmid, gain1, gp2,
                                g.reshape(2, 2, 2, QG, FL), gd.reshape(2, 2, QD, D))


def local(
    tokens, attn_gain, w_query, w_key, w_value, w_output, ffn_gain, w_gate, w_up, w_down, cotangent
):
    t = lax.axis_index("tensor")
    zi = lax.axis_index("seq")
    pq, pkv, po = (jnp.asarray(v, bf16) for v in pick_tables())
    tok = jnp.swapaxes(tokens, 0, 1)
    cot = jnp.swapaxes(cotangent, 0, 1)
    S, RP, D = tok.shape
    cos, sin = rope_tables(zi * 4 * RP, 4 * RP, t)
    X1, C, q, KV, att, lse, wqkv, wo, mid, n2 = attend_forward(
        tok, cot, w_query, w_key.T, w_value.T, w_output, pq, pkv, po, cos, sin, attn_gain, ffn_gain)
    summed = lax.axis_size("dp") == 2
    dn, g, gd, down, dmid, gp2 = feed_forward(n2, mid, C, w_gate, w_up, w_down, ffn_gain, summed)
    down_local = lax.psum_scatter(down, "tensor", scatter_dimension=0, tiled=True)[0]
    ig, gains, gate, up, wd, out, rest = attend_backward(
        dn, q, KV, att, lse, wo, wqkv, X1, pq, pkv, po, cos, sin, tok, dmid, attn_gain, gp2, g, gd, summed)
    if not summed:
        g, wd, out, rest = lax.psum((g.astype(f32), gd.astype(f32), out.astype(f32), rest.astype(f32)), ("dp", "seq"))
        gate, up = g[0], g[1]
        gains = lax.psum(gains, ("dp", "seq", "tensor"))
    rest = rest.reshape(-1, D)
    nq, nk = w_query.shape[1], w_key.shape[1]
    activation = (mid + down_local.astype(f32)).astype(bf16)
    return (
        jnp.swapaxes(activation, 0, 1),
        jnp.swapaxes(ig, 0, 1),
        gains[0],
        rest[:nq].astype(f32).T,
        rest[nq:nq + nk].astype(f32).T,
        rest[nq + nk:nq + 2 * nk].astype(f32).T,
        out.reshape(-1, D).astype(f32),
        gains[1],
        gate.reshape(D, -1).astype(f32),
        up.reshape(D, -1).astype(f32),
        wd.reshape(-1, D).astype(f32),
    )


def solution(mesh):
    rows = P(("seq", "tensor"), "dp", None)
    columns = P(None, "tensor")
    placed = (rows, P(), columns, columns, columns, P("tensor", None), P(), columns, columns, P("tensor", None), rows)
    return jax.shard_map(
        local,
        mesh=mesh,
        in_specs=placed,
        out_specs=(rows, rows, P(), columns, columns, columns, P("tensor", None), P(), columns, columns, P("tensor", None)),
        check_vma=False,
    )
```
